256 devices in a mesh: prow: 32 (over x_hi, z, core), pcol: 8 (over y, x_lo).
Axes of the slice: x: 4 (x_hi: 2, x_lo: 2; x = x_hi * 2 + x_lo), y: 4, z: 8, core: 2. Of those that a mesh axis runs over, the one named last changes fastest.
Arguments:
- features: bfloat16 [32768, 256], P(('prow', 'pcol')), may hold values from -6 to 6
- cotangent: bfloat16 [32768, 256], P(('prow', 'pcol')), may hold values from -0.1875 to 0.1875
- self_weight: bfloat16 [256, 256], replicated, may hold values from -0.375 to 0.375
- basis_weights: bfloat16 [32, 256, 256], replicated, may hold values from -0.375 to 0.375
- coefficients: float32 [2690, 32], replicated, may hold values from -1 to 1
- tile_list: int32 [32, 8, 16, 3], P('prow', 'pcol'), may hold values from 0 to 1344, as said below
- tile_mask: int32 [32, 8, 16, 128, 128], P('prow', 'pcol'), may hold values 0 or 1
- live_tiles: int32 [32, 8], P('prow', 'pcol'), may hold values from 1 to 16, as said below
Outputs:
- layer_output: bfloat16 [32768, 256], P(('prow', 'pcol'))
- coefficient_grads: float32 [2690, 32], replicated
The draws below stay inside these ranges and needn't reach their ends.
Inputs may be any that keep to these rules, and one draw needn't show every extreme that they name: `tile_list`: entries are (relation below 1345, source row index below 32, target column index below 8). `live_tiles`: tile slots at or beyond a cell's count are padding.
All inputs are finite; a program needn't handle non-finite values. No bound on the sum of `tile_mask` on one device may be relied on, other than what follows from the above.
Results may differ from the reference program's by a relative error of at most 0.0054.
Values may be sent and summed in bfloat16 or wider, within the bound.
No kernel may reach another device: no remote copies, remote signals or barrier semaphores. Data moves between devices by JAX's collectives and lax.ppermute only.
A program may use at most 64 MiB of HBM per device.

```python
import jax
import jax.numpy as jnp
from jax import lax

D = 256
BASES = 32
REL = 1345
BLK = 128
TILES = 16
ENTITIES = 32768
N_PROW = 32
N_PCOL = 8


def draw_tile_list(key, part):
    key = jax.random.fold_in(key, 11)
    first, second, third = jax.random.split(key, 3)
    shape = (N_PROW, N_PCOL, TILES)
    relation = jax.random.randint(first, shape, 0, REL)
    source = jax.random.randint(second, shape, 0, N_PROW)
    target = jax.random.randint(third, shape, 0, N_PCOL)
    relation = relation.at[0, 0, 0].set(REL - 1)
    source = source.at[0, 0, 0].set(N_PROW - 1)
    target = target.at[0, 0, 0].set(N_PCOL - 1)
    return jnp.stack([relation, source, target], axis=-1).astype(jnp.int32)


def draw_live_tiles(key, part):
    key = jax.random.fold_in(key, 23)
    first, second = jax.random.split(key, 2)
    counts = jax.random.randint(first, (N_PROW * N_PCOL,), max(TILES // 4, 1), TILES + 1)
    spot = jax.random.randint(second, (), 0, N_PROW * N_PCOL)
    counts = counts.at[spot].set(TILES)
    return counts.reshape(N_PROW, N_PCOL).astype(jnp.int32)


def place_ends(array, key, smallest, largest):
    index_at = [jax.random.randint(jax.random.fold_in(key, axis), (), 0, length) for axis, length in enumerate(array.shape)]
    longest = array.shape.index(max(array.shape))
    neighbour = index_at[:longest] + [(index_at[longest] + 1) % array.shape[longest]] + index_at[longest + 1:]
    return array.at[tuple(index_at)].set(smallest).at[tuple(neighbour)].set(largest)


def block_levels(key, shape, shards, least, high):
    level, own = 1.0, jax.random.fold_in(key, 6)
    for dim, parts in shards:
        draws = jnp.exp(jax.random.uniform(jax.random.fold_in(own, dim), (parts,), jnp.float32, least / len(shards), high / len(shards)))
        level = level * jnp.repeat(draws, shape[dim] // parts).reshape([-1 if axis == dim else 1 for axis in range(len(shape))])
    return level


def bell_draw(key, dims, spread, limit, shards=(), kind=jnp.bfloat16):
    loudness = block_levels(key, dims, shards, -0.22, 0.18) if shards else 1.0
    result = jax.random.normal(key, dims, jnp.float32) * spread * loudness
    return jnp.minimum(jnp.maximum(result, -limit), limit).astype(kind)


def setup_inputs(seed: int = 0) -> dict:
    key_of = jax.random.split(jax.random.key(seed), 9)
    features = bell_draw(key_of[0], (ENTITIES, D), 1.0, 6.0, ((0, 256),))
    cotangent = bell_draw(key_of[1], (ENTITIES, D), (0.5 * D ** -0.5), 0.1875, ((0, 256),))
    self_weight = bell_draw(key_of[2], (D, D), D ** -0.5, 0.375)
    basis_weights = bell_draw(key_of[3], (BASES, D, D), D ** -0.5, 0.375)
    coefficients = bell_draw(key_of[4], (2 * REL, BASES), (BASES ** -0.5), 1.0, (), jnp.float32)
    tile_list = draw_tile_list(jax.random.fold_in(key_of[8], 71), 0)
    tile_mask = place_ends((jax.random.randint(key_of[6], (N_PROW, N_PCOL, TILES, BLK, BLK), 0, 4) < 1).astype(jnp.int32), jax.random.fold_in(key_of[6], 1), 0, 1)
    live_tiles = draw_live_tiles(jax.random.fold_in(key_of[8], 71), 0)
    return dict(features=features, cotangent=cotangent, self_weight=self_weight, basis_weights=basis_weights, coefficients=coefficients, tile_list=tile_list, tile_mask=tile_mask, live_tiles=live_tiles)


def reference(features, cotangent, self_weight, basis_weights, coefficients, tile_list, tile_mask, live_tiles):
    row_count = N_PROW
    column_count = N_PCOL
    basis_wide = basis_weights.astype(jnp.float32)
    layer_sum = jnp.dot(features, self_weight, preferred_element_type=jnp.float32)
    grads_start = jnp.zeros((2 * REL, BASES), jnp.float32)
    flat = jnp.arange(row_count * column_count * TILES, dtype=jnp.int32)
    row_index = flat // (column_count * TILES)
    column_index = (flat // TILES) % column_count
    position = flat % TILES
    weighting = (position < live_tiles.reshape(-1)[flat // TILES]).astype(jnp.float32)
    entries = tile_list.reshape(-1, 3)
    masks = tile_mask.reshape(-1, BLK, BLK)

    def step(carry, item):
        running, grads = carry
        entry, mask, row_at, column_at, weight = item
        relation = entry[0]
        source = entry[1]
        target = entry[2]
        target_start = ((row_at * column_count + target) * BLK).astype(jnp.int32)
        source_start = ((source * column_count + column_at) * BLK).astype(jnp.int32)
        x_source = lax.dynamic_slice_in_dim(features, source_start, BLK, 0)
        x_target = lax.dynamic_slice_in_dim(features, target_start, BLK, 0)
        g_source = lax.dynamic_slice_in_dim(cotangent, source_start, BLK, 0)
        g_target = lax.dynamic_slice_in_dim(cotangent, target_start, BLK, 0)
        mask_float = mask.astype(jnp.float32)
        forward_adjacency = (mask_float / (1.0 + jnp.sum(mask_float, axis=1, keepdims=True))).astype(jnp.bfloat16)
        inverse_adjacency = (mask_float.T / (1.0 + jnp.sum(mask_float, axis=0)[:, None])).astype(jnp.bfloat16)
        forward_rows = jnp.dot(forward_adjacency, x_source, preferred_element_type=jnp.float32).astype(jnp.bfloat16)
        inverse_rows = jnp.dot(inverse_adjacency, x_target, preferred_element_type=jnp.float32).astype(jnp.bfloat16)
        selected = jnp.stack([coefficients[relation], coefficients[relation + REL]])
        weights = jnp.einsum('rb,bde->rde', selected, basis_wide, precision=lax.Precision.HIGHEST).astype(jnp.bfloat16)
        forward_message = jnp.dot(forward_rows, weights[0], preferred_element_type=jnp.float32) * weight
        inverse_message = jnp.dot(inverse_rows, weights[1], preferred_element_type=jnp.float32) * weight
        piece = lax.dynamic_slice_in_dim(running, target_start, BLK, 0) + forward_message
        running = lax.dynamic_update_slice_in_dim(running, piece, target_start, 0)
        piece = lax.dynamic_slice_in_dim(running, source_start, BLK, 0) + inverse_message
        running = lax.dynamic_update_slice_in_dim(running, piece, source_start, 0)
        forward_moment = jnp.dot(forward_rows.T, g_target, preferred_element_type=jnp.float32)
        inverse_moment = jnp.dot(inverse_rows.T, g_source, preferred_element_type=jnp.float32)
        moments = jnp.stack([forward_moment, inverse_moment])
        per_tile = jnp.einsum('rde,bde->rb', moments, basis_wide, precision=lax.Precision.HIGHEST) * weight
        grads = grads.at[relation].add(per_tile[0])
        grads = grads.at[relation + REL].add(per_tile[1])
        return (running, grads), None

    (layer_sum, grads), _ = lax.scan(step, (layer_sum, grads_start), (entries, masks, row_index, column_index, weighting))
    return layer_sum.astype(jnp.bfloat16), grads
```

```python
import functools
import jax
import jax.numpy as jnp
from jax import lax
from jax.experimental import pallas as pl
from jax.experimental.pallas import tpu as pltpu
from jax.sharding import PartitionSpec as P

F32, BF16 = jnp.float32, jnp.bfloat16
VMEM = pl.BlockSpec(memory_space=pltpu.VMEM)
SMEM = pl.BlockSpec(memory_space=pltpu.SMEM)
ANY = pl.BlockSpec(memory_space=pl.ANY)
LANES = 128
DIAGONAL = 16
PAYLOAD = 40


def params(mib):
    return pltpu.CompilerParams(vmem_limit_bytes=mib * 1024 * 1024)


def cost(flops, moved):
    return pl.CostEstimate(flops=flops, bytes_accessed=moved, transcendentals=0)


def split(wide):
    high = wide.astype(BF16)
    return high, (wide - high.astype(F32)).astype(BF16)


def iota(shape, dim):
    return lax.broadcasted_iota(jnp.int32, shape, dim)


def weights_kernel(row_ref, coefficient_ref, basis_ref, weight_ref, spread):
    bases, named = coefficient_ref.shape
    sides = row_ref.shape[1]
    tall, wide = sides * DIAGONAL, bases * DIAGONAL

    @pl.when(pl.program_id(0) == 0)
    def _():
        chosen = (iota((named, sides), 0) == row_ref[...]).astype(BF16)
        rows = (iota((tall, sides), 0) // DIAGONAL == iota((tall, sides), 1)).astype(BF16)
        columns = (iota((bases, wide), 1) // DIAGONAL == iota((bases, wide), 0)).astype(BF16)
        same = iota((tall, wide), 0) % DIAGONAL == iota((tall, wide), 1) % DIAGONAL
        for index, part in enumerate(split(coefficient_ref[...])):
            picked = jnp.dot(part, chosen, preferred_element_type=F32).astype(BF16)
            tower = lax.dot_general(rows, picked, (((1,), (1,)), ((), ())), preferred_element_type=F32).astype(BF16)
            full = jnp.dot(tower, columns, preferred_element_type=F32)
            spread[index] = jnp.where(same, full, 0.0).astype(BF16)

    for start in range(0, basis_ref.shape[1], DIAGONAL):
        part = basis_ref[:, start : start + DIAGONAL, :].reshape(wide, basis_ref.shape[2])
        total = jnp.dot(spread[0], part, preferred_element_type=F32)
        total += jnp.dot(spread[1], part, preferred_element_type=F32)
        weight_ref[:, start : start + DIAGONAL, :] = total.astype(BF16).reshape(sides, DIAGONAL, -1)


def relation_weights(rows_named, coefficients_t, basis, steps=4):
    bases, depth, width = basis.shape
    sides = rows_named.shape[1]
    part = depth // steps
    return pl.pallas_call(
        weights_kernel,
        out_shape=jax.ShapeDtypeStruct((sides, depth, width), BF16),
        grid=(steps,),
        in_specs=[
            pl.BlockSpec(rows_named.shape, lambda i: (0, 0)),
            pl.BlockSpec(coefficients_t.shape, lambda i: (0, 0)),
            pl.BlockSpec((bases, part, width), lambda i: (0, i, 0)),
        ],
        out_specs=pl.BlockSpec((sides, part, width), lambda i: (0, i, 0)),
        scratch_shapes=[pltpu.VMEM((2, sides * DIAGONAL, bases * DIAGONAL), BF16)],
        compiler_params=params(32),
        cost_estimate=cost(4 * 10**9, 2 * basis.size * 2),
        name="relation_weights",
    )(rows_named, coefficients_t, basis)


def normalised(mask, rows, dim):
    over = (((dim,), (0,)), ((), ()))
    summed = lax.dot_general(mask, rows, over, preferred_element_type=F32)
    degree = lax.dot_general(mask, jnp.ones((mask.shape[dim], LANES), BF16), over, preferred_element_type=F32)
    scale = (1.0 / (1.0 + degree)).astype(BF16).astype(F32)
    return (summed * jnp.concatenate([scale] * (rows.shape[1] // LANES), axis=1)).astype(BF16)


def block_at(index, size):
    return pl.ds(pl.multiple_of(index * size, size), size)


def inverse_kernel(entry_ref, live_ref, mask_ref, row_ref, weight_ref, rows_ref, keep_ref, send_ref, total):
    tiles, block, _ = mask_ref.shape
    total[...] = jnp.zeros_like(total)
    for tile in range(tiles):
        rows = row_ref[entry_ref[2, tile], :block, :]
        rows_ref[tile] = normalised(mask_ref[tile].astype(F32).astype(BF16), rows, 0)
    for tile in range(tiles):
        weighting = (tile < live_ref[0, 0]).astype(F32)
        message = jnp.dot(rows_ref[tile], weight_ref[tile], preferred_element_type=F32) * weighting
        total[block_at(entry_ref[1, tile], block), :] += message
    half = keep_ref.shape[0]
    keep_ref[...] = total[:half, :]
    send_ref[...] = total[half:, :].astype(BF16)


def inverse_messages(entries, live, mask, row_blocks, weights, row_count):
    tiles, block, _ = mask.shape
    width = row_blocks.shape[2]
    half = row_count * block // 2
    return pl.pallas_call(
        inverse_kernel,
        out_shape=(
            jax.ShapeDtypeStruct((tiles, block, width), BF16),
            jax.ShapeDtypeStruct((half, width), F32),
            jax.ShapeDtypeStruct((half, width), BF16),
        ),
        grid=(1,),
        in_specs=[
            SMEM,
            SMEM,
            pl.BlockSpec(mask.shape, lambda i: (0, 0, 0)),
            pl.BlockSpec(row_blocks.shape, lambda i: (0, 0, 0)),
            pl.BlockSpec((tiles, width, width), lambda i: (1, 0, 0)),
        ],
        out_specs=(
            pl.BlockSpec((tiles, block, width), lambda i: (0, 0, 0)),
            pl.BlockSpec((half, width), lambda i: (0, 0)),
            pl.BlockSpec((half, width), lambda i: (0, 0)),
        ),
        scratch_shapes=[pltpu.VMEM((2 * half, width), F32)],
        compiler_params=params(40),
        cost_estimate=cost(10**9, 8 * 10**6),
        name="inverse_messages",
    )(entries, live, mask, row_blocks, weights)


def forward_kernel(entry_ref, live_ref, rows_ref, weight_ref, part_ref, total):
    tiles, block, _ = rows_ref.shape
    total[...] = jnp.zeros_like(total)
    for tile in range(tiles):
        weighting = (tile < live_ref[0, 0]).astype(F32)
        message = jnp.dot(rows_ref[tile], weight_ref[tile], preferred_element_type=F32) * weighting
        total[entry_ref[2, tile]] += message
    part_ref[...] = total[...].astype(BF16)


def forward_messages(entries, live, rows, weights, column_count):
    tiles, block, width = rows.shape
    shape = (column_count, block, width)
    return pl.pallas_call(
        forward_kernel,
        out_shape=jax.ShapeDtypeStruct(shape, BF16),
        grid=(1,),
        in_specs=[
            SMEM,
            SMEM,
            pl.BlockSpec(rows.shape, lambda i: (0, 0, 0)),
            pl.BlockSpec((tiles, width, width), lambda i: (0, 0, 0)),
        ],
        out_specs=pl.BlockSpec(shape, lambda i: (0, 0, 0)),
        scratch_shapes=[pltpu.VMEM(shape, F32)],
        compiler_params=params(32),
        cost_estimate=cost(10**9, 4 * 10**6),
        name="forward_messages",
    )(entries, live, rows, weights)


def gradient_kernel(pieces, entry_ref, live_ref, core_ref, mask_ref, row_ref, inverse_ref, basis_ref, *refs):
    column_refs = refs[:pieces]
    rows_ref, mine_ref, other_ref = refs[pieces : pieces + 3]
    column, basis, moments, total, column_sem, basis_sem = refs[pieces + 3 :]
    tiles, block, _ = mask_ref.shape
    bases, depth, width = basis.shape
    sides = 2 * tiles
    size = column_refs[0].shape[0]
    copies = [
        pltpu.make_async_copy(ref, column.at[pl.ds(index * size, size)], column_sem.at[index])
        for index, ref in enumerate(column_refs)
    ]
    basis_copy = pltpu.make_async_copy(basis_ref, basis, basis_sem)
    for copy in copies:
        copy.start()
    basis_copy.start()
    for copy in copies:
        copy.wait()
    for tile in range(tiles):
        rows = column[entry_ref[1, tile], :block, :]
        rows_ref[tile] = normalised(mask_ref[tile].astype(F32).astype(BF16), rows, 1)
    over = (((0,), (0,)), ((), ()))
    for tile in range(tiles):
        target = row_ref[entry_ref[2, tile], block:, :]
        source = column[entry_ref[1, tile], block:, :]
        moments[tile] = lax.dot_general(rows_ref[tile], target, over, preferred_element_type=F32).astype(BF16)
        moments[tiles + tile] = lax.dot_general(
            inverse_ref[tile], source, over, preferred_element_type=F32
        ).astype(BF16)
    basis_copy.wait()
    tall, wide = bases * DIAGONAL, sides * DIAGONAL
    for start in range(0, depth, DIAGONAL):
        left = basis[:, start : start + DIAGONAL, :].reshape(tall, width)
        right = moments[:, start : start + DIAGONAL, :].reshape(wide, width)
        product = lax.dot_general(left, right, (((1,), (1,)), ((), ())), preferred_element_type=F32)
        if start == 0:
            total[...] = product
        else:
            total[...] += product
    same = iota((tall, wide), 0) % DIAGONAL == iota((tall, wide), 1) % DIAGONAL
    rows = (iota((bases, tall), 1) // DIAGONAL == iota((bases, tall), 0)).astype(BF16)
    columns = (iota((wide, sides), 0) // DIAGONAL == iota((wide, sides), 1)).astype(BF16)
    tower = jnp.zeros((bases, wide), F32)
    for part in split(jnp.where(same, total[...], 0.0)):
        tower += jnp.dot(rows, part, preferred_element_type=F32)
    per_tile = jnp.zeros((bases, sides), F32)
    for part in split(tower):
        per_tile += jnp.dot(part, columns, preferred_element_type=F32)
    live = live_ref[0, 0]
    per_tile = jnp.where(iota((bases, sides), 1) % tiles < live, per_tile, 0.0)
    first = core_ref[0] == 0
    forward, inverse = per_tile[:, :tiles], per_tile[:, tiles:]
    for ref, chosen in ((mine_ref, first), (other_ref, jnp.logical_not(first))):
        ref[:bases, :] = jnp.where(chosen, forward, inverse)
        ref[bases:, :] = jnp.zeros_like(ref[bases:, :])
        for tile in range(tiles):
            named = entry_ref[0, tile] + jnp.where(chosen, 0, entry_ref[3, tile])
            lane = iota((8, tiles), 1) == tile
            ref[bases:, :] = jnp.where(lane, named.astype(F32), ref[bases:, :])


def gradients(entries, live, core, mask, row_blocks, inverse_rows, basis, columns):
    tiles, block, _ = mask.shape
    bases, depth, width = basis.shape
    blocks = sum(piece.shape[0] for piece in columns)
    payload = jax.ShapeDtypeStruct((PAYLOAD, tiles), F32)
    return pl.pallas_call(
        functools.partial(gradient_kernel, len(columns)),
        out_shape=(jax.ShapeDtypeStruct((tiles, block, width), BF16), payload, payload),
        in_specs=[SMEM, SMEM, SMEM, VMEM, VMEM, VMEM, ANY] + [ANY] * len(columns),
        out_specs=(VMEM, VMEM, VMEM),
        scratch_shapes=[
            pltpu.VMEM((blocks, 2 * block, width), BF16),
            pltpu.VMEM(basis.shape, BF16),
            pltpu.VMEM((2 * tiles, depth, width), BF16),
            pltpu.VMEM((bases * DIAGONAL, 2 * tiles * DIAGONAL), F32),
            pltpu.SemaphoreType.DMA((len(columns),)),
            pltpu.SemaphoreType.DMA,
        ],
        compiler_params=params(48),
        cost_estimate=cost(4 * 10**9, 12 * 10**6),
        name="gradients",
    )(entries, live, core, mask, row_blocks, inverse_rows, basis, *columns)


def place_kernel(pieces, where_ref, *refs):
    piece_refs, out_ref, entries, total, sems = refs[:pieces], *refs[pieces:]
    bases, window = out_ref.shape
    span = entries.shape[2]
    per_piece = piece_refs[0].shape[1] // span
    copies = []
    for piece, ref in enumerate(piece_refs):
        for part in range(per_piece):
            index = piece * per_piece + part
            copies.append(
                pltpu.make_async_copy(
                    ref.at[:, pl.ds(part * span, span)], entries.at[where_ref[index]], sems.at[index]
                )
            )
    for copy in copies:
        copy.start()
    for copy in copies:
        copy.wait()
    total[...] = jnp.zeros_like(total)
    for index in range(entries.shape[0]):
        named = entries[index, bases : bases + 1, :].astype(jnp.int32)
        chosen = (iota((window, span), 0) == named).astype(F32).astype(BF16)
        high, low = split(entries[index, :bases, :])
        both = jnp.concatenate([high, low], axis=0)
        total[...] += lax.dot_general(both, chosen, (((1,), (1,)), ((), ())), preferred_element_type=F32)
    out_ref[...] = total[:bases, :] + total[bases:, :]


def place_rows(where, pieces, bases, window, span):
    count = where.shape[0]
    return pl.pallas_call(
        functools.partial(place_kernel, len(pieces)),
        out_shape=jax.ShapeDtypeStruct((bases, window), F32),
        in_specs=[SMEM] + [ANY] * len(pieces),
        out_specs=VMEM,
        scratch_shapes=[
            pltpu.VMEM((count, PAYLOAD, span), F32),
            pltpu.VMEM((2 * bases, window), F32),
            pltpu.SemaphoreType.DMA((count,)),
        ],
        compiler_params=params(32),
        cost_estimate=cost(10**9, 10**6),
        name="place_rows",
    )(where, *pieces)


X_HI, RING, CORES = 2, 8, 2
Y, X_LO = 4, 2


def from_row(array, dx=0, dz=0, dk=0):
    pairs = []
    for x in range(X_HI):
        for z in range(RING):
            for k in range(CORES):
                source = ((x ^ dx) * RING + (z + dz) % RING) * CORES + (k ^ dk)
                pairs.append((source, (x * RING + z) * CORES + k))
    return lax.ppermute(array, "prow", pairs)


def from_column(array, dy=0, dx=0):
    pairs = []
    for y in range(Y):
        for x in range(X_LO):
            pairs.append((((y + dy) % Y) * X_LO + (x ^ dx), y * X_LO + x))
    return lax.ppermute(array, "pcol", pairs)


def spread_rings(own, dim):
    def part(array, first):
        size = own.shape[dim]
        return lax.slice_in_dim(array, first * size, (first + 2) * size, axis=dim)

    even = jnp.concatenate([from_row(own, dz=6), own, from_row(own, dz=2), from_row(own, dz=4)], axis=dim)
    across = from_row(even, dx=1)
    up = from_row(jnp.concatenate([part(even, 1), part(across, 1)], axis=dim), dz=1)
    down = from_row(jnp.concatenate([part(even, 0), part(across, 0)], axis=dim), dz=7)
    return even, across, up, down


def piece_offsets():
    return (
        [(0, dz) for dz in (6, 0, 2, 4)]
        + [(1, dz) for dz in (6, 0, 2, 4)]
        + [(dx, dz) for dx in (0, 1) for dz in (1, 3)]
        + [(dx, dz) for dx in (0, 1) for dz in (5, 7)]
    )


def coordinates():
    row = lax.axis_index("prow")
    column = lax.axis_index("pcol")
    return row // (RING * CORES), (row // CORES) % RING, row % CORES, column // X_LO, column % X_LO


def column_position(source, x, z, k):
    dx = (source // (RING * CORES)) ^ x
    dz = ((source // CORES) % RING - z) % RING
    dk = (source % CORES) ^ k
    even = dx * 4 + ((dz + 2) % RING) // 2
    odd = 8 + 4 * (dz // 4) + 2 * dx + (dz % 4) // 2
    return dk * 16 + jnp.where(dz % 2 == 0, even, odd)


def ordered(first, own, other, dim):
    return jnp.concatenate([jnp.where(first, own, other), jnp.where(first, other, own)], axis=dim)


def reduce_inverse(keep, send, block):
    width = keep.shape[1]
    part = (keep + from_row(send, dk=1).astype(F32)).reshape(4, 4, block, width)
    up = from_row(part[2].astype(BF16), dz=7).astype(F32)
    down = from_row(part[3].astype(BF16), dz=1).astype(F32)

    def even(side):
        arrived_up, arrived_down = up[2 * side : 2 * side + 2], down[2 * side : 2 * side + 2]
        own = part[side]
        return jnp.stack([own[0] + arrived_down[0], own[1] + arrived_down[1] + arrived_up[0], own[2] + arrived_up[1], own[3]])

    total = even(0) + from_row(even(1).astype(BF16), dx=1).astype(F32)
    low = total.astype(BF16)
    arrived = from_row(low[0], dz=2), from_row(low[2], dz=6), from_row(low[3], dz=4)
    return total[1] + arrived[0].astype(F32) + arrived[1].astype(F32) + arrived[2].astype(F32)


def reduce_gradients(mine, other, place, relations, bases):
    x, z, k, y, x_lo = place
    entries = ordered(k == 0, mine, from_row(other, dk=1), 1)
    entries = ordered(x_lo == 0, entries, from_column(entries, dx=1), 1)
    around = [entries] + [from_column(entries, dy=dy) for dy in range(1, Y)]
    entries = jnp.concatenate(
        [functools.reduce(lambda a, dy: jnp.where(y == (at - dy) % Y, around[dy], a), range(1, Y), around[0]) for at in range(Y)],
        axis=1,
    )
    pieces = spread_rings(entries, 1)
    where = jnp.stack([(x ^ dx) * RING + (z + dz) % RING for dx, dz in piece_offsets()]).astype(jnp.int32)
    base = relations // LANES * LANES
    window = -(-(2 * relations - base) // LANES) * LANES
    own = place_rows(where, pieces, bases, window, entries.shape[1])
    partner = from_row(own, dk=1)
    low, high = jnp.where(k == 0, own, partner), jnp.where(k == 0, partner, own)
    shared = window - base
    full = jnp.concatenate([low[:, :base], low[:, base:] + high[:, :shared], high[:, shared:]], axis=1)
    return full[:, : 2 * relations].T


def on_device(features, cotangent, self_weight, basis_weights, coefficients, tile_list, tile_mask, live_tiles):
    block, width = features.shape
    relations = coefficients.shape[0] // 2
    bases = coefficients.shape[1]
    place = coordinates()
    x, z, k, _, _ = place
    mask = tile_mask[0, 0]
    relation, source, target = tile_list[0, 0, :, 0], tile_list[0, 0, :, 1], tile_list[0, 0, :, 2]
    shift = jnp.full_like(relation, relations % LANES)
    entries = jnp.stack([relation, column_position(source, x, z, k), target, shift])
    both = jnp.concatenate([features, cotangent], axis=0)[None]

    row_blocks = lax.all_to_all(jnp.broadcast_to(both, (Y * X_LO,) + both.shape[1:]), "pcol", 0, 0, tiled=True)
    near = spread_rings(both, 0)
    columns = near + tuple(from_row(piece, dk=1) for piece in near)
    rows_named = jnp.concatenate([relation, relation + relations])[None]
    weights = relation_weights(rows_named, coefficients.T, basis_weights)
    inverse_rows, keep, send = inverse_messages(entries, live_tiles, mask, row_blocks, weights, X_HI * RING * CORES)
    inverse_total = reduce_inverse(keep, send, block)
    forward_rows, mine, other = gradients(
        entries, live_tiles, k.reshape(1), mask, row_blocks, inverse_rows, basis_weights, columns
    )
    coefficient_grads = reduce_gradients(mine, other, place, relations, bases)
    forward_part = forward_messages(entries, live_tiles, forward_rows, weights, Y * X_LO)
    forward_total = jnp.sum(lax.all_to_all(forward_part, "pcol", 0, 0, tiled=True).astype(F32), axis=0)
    self_term = jnp.dot(features, self_weight, preferred_element_type=F32)
    layer_output = (self_term + forward_total + inverse_total).astype(BF16)
    return layer_output, coefficient_grads


def solution(mesh):
    return jax.shard_map(
        on_device,
        mesh=mesh,
        in_specs=(
            P(("prow", "pcol"), None),
            P(("prow", "pcol"), None),
            P(),
            P(),
            P(),
            P("prow", "pcol", None, None),
            P("prow", "pcol", None, None, None),
            P("prow", "pcol"),
        ),
        out_specs=(P(("prow", "pcol"), None), P()),
        check_vma=False,
    )
```

```python
import functools
import jax
import jax.numpy as jnp
from jax import lax
from jax.experimental import pallas as pl
from jax.experimental.pallas import tpu as pltpu
from jax.sharding import PartitionSpec as P

F32, BF16 = jnp.float32, jnp.bfloat16
VMEM = pl.BlockSpec(memory_space=pltpu.VMEM)
SMEM = pl.BlockSpec(memory_space=pltpu.SMEM)
ANY = pl.BlockSpec(memory_space=pl.ANY)
HBM = pl.BlockSpec(memory_space=pltpu.HBM)
LANES = 128
DIAGONAL = 16
PAYLOAD = 48


def params(mib):
    return pltpu.CompilerParams(vmem_limit_bytes=mib * 1024 * 1024)


def cost(flops, moved):
    return pl.CostEstimate(flops=flops, bytes_accessed=moved, transcendentals=0)


def split(wide):
    high = wide.astype(BF16)
    return high, (wide - high.astype(F32)).astype(BF16)


def iota(shape, dim):
    return lax.broadcasted_iota(jnp.int32, shape, dim)


def weights_kernel(parts, row_ref, coefficient_ref, basis_ref, weight_ref, spread, basis, weight, in_sems, out_sems):
    bases, named = coefficient_ref.shape
    sides = row_ref.shape[1]
    depth, width = basis.shape[1:]
    size = depth // parts
    tall, wide = sides * DIAGONAL, bases * DIAGONAL
    arrive, leave = [], []
    for part in range(parts):
        rows = pl.ds(part * size, size)
        arrive.append(pltpu.make_async_copy(basis_ref.at[:, rows, :], basis.at[:, rows, :], in_sems.at[part]))
        leave.append(pltpu.make_async_copy(weight.at[:, rows, :], weight_ref.at[:, rows, :], out_sems.at[part]))
    for copy in arrive:
        copy.start()
    chosen = (iota((named, sides), 0) == row_ref[...]).astype(F32).astype(BF16)
    rows = (iota((tall, sides), 0) // DIAGONAL == iota((tall, sides), 1)).astype(F32).astype(BF16)
    columns = (iota((bases, wide), 1) // DIAGONAL == iota((bases, wide), 0)).astype(F32).astype(BF16)
    same = iota((tall, wide), 0) % DIAGONAL == iota((tall, wide), 1) % DIAGONAL
    for index, part in enumerate(split(coefficient_ref[...])):
        picked = jnp.dot(part, chosen, preferred_element_type=F32).astype(BF16)
        tower = lax.dot_general(rows, picked, (((1,), (1,)), ((), ())), preferred_element_type=F32).astype(BF16)
        full = jnp.dot(tower, columns, preferred_element_type=F32)
        spread[index] = jnp.where(same, full, 0.0).astype(BF16)
    for start in range(0, depth, DIAGONAL):
        if start % size == 0:
            arrive[start // size].wait()
        part = basis[:, start : start + DIAGONAL, :].reshape(wide, width)
        total = jnp.dot(spread[0], part, preferred_element_type=F32)
        total += jnp.dot(spread[1], part, preferred_element_type=F32)
        weight[:, start : start + DIAGONAL, :] = total.astype(BF16).reshape(sides, DIAGONAL, width)
        if (start + DIAGONAL) % size == 0:
            leave[start // size].start()
    for copy in leave:
        copy.wait()


def relation_weights(rows_named, coefficients_t, basis, parts=4):
    bases, depth, width = basis.shape
    sides = rows_named.shape[1]
    return pl.pallas_call(
        functools.partial(weights_kernel, parts),
        out_shape=jax.ShapeDtypeStruct((sides, depth, width), BF16),
        in_specs=[VMEM, VMEM, HBM],
        out_specs=HBM,
        scratch_shapes=[
            pltpu.VMEM((2, sides * DIAGONAL, bases * DIAGONAL), BF16),
            pltpu.VMEM(basis.shape, BF16),
            pltpu.VMEM((sides, depth, width), BF16),
            pltpu.SemaphoreType.DMA((parts,)),
            pltpu.SemaphoreType.DMA((parts,)),
        ],
        compiler_params=params(56),
        cost_estimate=cost(4 * 10**9, 2 * basis.size * 2),
        name="relation_weights",
    )(rows_named, coefficients_t, basis)


def normalised(mask, rows, dim):
    over = (((dim,), (0,)), ((), ()))
    summed = lax.dot_general(mask, rows, over, preferred_element_type=F32)
    degree = lax.dot_general(mask, jnp.ones((mask.shape[dim], LANES), BF16), over, preferred_element_type=F32)
    scale = (1.0 / (1.0 + degree)).astype(BF16).astype(F32)
    return (summed * jnp.concatenate([scale] * (rows.shape[1] // LANES), axis=1)).astype(BF16)


def block_at(index, size):
    return pl.ds(pl.multiple_of(index * size, size), size)


def inverse_kernel(
    entry_ref, live_ref, mask_ref, row_ref, weights_ref, rows_ref, keep_ref, send_ref, total, weight_ref, sem
):
    tiles, block, _ = mask_ref.shape
    copy = pltpu.make_async_copy(weights_ref.at[pl.ds(tiles, tiles)], weight_ref, sem)
    copy.start()
    total[...] = jnp.zeros_like(total)
    for tile in range(tiles):
        rows = row_ref[entry_ref[2, tile], :block, :]
        rows_ref[tile] = normalised(mask_ref[tile].astype(F32).astype(BF16), rows, 0)
    copy.wait()
    for tile in range(tiles):
        weighting = (tile < live_ref[0, 0]).astype(F32)
        message = jnp.dot(rows_ref[tile], weight_ref[tile], preferred_element_type=F32) * weighting
        total[block_at(entry_ref[4, tile], block), :] += message
    half = keep_ref.shape[0]
    keep_ref[...] = total[:half, :]
    send_ref[...] = total[half:, :].astype(BF16)


def inverse_messages(entries, live, mask, row_blocks, weights, row_count):
    tiles, block, _ = mask.shape
    width = row_blocks.shape[2]
    half = row_count * block // 2
    return pl.pallas_call(
        inverse_kernel,
        out_shape=(
            jax.ShapeDtypeStruct((tiles, block, width), BF16),
            jax.ShapeDtypeStruct((half, width), F32),
            jax.ShapeDtypeStruct((half, width), BF16),
        ),
        in_specs=[SMEM, SMEM, VMEM, VMEM, HBM],
        out_specs=(VMEM, VMEM, VMEM),
        scratch_shapes=[
            pltpu.VMEM((2 * half, width), F32),
            pltpu.VMEM((tiles, width, width), BF16),
            pltpu.SemaphoreType.DMA,
        ],
        compiler_params=params(56),
        cost_estimate=cost(10**9, 8 * 10**6),
        name="inverse_messages",
    )(entries, live, mask, row_blocks, weights)


def forward_kernel(entry_ref, live_ref, rows_ref, weights_ref, part_ref, total, weight_ref, sem):
    tiles, block, _ = rows_ref.shape
    copy = pltpu.make_async_copy(weights_ref.at[pl.ds(0, tiles)], weight_ref, sem)
    copy.start()
    total[...] = jnp.zeros_like(total)
    copy.wait()
    for tile in range(tiles):
        weighting = (tile < live_ref[0, 0]).astype(F32)
        message = jnp.dot(rows_ref[tile], weight_ref[tile], preferred_element_type=F32) * weighting
        total[entry_ref[2, tile]] += message
    part_ref[...] = total[...].astype(BF16)


def forward_messages(entries, live, rows, weights, column_count):
    tiles, block, width = rows.shape
    shape = (column_count, block, width)
    return pl.pallas_call(
        forward_kernel,
        out_shape=jax.ShapeDtypeStruct(shape, BF16),
        in_specs=[SMEM, SMEM, VMEM, HBM],
        out_specs=VMEM,
        scratch_shapes=[
            pltpu.VMEM(shape, F32),
            pltpu.VMEM((tiles, width, width), BF16),
            pltpu.SemaphoreType.DMA,
        ],
        compiler_params=params(56),
        cost_estimate=cost(10**9, 4 * 10**6),
        name="forward_messages",
    )(entries, live, rows, weights)


def gradient_kernel(pieces, entry_ref, live_ref, core_ref, mask_ref, row_ref, inverse_ref, basis_ref, *refs):
    column_refs = refs[:pieces]
    rows_ref, mine_ref, other_ref = refs[pieces : pieces + 3]
    column, basis, moments, total, column_sem, basis_sem = refs[pieces + 3 :]
    tiles, block, _ = mask_ref.shape
    bases, depth, width = basis.shape
    sides = 2 * tiles
    size = column_refs[0].shape[0]
    copies = [
        pltpu.make_async_copy(ref, column.at[pl.ds(index * size, size)], column_sem.at[index])
        for index, ref in enumerate(column_refs)
    ]
    basis_copy = pltpu.make_async_copy(basis_ref, basis, basis_sem)
    for copy in copies:
        copy.start()
    basis_copy.start()
    for copy in copies:
        copy.wait()
    for tile in range(tiles):
        rows = column[entry_ref[1, tile], :block, :]
        rows_ref[tile] = normalised(mask_ref[tile].astype(F32).astype(BF16), rows, 1)
    over = (((0,), (0,)), ((), ()))
    for tile in range(tiles):
        target = row_ref[entry_ref[2, tile], block:, :]
        source = column[entry_ref[1, tile], block:, :]
        moments[tile] = lax.dot_general(rows_ref[tile], target, over, preferred_element_type=F32).astype(BF16)
        moments[tiles + tile] = lax.dot_general(
            inverse_ref[tile], source, over, preferred_element_type=F32
        ).astype(BF16)
    basis_copy.wait()
    tall, wide = bases * DIAGONAL, sides * DIAGONAL
    for start in range(0, depth, DIAGONAL):
        left = basis[:, start : start + DIAGONAL, :].reshape(tall, width)
        right = moments[:, start : start + DIAGONAL, :].reshape(wide, width)
        product = lax.dot_general(left, right, (((1,), (1,)), ((), ())), preferred_element_type=F32)
        if start == 0:
            total[...] = product
        else:
            total[...] += product
    same = iota((tall, wide), 0) % DIAGONAL == iota((tall, wide), 1) % DIAGONAL
    rows = (iota((bases, tall), 1) // DIAGONAL == iota((bases, tall), 0)).astype(BF16)
    columns = (iota((wide, sides), 0) // DIAGONAL == iota((wide, sides), 1)).astype(BF16)
    tower = jnp.zeros((bases, wide), F32)
    for part in split(jnp.where(same, total[...], 0.0)):
        tower += jnp.dot(rows, part, preferred_element_type=F32)
    per_tile = jnp.zeros((bases, sides), F32)
    for part in split(tower):
        per_tile += jnp.dot(part, columns, preferred_element_type=F32)
    live = live_ref[0, 0]
    per_tile = jnp.where(iota((bases, sides), 1) % tiles < live, per_tile, 0.0)
    first = core_ref[0] == 0
    forward, inverse = per_tile[:, :tiles], per_tile[:, tiles:]
    names = iota((PAYLOAD - bases, tiles), 0)
    lane = iota((PAYLOAD - bases, tiles), 1)
    for ref, chosen in ((mine_ref, first), (other_ref, jnp.logical_not(first))):
        ref[:bases, :] = jnp.where(chosen, forward, inverse).astype(BF16)
        named = jnp.zeros((PAYLOAD - bases, tiles), jnp.int32)
        for tile in range(tiles):
            name = entry_ref[0, tile] + jnp.where(chosen, 0, entry_ref[3, tile])
            digits = jnp.where(names == 0, name // LANES, jnp.where(names == 1, name % LANES, 0))
            named = jnp.where(lane == tile, digits, named)
        ref[bases:, :] = named.astype(F32).astype(BF16)


def gradients(entries, live, core, mask, row_blocks, inverse_rows, basis, columns):
    tiles, block, _ = mask.shape
    bases, depth, width = basis.shape
    blocks = sum(piece.shape[0] for piece in columns)
    payload = jax.ShapeDtypeStruct((PAYLOAD, tiles), BF16)
    return pl.pallas_call(
        functools.partial(gradient_kernel, len(columns)),
        out_shape=(jax.ShapeDtypeStruct((tiles, block, width), BF16), payload, payload),
        in_specs=[SMEM, SMEM, SMEM, VMEM, VMEM, VMEM, HBM] + [ANY] * len(columns),
        out_specs=(VMEM, VMEM, VMEM),
        scratch_shapes=[
            pltpu.VMEM((blocks, 2 * block, width), BF16),
            pltpu.VMEM(basis.shape, BF16),
            pltpu.VMEM((2 * tiles, depth, width), BF16),
            pltpu.VMEM((bases * DIAGONAL, 2 * tiles * DIAGONAL), F32),
            pltpu.SemaphoreType.DMA((len(columns),)),
            pltpu.SemaphoreType.DMA,
        ],
        compiler_params=params(52),
        cost_estimate=cost(4 * 10**9, 12 * 10**6),
        name="gradients",
    )(entries, live, core, mask, row_blocks, inverse_rows, basis, *columns)


def place_kernel(entry_ref, out_ref, total):
    bases, window = out_ref.shape
    count, _, span = entry_ref.shape
    for index in range(count):
        values = entry_ref[index, :bases, :].astype(F32)
        names = entry_ref[index, bases:, :].astype(F32)
        high, low = names[:1], names[1:2]
        chosen = (iota((LANES, span), 0).astype(F32) == low).astype(F32).astype(BF16)
        spread = [jnp.where(high == part, values, 0.0).astype(BF16) for part in range(window // LANES)]
        product = lax.dot_general(
            jnp.concatenate(spread, axis=0), chosen, (((1,), (1,)), ((), ())), preferred_element_type=F32
        )
        if index == 0:
            total[...] = product
        else:
            total[...] += product
    for part in range(window // LANES):
        out_ref[:, part * LANES : part * LANES + LANES] = total[part * bases : part * bases + bases, :]


def place_rows(entries, bases, window):
    return pl.pallas_call(
        place_kernel,
        out_shape=jax.ShapeDtypeStruct((bases, window), F32),
        in_specs=[VMEM],
        out_specs=VMEM,
        scratch_shapes=[pltpu.VMEM((window // LANES * bases, LANES), F32)],
        compiler_params=params(16),
        cost_estimate=cost(10**9, 10**6),
        name="place_rows",
    )(entries)


def join_kernel(plan, count, *refs):
    sems = refs[-1]
    copies = []
    for output, pieces in enumerate(plan):
        at = 0
        for source, start, size in pieces:
            copies.append(
                pltpu.make_async_copy(
                    refs[source].at[pl.ds(start, size)],
                    refs[count + output].at[pl.ds(at, size)],
                    sems.at[len(copies)],
                )
            )
            at += size
    for copy in copies:
        copy.start()
    for copy in copies:
        copy.wait()


def join(sources, plan):
    shape = sources[0].shape[1:]
    sizes = [sum(size for _, _, size in pieces) for pieces in plan]
    return pl.pallas_call(
        functools.partial(join_kernel, plan, len(sources)),
        out_shape=tuple(jax.ShapeDtypeStruct((size,) + shape, sources[0].dtype) for size in sizes),
        in_specs=[ANY] * len(sources),
        out_specs=tuple(ANY for _ in plan),
        scratch_shapes=[pltpu.SemaphoreType.DMA((sum(len(pieces) for pieces in plan),))],
        compiler_params=params(4),
        cost_estimate=cost(0, 10**6),
        name="join",
    )(*sources)


def finish_kernel(base, core_ref, own_ref, partner_ref, out_ref):
    window = own_ref.shape[1]
    shared = window - base
    last = out_ref.shape[1]
    first = core_ref[0] == 0
    out_ref[:, :base] = jnp.where(first, own_ref[:, :base], partner_ref[:, :base])
    out_ref[:, base:window] = jnp.where(first, own_ref[:, base:], partner_ref[:, base:]) + jnp.where(
        first, partner_ref[:, :shared], own_ref[:, :shared]
    )
    out_ref[:, window:] = jnp.where(
        first, partner_ref[:, shared : last - base], own_ref[:, shared : last - base]
    )


def finish(core, own, partner, base, relations):
    return pl.pallas_call(
        functools.partial(finish_kernel, base),
        out_shape=jax.ShapeDtypeStruct((own.shape[0], 2 * relations), F32),
        in_specs=[SMEM, VMEM, VMEM],
        out_specs=VMEM,
        compiler_params=params(8),
        cost_estimate=cost(0, 10**6),
        name="finish",
    )(core, own, partner)


def pack_kernel(feature_ref, cotangent_ref, own_ref, copies_ref):
    block = feature_ref.shape[0]
    for start, ref in ((0, feature_ref), (block, cotangent_ref)):
        own_ref[0, start : start + block, :] = ref[...]
        for copy in range(copies_ref.shape[0]):
            copies_ref[copy, start : start + block, :] = ref[...]


def pack(features, cotangent, count):
    block, width = features.shape
    return pl.pallas_call(
        pack_kernel,
        out_shape=(
            jax.ShapeDtypeStruct((1, 2 * block, width), BF16),
            jax.ShapeDtypeStruct((count, 2 * block, width), BF16),
        ),
        in_specs=[VMEM, VMEM],
        out_specs=(VMEM, VMEM),
        compiler_params=params(8),
        cost_estimate=cost(0, 10**6),
        name="pack",
    )(features, cotangent)


X_HI, RING, CORES = 2, 8, 2
Y, X_LO = 4, 2


def from_row(array, dx=0, dz=0, dk=0):
    pairs = []
    for x in range(X_HI):
        for z in range(RING):
            for k in range(CORES):
                source = ((x ^ dx) * RING + (z + dz) % RING) * CORES + (k ^ dk)
                pairs.append((source, (x * RING + z) * CORES + k))
    return lax.ppermute(array, "prow", pairs)


def from_column(array, dy=0, dx=0):
    pairs = []
    for y in range(Y):
        for x in range(X_LO):
            pairs.append((((y + dy) % Y) * X_LO + (x ^ dx), y * X_LO + x))
    return lax.ppermute(array, "pcol", pairs)


def tie(*arrays):
    return lax.optimization_barrier(arrays)


def coordinates():
    row = lax.axis_index("prow")
    column = lax.axis_index("pcol")
    return row // (RING * CORES), (row // CORES) % RING, row % CORES, column // X_LO, column % X_LO


def column_position(source, x, z, k):
    dx = (source // (RING * CORES)) ^ x
    dz = ((source // CORES) % RING - z) % RING
    dk = (source % CORES) ^ k
    even = dx * 4 + ((dz + 2) % RING) // 2
    odd = 8 + 4 * (dz // 4) + 2 * dx + (dz % 4) // 2
    return dk * 16 + jnp.where(dz % 2 == 0, even, odd)


def ordered(first, own, other, dim):
    return jnp.concatenate([jnp.where(first, own, other), jnp.where(first, other, own)], axis=dim)


def row_groups(over_x):
    def at(x, z, k):
        return (x * RING + z) * CORES + k

    if over_x:
        return [[at(x, z, k) for x in range(X_HI) for z in range(RING)] for k in range(CORES)]
    return [[at(x, z, k) for z in range(RING)] for x in range(X_HI) for k in range(CORES)]


def reduce_gradients(mine, arrived, forward_part, place, relations, bases):
    _, _, k, y, x_lo = place
    entries = ordered(k == 0, mine, arrived, 1)
    entries = ordered(x_lo == 0, entries, from_column(entries, dx=1), 1)
    around = [entries] + [from_column(entries, dy=dy) for dy in range(1, Y)]
    entries = jnp.concatenate(
        [functools.reduce(lambda a, dy: jnp.where(y == (at - dy) % Y, around[dy], a), range(1, Y), around[0]) for at in range(Y)],
        axis=1,
    )
    copies = jnp.broadcast_to(entries[None], (X_HI * RING,) + entries.shape)
    copies, forward_part = tie(copies, forward_part)
    gathered = lax.all_to_all(copies, "prow", 0, 0, tiled=True, axis_index_groups=row_groups(True))
    base = relations // LANES * LANES
    window = -(-(2 * relations - base) // LANES) * LANES
    own = place_rows(gathered, bases, window)
    return finish(k.reshape(1), own, from_row(own, dk=1), base, relations).T, forward_part


def on_device(features, cotangent, self_weight, basis_weights, coefficients, tile_list, tile_mask, live_tiles):
    block, width = features.shape
    relations = coefficients.shape[0] // 2
    bases = coefficients.shape[1]
    columns_count, rows_count = Y * X_LO, X_HI * RING * CORES
    place = coordinates()
    x, z, k, _, _ = place
    mask = tile_mask[0, 0]
    relation, source, target = tile_list[0, 0, :, 0], tile_list[0, 0, :, 1], tile_list[0, 0, :, 2]
    apart = ((source % CORES) ^ k) * RING + (source // CORES) % RING
    entries = jnp.stack(
        [
            relation,
            column_position(source, x, z, k),
            target,
            jnp.full_like(relation, relations % LANES),
            apart * X_HI + ((source // (RING * CORES)) ^ x),
        ]
    )
    rows_named = jnp.concatenate([relation, relation + relations])[None]

    own, copies = pack(features, cotangent, columns_count)
    ring = [from_row(own, dz=6), from_row(own, dz=2), from_row(own, dz=4)]
    row_blocks = lax.all_to_all(copies, "pcol", 0, 0, tiled=True)
    weights = relation_weights(rows_named, coefficients.T, basis_weights)
    *ring, weights = tie(*ring, weights)
    (even,) = join([ring[0], own, ring[1], ring[2]], (((0, 0, 1), (1, 0, 1), (2, 0, 1), (3, 0, 1)),))
    across = from_row(even, dx=1)
    inverse_rows, keep, send = inverse_messages(entries, live_tiles, mask, row_blocks, weights, rows_count)
    across, inverse_rows, keep, send = tie(across, inverse_rows, keep, send)
    upward, downward = join([even, across], (((0, 1, 2), (1, 1, 2)), ((0, 0, 2), (1, 0, 2))))
    up, down = from_row(upward, dz=1), from_row(downward, dz=7)
    near = (even, across, up, down)
    columns = near + tuple(from_row(piece, dk=1) for piece in near)
    inverse_part = keep + from_row(send, dk=1).astype(F32)
    *columns, inverse_part = tie(*columns, inverse_part)
    inverse_pair = lax.psum_scatter(
        inverse_part, "prow", scatter_dimension=0, tiled=True, axis_index_groups=row_groups(False)
    )
    inverse_total = inverse_pair[:block] + from_row(inverse_pair[block:], dx=1)
    forward_rows, mine, other = gradients(
        entries, live_tiles, k.reshape(1), mask, row_blocks, inverse_rows, basis_weights, columns
    )
    forward_part = forward_messages(entries, live_tiles, forward_rows, weights, columns_count)
    arrived, forward_part = tie(from_row(other, dk=1), forward_part)
    coefficient_grads, forward_part = reduce_gradients(mine, arrived, forward_part, place, relations, bases)
    forward_total = jnp.sum(lax.all_to_all(forward_part, "pcol", 0, 0, tiled=True).astype(F32), axis=0)
    self_term = jnp.dot(features, self_weight, preferred_element_type=F32)
    layer_output = (self_term + forward_total + inverse_total).astype(BF16)
    return layer_output, coefficient_grads


def solution(mesh):
    return jax.shard_map(
        on_device,
        mesh=mesh,
        in_specs=(
            P(("prow", "pcol"), None),
            P(("prow", "pcol"), None),
            P(),
            P(),
            P(),
            P("prow", "pcol", None, None),
            P("prow", "pcol", None, None, None),
            P("prow", "pcol"),
        ),
        out_specs=(P(("prow", "pcol"), None), P()),
        check_vma=False,
    )
```

```python
import functools
import jax
import jax.numpy as jnp
from jax import lax
from jax.experimental import pallas as pl
from jax.experimental.pallas import tpu as pltpu
from jax.sharding import PartitionSpec as P

F32, BF16 = jnp.float32, jnp.bfloat16
VMEM = pl.BlockSpec(memory_space=pltpu.VMEM)
SMEM = pl.BlockSpec(memory_space=pltpu.SMEM)
ANY = pl.BlockSpec(memory_space=pl.ANY)
HBM = pl.BlockSpec(memory_space=pltpu.HBM)
LANES = 128
DIAGONAL = 16
PAYLOAD = 48


def params(mib):
    return pltpu.CompilerParams(vmem_limit_bytes=mib * 1024 * 1024)


def cost(flops, moved):
    return pl.CostEstimate(flops=flops, bytes_accessed=moved, transcendentals=0)


def split(wide):
    high = wide.astype(BF16)
    return high, (wide - high.astype(F32)).astype(BF16)


def iota(shape, dim):
    return lax.broadcasted_iota(jnp.int32, shape, dim)


def weights_kernel(parts, row_ref, coefficient_ref, basis_ref, weight_ref, spread, basis, weight, in_sems, out_sems):
    bases, named = coefficient_ref.shape
    sides = row_ref.shape[1]
    depth, width = basis.shape[1:]
    size = depth // parts
    tall, wide = sides * DIAGONAL, bases * DIAGONAL
    arrive, leave = [], []
    for part in range(parts):
        rows = pl.ds(part * size, size)
        arrive.append(pltpu.make_async_copy(basis_ref.at[:, rows, :], basis.at[:, rows, :], in_sems.at[part]))
        leave.append(pltpu.make_async_copy(weight.at[:, rows, :], weight_ref.at[:, rows, :], out_sems.at[part]))
    for copy in arrive:
        copy.start()
    chosen = (iota((named, sides), 0) == row_ref[...]).astype(F32).astype(BF16)
    rows = (iota((tall, sides), 0) // DIAGONAL == iota((tall, sides), 1)).astype(F32).astype(BF16)
    columns = (iota((bases, wide), 1) // DIAGONAL == iota((bases, wide), 0)).astype(F32).astype(BF16)
    same = iota((tall, wide), 0) % DIAGONAL == iota((tall, wide), 1) % DIAGONAL
    for index, part in enumerate(split(coefficient_ref[...])):
        picked = jnp.dot(part, chosen, preferred_element_type=F32).astype(BF16)
        tower = lax.dot_general(rows, picked, (((1,), (1,)), ((), ())), preferred_element_type=F32).astype(BF16)
        full = jnp.dot(tower, columns, preferred_element_type=F32)
        spread[index] = jnp.where(same, full, 0.0).astype(BF16)
    for start in range(0, depth, DIAGONAL):
        if start % size == 0:
            arrive[start // size].wait()
        part = basis[:, start : start + DIAGONAL, :].reshape(wide, width)
        total = jnp.dot(spread[0], part, preferred_element_type=F32)
        total += jnp.dot(spread[1], part, preferred_element_type=F32)
        weight[:, start : start + DIAGONAL, :] = total.astype(BF16).reshape(sides, DIAGONAL, width)
        if (start + DIAGONAL) % size == 0:
            leave[start // size].start()
    for copy in leave:
        copy.wait()


def relation_weights(rows_named, coefficients_t, basis, parts=4):
    bases, depth, width = basis.shape
    sides = rows_named.shape[1]
    return pl.pallas_call(
        functools.partial(weights_kernel, parts),
        out_shape=jax.ShapeDtypeStruct((sides, depth, width), BF16),
        in_specs=[VMEM, VMEM, HBM],
        out_specs=HBM,
        scratch_shapes=[
            pltpu.VMEM((2, sides * DIAGONAL, bases * DIAGONAL), BF16),
            pltpu.VMEM(basis.shape, BF16),
            pltpu.VMEM((sides, depth, width), BF16),
            pltpu.SemaphoreType.DMA((parts,)),
            pltpu.SemaphoreType.DMA((parts,)),
        ],
        compiler_params=params(56),
        cost_estimate=cost(4 * 10**9, 2 * basis.size * 2),
        name="relation_weights",
    )(rows_named, coefficients_t, basis)


def normalised(mask, rows, dim):
    over = (((dim,), (0,)), ((), ()))
    summed = lax.dot_general(mask, rows, over, preferred_element_type=F32)
    degree = lax.dot_general(mask, jnp.ones((mask.shape[dim], LANES), BF16), over, preferred_element_type=F32)
    scale = (1.0 / (1.0 + degree)).astype(BF16).astype(F32)
    return (summed * jnp.concatenate([scale] * (rows.shape[1] // LANES), axis=1)).astype(BF16)


def copies_into(target, refs, sems):
    copies, at = [], 0
    for index, ref in enumerate(refs):
        size = ref.shape[0]
        copies.append(pltpu.make_async_copy(ref, target.at[pl.ds(at, size)], sems.at[index]))
        at += size
    for copy in copies:
        copy.start()
    return copies


def block_at(index, size):
    return pl.ds(pl.multiple_of(index * size, size), size)


def inverse_kernel(pieces, entry_ref, live_ref, mask_ref, weights_ref, *refs):
    rows_ref, keep_ref, send_ref, total, row, weight, row_sems, sem = refs[pieces:]
    tiles, block, _ = mask_ref.shape
    arrive = copies_into(row, refs[:pieces], row_sems)
    copy = pltpu.make_async_copy(weights_ref.at[pl.ds(tiles, tiles)], weight, sem)
    copy.start()
    total[...] = jnp.zeros_like(total)
    for part in arrive:
        part.wait()
    for tile in range(tiles):
        rows = row[entry_ref[2, tile], :block, :]
        rows_ref[tile] = normalised(mask_ref[tile].astype(F32).astype(BF16), rows, 0)
    copy.wait()
    for tile in range(tiles):
        weighting = (tile < live_ref[0, 0]).astype(F32)
        message = jnp.dot(rows_ref[tile], weight[tile], preferred_element_type=F32) * weighting
        total[block_at(entry_ref[4, tile], block), :] += message
    half = keep_ref.shape[0]
    keep_ref[...] = total[:half, :]
    send_ref[...] = total[half:, :].astype(BF16)


def inverse_messages(entries, live, mask, row_pieces, weights, row_count):
    tiles, block, _ = mask.shape
    width = row_pieces[0].shape[2]
    half = row_count * block // 2
    columns = sum(piece.shape[0] for piece in row_pieces)
    return pl.pallas_call(
        functools.partial(inverse_kernel, len(row_pieces)),
        out_shape=(
            jax.ShapeDtypeStruct((tiles, block, width), BF16),
            jax.ShapeDtypeStruct((half, width), F32),
            jax.ShapeDtypeStruct((half, width), BF16),
        ),
        in_specs=[SMEM, SMEM, VMEM, HBM] + [ANY] * len(row_pieces),
        out_specs=(VMEM, VMEM, VMEM),
        scratch_shapes=[
            pltpu.VMEM((2 * half, width), F32),
            pltpu.VMEM((columns,) + row_pieces[0].shape[1:], BF16),
            pltpu.VMEM((tiles, width, width), BF16),
            pltpu.SemaphoreType.DMA((len(row_pieces),)),
            pltpu.SemaphoreType.DMA,
        ],
        compiler_params=params(52),
        cost_estimate=cost(10**9, 8 * 10**6),
        name="inverse_messages",
    )(entries, live, mask, weights, *row_pieces)


def forward_kernel(entry_ref, live_ref, rows_ref, weights_ref, keep_ref, *refs):
    send_refs, (total, weight, sem) = refs[:-3], refs[-3:]
    tiles, block, _ = rows_ref.shape
    copy = pltpu.make_async_copy(weights_ref.at[pl.ds(0, tiles)], weight, sem)
    copy.start()
    total[...] = jnp.zeros_like(total)
    copy.wait()
    for tile in range(tiles):
        weighting = (tile < live_ref[0, 0]).astype(F32)
        message = jnp.dot(rows_ref[tile], weight[tile], preferred_element_type=F32) * weighting
        total[entry_ref[2, tile]] += message
    pair = keep_ref.shape[0]
    keep_ref[...] = total[:pair]
    for index, ref in enumerate(send_refs):
        ref[...] = total[pair * (index + 1) : pair * (index + 2)].astype(BF16)


def forward_messages(entries, live, rows, weights):
    tiles, block, width = rows.shape
    shape = (X_LO, block, width)
    return pl.pallas_call(
        forward_kernel,
        out_shape=(jax.ShapeDtypeStruct(shape, F32),) + (jax.ShapeDtypeStruct(shape, BF16),) * (Y - 1),
        in_specs=[SMEM, SMEM, VMEM, HBM],
        out_specs=(VMEM,) * Y,
        scratch_shapes=[
            pltpu.VMEM((Y * X_LO, block, width), F32),
            pltpu.VMEM((tiles, width, width), BF16),
            pltpu.SemaphoreType.DMA,
        ],
        compiler_params=params(56),
        cost_estimate=cost(10**9, 4 * 10**6),
        name="forward_messages",
    )(entries, live, rows, weights)


def gradient_kernel(pieces, row_pieces, entry_ref, live_ref, core_ref, mask_ref, inverse_ref, basis_ref, *refs):
    column_refs, row_refs, refs = refs[:pieces], refs[pieces : pieces + row_pieces], refs[pieces + row_pieces :]
    rows_ref, mine_ref, other_ref, column, row, basis, moments, total, column_sem, row_sem, basis_sem = refs
    tiles, block, _ = mask_ref.shape
    bases, depth, width = basis.shape
    sides = 2 * tiles
    copies = copies_into(column, column_refs, column_sem) + copies_into(row, row_refs, row_sem)
    basis_copy = pltpu.make_async_copy(basis_ref, basis, basis_sem)
    basis_copy.start()
    for copy in copies:
        copy.wait()
    for tile in range(tiles):
        rows = column[entry_ref[1, tile], :block, :]
        rows_ref[tile] = normalised(mask_ref[tile].astype(F32).astype(BF16), rows, 1)
    over = (((0,), (0,)), ((), ()))
    for tile in range(tiles):
        target = row[entry_ref[2, tile], block:, :]
        source = column[entry_ref[1, tile], block:, :]
        moments[tile] = lax.dot_general(rows_ref[tile], target, over, preferred_element_type=F32).astype(BF16)
        moments[tiles + tile] = lax.dot_general(
            inverse_ref[tile], source, over, preferred_element_type=F32
        ).astype(BF16)
    basis_copy.wait()
    tall, wide = bases * DIAGONAL, sides * DIAGONAL
    for start in range(0, depth, DIAGONAL):
        left = basis[:, start : start + DIAGONAL, :].reshape(tall, width)
        right = moments[:, start : start + DIAGONAL, :].reshape(wide, width)
        product = lax.dot_general(left, right, (((1,), (1,)), ((), ())), preferred_element_type=F32)
        if start == 0:
            total[...] = product
        else:
            total[...] += product
    same = iota((tall, wide), 0) % DIAGONAL == iota((tall, wide), 1) % DIAGONAL
    rows = (iota((bases, tall), 1) // DIAGONAL == iota((bases, tall), 0)).astype(BF16)
    columns = (iota((wide, sides), 0) // DIAGONAL == iota((wide, sides), 1)).astype(BF16)
    tower = jnp.zeros((bases, wide), F32)
    for part in split(jnp.where(same, total[...], 0.0)):
        tower += jnp.dot(rows, part, preferred_element_type=F32)
    per_tile = jnp.zeros((bases, sides), F32)
    for part in split(tower):
        per_tile += jnp.dot(part, columns, preferred_element_type=F32)
    live = live_ref[0, 0]
    per_tile = jnp.where(iota((bases, sides), 1) % tiles < live, per_tile, 0.0)
    first = core_ref[0] == 0
    forward, inverse = per_tile[:, :tiles], per_tile[:, tiles:]
    names = iota((PAYLOAD - bases, tiles), 0)
    lane = iota((PAYLOAD - bases, tiles), 1)
    for ref, chosen in ((mine_ref, first), (other_ref, jnp.logical_not(first))):
        ref[:bases, :] = jnp.where(chosen, forward, inverse).astype(BF16)
        named = jnp.zeros((PAYLOAD - bases, tiles), jnp.int32)
        for tile in range(tiles):
            name = entry_ref[0, tile] + jnp.where(chosen, 0, entry_ref[3, tile])
            digits = jnp.where(names == 0, name // LANES, jnp.where(names == 1, name % LANES, 0))
            named = jnp.where(lane == tile, digits, named)
        ref[bases:, :] = named.astype(F32).astype(BF16)


def gradients(entries, live, core, mask, row_pieces, inverse_rows, basis, columns):
    tiles, block, _ = mask.shape
    bases, depth, width = basis.shape
    payload = jax.ShapeDtypeStruct((PAYLOAD, tiles), BF16)

    def room(pieces):
        return pltpu.VMEM((sum(piece.shape[0] for piece in pieces), 2 * block, width), BF16)

    return pl.pallas_call(
        functools.partial(gradient_kernel, len(columns), len(row_pieces)),
        out_shape=(jax.ShapeDtypeStruct((tiles, block, width), BF16), payload, payload),
        in_specs=[SMEM, SMEM, SMEM, VMEM, VMEM, HBM] + [ANY] * (len(columns) + len(row_pieces)),
        out_specs=(VMEM, VMEM, VMEM),
        scratch_shapes=[
            room(columns),
            room(row_pieces),
            pltpu.VMEM(basis.shape, BF16),
            pltpu.VMEM((2 * tiles, depth, width), BF16),
            pltpu.VMEM((bases * DIAGONAL, 2 * tiles * DIAGONAL), F32),
            pltpu.SemaphoreType.DMA((len(columns),)),
            pltpu.SemaphoreType.DMA((len(row_pieces),)),
            pltpu.SemaphoreType.DMA,
        ],
        compiler_params=params(50),
        cost_estimate=cost(4 * 10**9, 12 * 10**6),
        name="gradients",
    )(entries, live, core, mask, inverse_rows, basis, *columns, *row_pieces)


def place_kernel(entry_ref, out_ref, total):
    bases, window = out_ref.shape
    count, _, span = entry_ref.shape
    for index in range(count):
        values = entry_ref[index, :bases, :].astype(F32)
        names = entry_ref[index, bases:, :].astype(F32)
        high, low = names[:1], names[1:2]
        chosen = (iota((LANES, span), 0).astype(F32) == low).astype(F32).astype(BF16)
        spread = [jnp.where(high == part, values, 0.0).astype(BF16) for part in range(window // LANES)]
        product = lax.dot_general(
            jnp.concatenate(spread, axis=0), chosen, (((1,), (1,)), ((), ())), preferred_element_type=F32
        )
        if index == 0:
            total[...] = product
        else:
            total[...] += product
    for part in range(window // LANES):
        out_ref[:, part * LANES : part * LANES + LANES] = total[part * bases : part * bases + bases, :]


def place_rows(entries, bases, window):
    return pl.pallas_call(
        place_kernel,
        out_shape=jax.ShapeDtypeStruct((bases, window), F32),
        in_specs=[VMEM],
        out_specs=VMEM,
        scratch_shapes=[pltpu.VMEM((window // LANES * bases, LANES), F32)],
        compiler_params=params(16),
        cost_estimate=cost(10**9, 10**6),
        name="place_rows",
    )(entries)


def join_kernel(plan, count, *refs):
    sems = refs[-1]
    copies = []
    for output, pieces in enumerate(plan):
        at = 0
        for source, start, size in pieces:
            copies.append(
                pltpu.make_async_copy(
                    refs[source].at[pl.ds(start, size)],
                    refs[count + output].at[pl.ds(at, size)],
                    sems.at[len(copies)],
                )
            )
            at += size
    for copy in copies:
        copy.start()
    for copy in copies:
        copy.wait()


def join(sources, plan):
    shape = sources[0].shape[1:]
    sizes = [sum(size for _, _, size in pieces) for pieces in plan]
    return pl.pallas_call(
        functools.partial(join_kernel, plan, len(sources)),
        out_shape=tuple(jax.ShapeDtypeStruct((size,) + shape, sources[0].dtype) for size in sizes),
        in_specs=[ANY] * len(sources),
        out_specs=tuple(ANY for _ in plan),
        scratch_shapes=[pltpu.SemaphoreType.DMA((sum(len(pieces) for pieces in plan),))],
        compiler_params=params(4),
        cost_estimate=cost(0, 10**6),
        name="join",
    )(*sources)


def finish_kernel(base, core_ref, own_ref, partner_ref, out_ref):
    window = own_ref.shape[1]
    shared = window - base
    last = out_ref.shape[1]
    first = core_ref[0] == 0
    out_ref[:, :base] = jnp.where(first, own_ref[:, :base], partner_ref[:, :base])
    out_ref[:, base:window] = jnp.where(first, own_ref[:, base:], partner_ref[:, base:]) + jnp.where(
        first, partner_ref[:, :shared], own_ref[:, :shared]
    )
    out_ref[:, window:] = jnp.where(
        first, partner_ref[:, shared : last - base], own_ref[:, shared : last - base]
    )


def finish(core, own, partner, base, relations):
    return pl.pallas_call(
        functools.partial(finish_kernel, base),
        out_shape=jax.ShapeDtypeStruct((own.shape[0], 2 * relations), F32),
        in_specs=[SMEM, VMEM, VMEM],
        out_specs=VMEM,
        compiler_params=params(8),
        cost_estimate=cost(0, 10**6),
        name="finish",
    )(core, own, partner)


def pack_kernel(feature_ref, cotangent_ref, own_ref, copies_ref, sems):
    block = feature_ref.shape[0]
    copies = []
    slots = [own_ref.at[0]] + [copies_ref.at[index] for index in range(copies_ref.shape[0])]
    for slot in slots:
        for start, ref in ((0, feature_ref), (block, cotangent_ref)):
            target = slot.at[pl.ds(start, block), :]
            copies.append(pltpu.make_async_copy(ref, target, sems.at[len(copies)]))
    for copy in copies:
        copy.start()
    for copy in copies:
        copy.wait()


def pack(features, cotangent, count):
    block, width = features.shape
    return pl.pallas_call(
        pack_kernel,
        out_shape=tuple(jax.ShapeDtypeStruct((blocks, 2 * block, width), BF16) for blocks in (1, count)),
        in_specs=[ANY, ANY],
        out_specs=(ANY, ANY),
        scratch_shapes=[pltpu.SemaphoreType.DMA((2 * count + 2,))],
        compiler_params=params(56),
        cost_estimate=cost(0, 10**6),
        name="pack",
    )(features, cotangent)


X_HI, RING, CORES = 2, 8, 2
Y, X_LO = 4, 2


def from_row(array, dx=0, dz=0, dk=0):
    pairs = []
    for x in range(X_HI):
        for z in range(RING):
            for k in range(CORES):
                source = ((x ^ dx) * RING + (z + dz) % RING) * CORES + (k ^ dk)
                pairs.append((source, (x * RING + z) * CORES + k))
    return lax.ppermute(array, "prow", pairs)


def from_column(array, dy=0, dx=0):
    pairs = []
    for y in range(Y):
        for x in range(X_LO):
            pairs.append((((y + dy) % Y) * X_LO + (x ^ dx), y * X_LO + x))
    return lax.ppermute(array, "pcol", pairs)


def tie(*arrays):
    return lax.optimization_barrier(arrays)


def coordinates():
    row = lax.axis_index("prow")
    column = lax.axis_index("pcol")
    return row // (RING * CORES), (row // CORES) % RING, row % CORES, column // X_LO, column % X_LO


def column_position(source, z, k):
    x, z_at, core = source // (RING * CORES), (source // CORES) % RING, source % CORES
    return ((core ^ k) * 2 + ((z_at ^ z) & 1)) * 8 + x * (RING // 2) + z_at // 2


def ordered(first, own, other, dim):
    return jnp.concatenate([jnp.where(first, own, other), jnp.where(first, other, own)], axis=dim)


def row_groups(apart):
    return [
        [(x * RING + z) * CORES + k for x in range(X_HI) for z in range(first, RING, apart)]
        for first in range(apart)
        for k in range(CORES)
    ]


def reduce_gradients(mine, arrived, held, place, relations, bases):
    _, _, k, y, x_lo = place
    entries = ordered(k == 0, mine, arrived, 1)
    entries = ordered(x_lo == 0, entries, from_column(entries, dx=1), 1)
    around = [entries] + [from_column(entries, dy=dy) for dy in range(1, Y)]
    entries = jnp.concatenate(
        [functools.reduce(lambda a, dy: jnp.where(y == (at - dy) % Y, around[dy], a), range(1, Y), around[0]) for at in range(Y)],
        axis=1,
    )
    copies = jnp.broadcast_to(entries[None], (X_HI * RING,) + entries.shape)
    copies, *held = tie(copies, *held)
    gathered = lax.all_to_all(copies, "prow", 0, 0, tiled=True, axis_index_groups=row_groups(1))
    base = relations // LANES * LANES
    window = -(-(2 * relations - base) // LANES) * LANES
    own = place_rows(gathered, bases, window)
    return finish(k.reshape(1), own, from_row(own, dk=1), base, relations).T, held


def on_device(features, cotangent, self_weight, basis_weights, coefficients, tile_list, tile_mask, live_tiles):
    block, width = features.shape
    relations = coefficients.shape[0] // 2
    bases = coefficients.shape[1]
    rows_count = X_HI * RING * CORES
    place = coordinates()
    _, z, k, y, x_lo = place
    mask = tile_mask[0, 0]
    relation, source, target = tile_list[0, 0, :, 0], tile_list[0, 0, :, 1], tile_list[0, 0, :, 2]
    apart = ((source % CORES) ^ k) * (X_HI * RING) + source // CORES
    target = (target // X_LO - y) % Y * X_LO + (target % X_LO ^ x_lo)
    entries = jnp.stack(
        [relation, column_position(source, z, k), target, jnp.full_like(relation, relations % LANES), apart]
    )
    rows_named = jnp.concatenate([relation, relation + relations])[None]

    own, copies = pack(features, cotangent, X_HI * RING // 2)
    alike = lax.all_to_all(copies, "prow", 0, 0, tiled=True, axis_index_groups=row_groups(2))
    (pair,) = join([own, from_column(own, dx=1)], (((0, 0, 1), (1, 0, 1)),))
    row_pieces = [pair] + [from_column(pair, dy=dy) for dy in range(1, Y)]
    weights = relation_weights(rows_named, coefficients.T, basis_weights)
    inverse_rows, keep, send = inverse_messages(entries, live_tiles, mask, row_pieces, weights, rows_count)
    alike, inverse_rows, keep, send = tie(alike, inverse_rows, keep, send)
    half = alike.shape[0] // 2
    low, high = join([alike], (((0, 0, half),), ((0, half, half),)))
    near = (alike, from_row(low, dz=1), from_row(high, dz=7))
    columns = near + tuple(from_row(piece, dk=1) for piece in near)
    inverse_part = (keep + from_row(send, dk=1).astype(F32)).astype(BF16).reshape(X_HI * RING, block, width)
    *columns, inverse_part = tie(*columns, inverse_part)
    inverse_parts = lax.all_to_all(inverse_part, "prow", 0, 0, tiled=True, axis_index_groups=row_groups(1))
    forward_rows, mine, other = gradients(
        entries, live_tiles, k.reshape(1), mask, row_pieces, inverse_rows, basis_weights, columns
    )
    arrived, forward_rows = tie(from_row(other, dk=1), forward_rows)
    coefficient_grads, (forward_rows, inverse_parts) = reduce_gradients(
        mine, arrived, (forward_rows, inverse_parts), place, relations, bases
    )
    forward_pair, *sends = forward_messages(entries, live_tiles, forward_rows, weights)
    for dy, part in enumerate(sends, 1):
        forward_pair += from_column(part, dy=Y - dy).astype(F32)
    forward_sum = forward_pair[0] + from_column(forward_pair[1].astype(BF16), dx=1).astype(F32)
    layer_sum = jnp.dot(features, self_weight, preferred_element_type=F32)
    layer_sum += jnp.sum(inverse_parts.astype(F32), axis=0) + forward_sum
    return layer_sum.astype(BF16), coefficient_grads


def solution(mesh):
    return jax.shard_map(
        on_device,
        mesh=mesh,
        in_specs=(
            P(("prow", "pcol"), None),
            P(("prow", "pcol"), None),
            P(),
            P(),
            P(),
            P("prow", "pcol", None, None),
            P("prow", "pcol", None, None, None),
            P("prow", "pcol"),
        ),
        out_specs=(P(("prow", "pcol"), None), P()),
        check_vma=False,
    )
```

```python
import functools
import jax
import jax.numpy as jnp
from jax import lax
from jax.experimental import pallas as pl
from jax.experimental.pallas import tpu as pltpu
from jax.sharding import PartitionSpec as P

F32, BF16 = jnp.float32, jnp.bfloat16
VMEM = pl.BlockSpec(memory_space=pltpu.VMEM)
SMEM = pl.BlockSpec(memory_space=pltpu.SMEM)
ANY = pl.BlockSpec(memory_space=pl.ANY)
HBM = pl.BlockSpec(memory_space=pltpu.HBM)
LANES = 128
DIAGONAL = 16
PAYLOAD = 48


def params(mib):
    return pltpu.CompilerParams(vmem_limit_bytes=mib * 1024 * 1024)


def cost(flops, moved):
    return pl.CostEstimate(flops=flops, bytes_accessed=moved, transcendentals=0)


def split(wide):
    high = wide.astype(BF16)
    return high, (wide - high.astype(F32)).astype(BF16)


def iota(shape, dim):
    return lax.broadcasted_iota(jnp.int32, shape, dim)


def weights_kernel(parts, row_ref, coefficient_ref, basis_ref, weight_ref, spread, basis, weight, in_sems, out_sems):
    bases, named = coefficient_ref.shape
    sides = row_ref.shape[1]
    depth, width = basis.shape[1:]
    size = depth // parts
    tall, wide = sides * DIAGONAL, bases * DIAGONAL
    arrive, leave = [], []
    for part in range(parts):
        rows = pl.ds(part * size, size)
        arrive.append(pltpu.make_async_copy(basis_ref.at[:, rows, :], basis.at[:, rows, :], in_sems.at[part]))
        leave.append(pltpu.make_async_copy(weight.at[:, rows, :], weight_ref.at[:, rows, :], out_sems.at[part]))
    for copy in arrive:
        copy.start()
    chosen = (iota((named, sides), 0) == row_ref[...]).astype(F32).astype(BF16)
    rows = (iota((tall, sides), 0) // DIAGONAL == iota((tall, sides), 1)).astype(F32).astype(BF16)
    columns = (iota((bases, wide), 1) // DIAGONAL == iota((bases, wide), 0)).astype(F32).astype(BF16)
    same = iota((tall, wide), 0) % DIAGONAL == iota((tall, wide), 1) % DIAGONAL
    for index, part in enumerate(split(coefficient_ref[...])):
        picked = jnp.dot(part, chosen, preferred_element_type=F32).astype(BF16)
        tower = lax.dot_general(rows, picked, (((1,), (1,)), ((), ())), preferred_element_type=F32).astype(BF16)
        full = jnp.dot(tower, columns, preferred_element_type=F32)
        spread[index] = jnp.where(same, full, 0.0).astype(BF16)
    for start in range(0, depth, DIAGONAL):
        if start % size == 0:
            arrive[start // size].wait()
        part = basis[:, start : start + DIAGONAL, :].reshape(wide, width)
        total = jnp.dot(spread[0], part, preferred_element_type=F32)
        total += jnp.dot(spread[1], part, preferred_element_type=F32)
        weight[:, start : start + DIAGONAL, :] = total.astype(BF16).reshape(sides, DIAGONAL, width)
        if (start + DIAGONAL) % size == 0:
            leave[start // size].start()
    for copy in leave:
        copy.wait()


def relation_weights(rows_named, coefficients_t, basis, parts=4):
    bases, depth, width = basis.shape
    sides = rows_named.shape[1]
    return pl.pallas_call(
        functools.partial(weights_kernel, parts),
        out_shape=jax.ShapeDtypeStruct((sides, depth, width), BF16),
        in_specs=[VMEM, VMEM, HBM],
        out_specs=HBM,
        scratch_shapes=[
            pltpu.VMEM((2, sides * DIAGONAL, bases * DIAGONAL), BF16),
            pltpu.VMEM(basis.shape, BF16),
            pltpu.VMEM((sides, depth, width), BF16),
            pltpu.SemaphoreType.DMA((parts,)),
            pltpu.SemaphoreType.DMA((parts,)),
        ],
        compiler_params=params(56),
        cost_estimate=cost(4 * 10**9, 2 * basis.size * 2),
        name="relation_weights",
    )(rows_named, coefficients_t, basis)


def normalised(mask, rows, dim):
    over = (((dim,), (0,)), ((), ()))
    summed = lax.dot_general(mask, rows, over, preferred_element_type=F32)
    degree = lax.dot_general(mask, jnp.ones((mask.shape[dim], LANES), BF16), over, preferred_element_type=F32)
    scale = (1.0 / (1.0 + degree)).astype(BF16).astype(F32)
    return (summed * jnp.concatenate([scale] * (rows.shape[1] // LANES), axis=1)).astype(BF16)


def copies_into(target, refs, sems):
    copies, at = [], 0
    for index, ref in enumerate(refs):
        size = ref.shape[0]
        copies.append(pltpu.make_async_copy(ref, target.at[pl.ds(at, size)], sems.at[index]))
        at += size
    for copy in copies:
        copy.start()
    return copies


def block_at(index, size):
    return pl.ds(pl.multiple_of(index * size, size), size)


def inverse_kernel(pieces, entry_ref, live_ref, mask_ref, weights_ref, *refs):
    rows_ref, keep_ref, send_ref, total, row, weight, row_sems, sem = refs[pieces:]
    tiles, block, _ = mask_ref.shape
    arrive = copies_into(row, refs[:pieces], row_sems)
    copy = pltpu.make_async_copy(weights_ref.at[pl.ds(tiles, tiles)], weight, sem)
    copy.start()
    total[...] = jnp.zeros_like(total)
    for part in arrive:
        part.wait()
    for tile in range(tiles):
        rows = row[entry_ref[2, tile], :block, :]
        rows_ref[tile] = normalised(mask_ref[tile].astype(F32).astype(BF16), rows, 0)
    copy.wait()
    for tile in range(tiles):
        weighting = (tile < live_ref[0, 0]).astype(F32)
        message = jnp.dot(rows_ref[tile], weight[tile], preferred_element_type=F32) * weighting
        total[block_at(entry_ref[4, tile], block), :] += message
    half = keep_ref.shape[0]
    keep_ref[...] = total[:half, :]
    send_ref[...] = total[half:, :].astype(BF16)


def inverse_messages(entries, live, mask, row_pieces, weights, row_count):
    tiles, block, _ = mask.shape
    width = row_pieces[0].shape[2]
    half = row_count * block // 2
    columns = sum(piece.shape[0] for piece in row_pieces)
    return pl.pallas_call(
        functools.partial(inverse_kernel, len(row_pieces)),
        out_shape=(
            jax.ShapeDtypeStruct((tiles, block, width), BF16),
            jax.ShapeDtypeStruct((half, width), F32),
            jax.ShapeDtypeStruct((half, width), BF16),
        ),
        in_specs=[SMEM, SMEM, VMEM, HBM] + [ANY] * len(row_pieces),
        out_specs=(VMEM, VMEM, VMEM),
        scratch_shapes=[
            pltpu.VMEM((2 * half, width), F32),
            pltpu.VMEM((columns,) + row_pieces[0].shape[1:], BF16),
            pltpu.VMEM((tiles, width, width), BF16),
            pltpu.SemaphoreType.DMA((len(row_pieces),)),
            pltpu.SemaphoreType.DMA,
        ],
        compiler_params=params(52),
        cost_estimate=cost(10**9, 8 * 10**6),
        name="inverse_messages",
    )(entries, live, mask, weights, *row_pieces)


def forward_kernel(entry_ref, live_ref, rows_ref, weights_ref, keep_ref, *refs):
    send_refs, (total, weight, sem) = refs[:-3], refs[-3:]
    tiles, block, _ = rows_ref.shape
    copy = pltpu.make_async_copy(weights_ref.at[pl.ds(0, tiles)], weight, sem)
    copy.start()
    total[...] = jnp.zeros_like(total)
    copy.wait()
    for tile in range(tiles):
        weighting = (tile < live_ref[0, 0]).astype(F32)
        message = jnp.dot(rows_ref[tile], weight[tile], preferred_element_type=F32) * weighting
        total[entry_ref[5, tile]] += message
    pair = keep_ref.shape[0]
    keep_ref[...] = total[:pair]
    for index, ref in enumerate(send_refs):
        ref[...] = total[pair * (index + 1) : pair * (index + 2)].astype(BF16)


def forward_messages(entries, live, rows, weights):
    tiles, block, width = rows.shape
    shape = (X_LO, block, width)
    return pl.pallas_call(
        forward_kernel,
        out_shape=(jax.ShapeDtypeStruct(shape, F32),) + (jax.ShapeDtypeStruct(shape, BF16),) * (Y - 1),
        in_specs=[SMEM, SMEM, VMEM, HBM],
        out_specs=(VMEM,) * Y,
        scratch_shapes=[
            pltpu.VMEM((Y * X_LO, block, width), F32),
            pltpu.VMEM((tiles, width, width), BF16),
            pltpu.SemaphoreType.DMA,
        ],
        compiler_params=params(56),
        cost_estimate=cost(10**9, 4 * 10**6),
        name="forward_messages",
    )(entries, live, rows, weights)


def gradient_kernel(pieces, row_pieces, entry_ref, live_ref, core_ref, mask_ref, inverse_ref, basis_ref, *refs):
    column_refs, row_refs, refs = refs[:pieces], refs[pieces : pieces + row_pieces], refs[pieces + row_pieces :]
    rows_ref, mine_ref, other_ref, column, row, basis, moments, total, column_sem, row_sem, basis_sem = refs
    tiles, block, _ = mask_ref.shape
    bases, depth, width = basis.shape
    sides = 2 * tiles
    copies = copies_into(column, column_refs, column_sem) + copies_into(row, row_refs, row_sem)
    basis_copy = pltpu.make_async_copy(basis_ref, basis, basis_sem)
    basis_copy.start()
    for copy in copies:
        copy.wait()
    for tile in range(tiles):
        rows = column[entry_ref[1, tile], :block, :]
        rows_ref[tile] = normalised(mask_ref[tile].astype(F32).astype(BF16), rows, 1)
    over = (((0,), (0,)), ((), ()))
    for tile in range(tiles):
        target = row[entry_ref[2, tile], block:, :]
        source = column[entry_ref[1, tile], block:, :]
        moments[tile] = lax.dot_general(rows_ref[tile], target, over, preferred_element_type=F32).astype(BF16)
        moments[tiles + tile] = lax.dot_general(
            inverse_ref[tile], source, over, preferred_element_type=F32
        ).astype(BF16)
    basis_copy.wait()
    tall, wide = bases * DIAGONAL, sides * DIAGONAL
    for start in range(0, depth, DIAGONAL):
        left = basis[:, start : start + DIAGONAL, :].reshape(tall, width)
        right = moments[:, start : start + DIAGONAL, :].reshape(wide, width)
        product = lax.dot_general(left, right, (((1,), (1,)), ((), ())), preferred_element_type=F32)
        if start == 0:
            total[...] = product
        else:
            total[...] += product
    same = iota((tall, wide), 0) % DIAGONAL == iota((tall, wide), 1) % DIAGONAL
    rows = (iota((bases, tall), 1) // DIAGONAL == iota((bases, tall), 0)).astype(BF16)
    columns = (iota((wide, sides), 0) // DIAGONAL == iota((wide, sides), 1)).astype(BF16)
    tower = jnp.zeros((bases, wide), F32)
    for part in split(jnp.where(same, total[...], 0.0)):
        tower += jnp.dot(rows, part, preferred_element_type=F32)
    per_tile = jnp.zeros((bases, sides), F32)
    for part in split(tower):
        per_tile += jnp.dot(part, columns, preferred_element_type=F32)
    live = live_ref[0, 0]
    per_tile = jnp.where(iota((bases, sides), 1) % tiles < live, per_tile, 0.0)
    first = core_ref[0] == 0
    forward, inverse = per_tile[:, :tiles], per_tile[:, tiles:]
    names = iota((PAYLOAD - bases, tiles), 0)
    lane = iota((PAYLOAD - bases, tiles), 1)
    for ref, chosen in ((mine_ref, first), (other_ref, jnp.logical_not(first))):
        ref[:bases, :] = jnp.where(chosen, forward, inverse).astype(BF16)
        named = jnp.zeros((PAYLOAD - bases, tiles), jnp.int32)
        for tile in range(tiles):
            name = entry_ref[0, tile] + jnp.where(chosen, 0, entry_ref[3, tile])
            digits = jnp.where(names == 0, name // LANES, jnp.where(names == 1, name % LANES, 0))
            named = jnp.where(lane == tile, digits, named)
        ref[bases:, :] = named.astype(F32).astype(BF16)


def gradients(entries, live, core, mask, row_pieces, inverse_rows, basis, columns):
    tiles, block, _ = mask.shape
    bases, depth, width = basis.shape
    payload = jax.ShapeDtypeStruct((PAYLOAD, tiles), BF16)

    def room(pieces):
        return pltpu.VMEM((sum(piece.shape[0] for piece in pieces), 2 * block, width), BF16)

    return pl.pallas_call(
        functools.partial(gradient_kernel, len(columns), len(row_pieces)),
        out_shape=(jax.ShapeDtypeStruct((tiles, block, width), BF16), payload, payload),
        in_specs=[SMEM, SMEM, SMEM, VMEM, VMEM, HBM] + [ANY] * (len(columns) + len(row_pieces)),
        out_specs=(VMEM, VMEM, VMEM),
        scratch_shapes=[
            room(columns),
            room(row_pieces),
            pltpu.VMEM(basis.shape, BF16),
            pltpu.VMEM((2 * tiles, depth, width), BF16),
            pltpu.VMEM((bases * DIAGONAL, 2 * tiles * DIAGONAL), F32),
            pltpu.SemaphoreType.DMA((len(columns),)),
            pltpu.SemaphoreType.DMA((len(row_pieces),)),
            pltpu.SemaphoreType.DMA,
        ],
        compiler_params=params(50),
        cost_estimate=cost(4 * 10**9, 12 * 10**6),
        name="gradients",
    )(entries, live, core, mask, inverse_rows, basis, *columns, *row_pieces)


def place_kernel(entry_ref, out_ref, total):
    bases, window = out_ref.shape
    count, _, span = entry_ref.shape
    for index in range(count):
        values = entry_ref[index, :bases, :].astype(F32)
        names = entry_ref[index, bases:, :].astype(F32)
        high, low = names[:1], names[1:2]
        chosen = (iota((LANES, span), 0).astype(F32) == low).astype(F32).astype(BF16)
        spread = [jnp.where(high == part, values, 0.0).astype(BF16) for part in range(window // LANES)]
        product = lax.dot_general(
            jnp.concatenate(spread, axis=0), chosen, (((1,), (1,)), ((), ())), preferred_element_type=F32
        )
        if index == 0:
            total[...] = product
        else:
            total[...] += product
    for part in range(window // LANES):
        out_ref[:, part * LANES : part * LANES + LANES] = total[part * bases : part * bases + bases, :]


def place_rows(entries, bases, window):
    return pl.pallas_call(
        place_kernel,
        out_shape=jax.ShapeDtypeStruct((bases, window), F32),
        in_specs=[VMEM],
        out_specs=VMEM,
        scratch_shapes=[pltpu.VMEM((window // LANES * bases, LANES), F32)],
        compiler_params=params(16),
        cost_estimate=cost(10**9, 10**6),
        name="place_rows",
    )(entries)


def join_kernel(plan, count, *refs):
    sems = refs[-1]
    copies = []
    for output, pieces in enumerate(plan):
        at = 0
        for source, start, size in pieces:
            copies.append(
                pltpu.make_async_copy(
                    refs[source].at[pl.ds(start, size)],
                    refs[count + output].at[pl.ds(at, size)],
                    sems.at[len(copies)],
                )
            )
            at += size
    for copy in copies:
        copy.start()
    for copy in copies:
        copy.wait()


def join(sources, plan):
    shape = sources[0].shape[1:]
    sizes = [sum(size for _, _, size in pieces) for pieces in plan]
    return pl.pallas_call(
        functools.partial(join_kernel, plan, len(sources)),
        out_shape=tuple(jax.ShapeDtypeStruct((size,) + shape, sources[0].dtype) for size in sizes),
        in_specs=[ANY] * len(sources),
        out_specs=tuple(ANY for _ in plan),
        scratch_shapes=[pltpu.SemaphoreType.DMA((sum(len(pieces) for pieces in plan),))],
        compiler_params=params(4),
        cost_estimate=cost(0, 10**6),
        name="join",
    )(*sources)


def finish_kernel(base, core_ref, own_ref, partner_ref, out_ref):
    window = own_ref.shape[1]
    shared = window - base
    last = out_ref.shape[1]
    first = core_ref[0] == 0
    out_ref[:, :base] = jnp.where(first, own_ref[:, :base], partner_ref[:, :base])
    out_ref[:, base:window] = jnp.where(first, own_ref[:, base:], partner_ref[:, base:]) + jnp.where(
        first, partner_ref[:, :shared], own_ref[:, :shared]
    )
    out_ref[:, window:] = jnp.where(
        first, partner_ref[:, shared : last - base], own_ref[:, shared : last - base]
    )


def finish(core, own, partner, base, relations):
    return pl.pallas_call(
        functools.partial(finish_kernel, base),
        out_shape=jax.ShapeDtypeStruct((own.shape[0], 2 * relations), F32),
        in_specs=[SMEM, VMEM, VMEM],
        out_specs=VMEM,
        compiler_params=params(8),
        cost_estimate=cost(0, 10**6),
        name="finish",
    )(core, own, partner)


def pack_kernel(feature_ref, cotangent_ref, own_ref, copies_ref, sems):
    block = feature_ref.shape[0]
    copies = [
        pltpu.make_async_copy(ref, own_ref.at[0, pl.ds(index * block, block), :], sems.at[index])
        for index, ref in enumerate((feature_ref, cotangent_ref))
    ]
    for copy in copies:
        copy.start()
    for copy in copies:
        copy.wait()
    for index in range(copies_ref.shape[0]):
        copies_ref[index] = own_ref[0]


def pack(features, cotangent, count):
    block, width = features.shape
    return pl.pallas_call(
        pack_kernel,
        out_shape=tuple(jax.ShapeDtypeStruct((blocks, 2 * block, width), BF16) for blocks in (1, count)),
        in_specs=[HBM, HBM],
        out_specs=(VMEM, VMEM),
        scratch_shapes=[pltpu.SemaphoreType.DMA((2,))],
        compiler_params=params(60),
        cost_estimate=cost(0, 10**6),
        name="pack",
    )(features, cotangent)


X_HI, RING, CORES = 2, 8, 2
Y, X_LO = 4, 2


def from_row(array, dx=0, dz=0, dk=0):
    pairs = []
    for x in range(X_HI):
        for z in range(RING):
            for k in range(CORES):
                source = ((x ^ dx) * RING + (z + dz) % RING) * CORES + (k ^ dk)
                pairs.append((source, (x * RING + z) * CORES + k))
    return lax.ppermute(array, "prow", pairs)


def from_column(array, dy=0, dx=0):
    pairs = []
    for y in range(Y):
        for x in range(X_LO):
            pairs.append((((y + dy) % Y) * X_LO + (x ^ dx), y * X_LO + x))
    return lax.ppermute(array, "pcol", pairs)


def tie(*arrays):
    return lax.optimization_barrier(arrays)


def coordinates():
    row = lax.axis_index("prow")
    column = lax.axis_index("pcol")
    return row // (RING * CORES), (row // CORES) % RING, row % CORES, column // X_LO, column % X_LO


def column_position(source, x, z, k):
    dx = (source // (RING * CORES)) ^ x
    dz = ((source // CORES) % RING - z) % RING
    dk = (source % CORES) ^ k
    even = dx * 4 + ((dz + 2) % RING) // 2
    odd = 8 + 4 * (dz // 4) + 2 * dx + (dz % 4) // 2
    return dk * 16 + jnp.where(dz % 2 == 0, even, odd)


def ordered(first, own, other, dim):
    return jnp.concatenate([jnp.where(first, own, other), jnp.where(first, other, own)], axis=dim)


def row_groups(apart):
    return [
        [(x * RING + z) * CORES + k for x in range(X_HI) for z in range(first, RING, apart)]
        for first in range(apart)
        for k in range(CORES)
    ]


def gather_gradients(mine, arrived, held, place):
    _, _, k, y, x_lo = place
    entries = ordered(k == 0, mine, arrived, 1)
    entries = ordered(x_lo == 0, entries, from_column(entries, dx=1), 1)
    around = [entries] + [from_column(entries, dy=dy) for dy in range(1, Y)]
    entries = jnp.concatenate(
        [functools.reduce(lambda a, dy: jnp.where(y == (at - dy) % Y, around[dy], a), range(1, Y), around[0]) for at in range(Y)],
        axis=1,
    )
    copies = jnp.broadcast_to(entries[None], (X_HI * RING,) + entries.shape)
    copies, *held = tie(copies, *held)
    gathered = lax.all_to_all(copies, "prow", 0, 0, tiled=True, axis_index_groups=row_groups(1))
    return gathered, held


def on_device(features, cotangent, self_weight, basis_weights, coefficients, tile_list, tile_mask, live_tiles):
    block, width = features.shape
    relations = coefficients.shape[0] // 2
    bases = coefficients.shape[1]
    rows_count = X_HI * RING * CORES
    place = coordinates()
    x, z, k, y, x_lo = place
    mask = tile_mask[0, 0]
    relation, source, target = tile_list[0, 0, :, 0], tile_list[0, 0, :, 1], tile_list[0, 0, :, 2]
    apart = ((source % CORES) ^ k) * (X_HI * RING) + source // CORES
    near = (target // X_LO - y) % Y * X_LO + (target % X_LO ^ x_lo)
    shift = jnp.full_like(relation, relations % LANES)
    entries = jnp.stack([relation, column_position(source, x, z, k), target, shift, apart, near])
    rows_named = jnp.concatenate([relation, relation + relations])[None]

    own, copies = pack(features, cotangent, Y * X_LO)
    ring = [from_row(own, dz=dz) for dz in (4, 2, 6)]
    row_blocks = lax.all_to_all(copies, "pcol", 0, 0, tiled=True)
    (even,) = join([ring[2], own, ring[1], ring[0]], (((0, 0, 1), (1, 0, 1), (2, 0, 1), (3, 0, 1)),))
    across = from_row(even, dx=1)
    even, rows_named = tie(even, rows_named)
    weights = relation_weights(rows_named, coefficients.T, basis_weights)
    row_pieces = [row_blocks]
    inverse_rows, keep, send = inverse_messages(entries, live_tiles, mask, row_pieces, weights, rows_count)
    across, inverse_rows, keep, send = tie(across, inverse_rows, keep, send)
    upward, downward = join([even, across], (((0, 1, 2), (1, 1, 2)), ((0, 0, 2), (1, 0, 2))))
    near = (even, across, from_row(upward, dz=1), from_row(downward, dz=7))
    columns = near + tuple(from_row(piece, dk=1) for piece in near)
    inverse_part = (keep + from_row(send, dk=1).astype(F32)).astype(BF16).reshape(X_HI * RING, block, width)
    *columns, inverse_part = tie(*columns, inverse_part)
    inverse_parts = lax.all_to_all(inverse_part, "prow", 0, 0, tiled=True, axis_index_groups=row_groups(1))
    forward_rows, mine, other = gradients(
        entries, live_tiles, k.reshape(1), mask, row_pieces, inverse_rows, basis_weights, columns
    )
    arrived, forward_rows = tie(from_row(other, dk=1), forward_rows)
    gathered, (forward_rows, inverse_parts) = gather_gradients(mine, arrived, (forward_rows, inverse_parts), place)
    forward_pair, *sends = forward_messages(entries, live_tiles, forward_rows, weights)
    sends = [from_column(part, dy=Y - dy) for dy, part in enumerate(sends, 1)]
    base = relations // LANES * LANES
    window = -(-(2 * relations - base) // LANES) * LANES
    placed = place_rows(gathered, bases, window)
    coefficient_grads = finish(k.reshape(1), placed, from_row(placed, dk=1), base, relations).T
    _, *sends = tie(placed, *sends)
    for part in sends:
        forward_pair += part.astype(F32)
    forward_sum = forward_pair[0] + from_column(forward_pair[1].astype(BF16), dx=1).astype(F32)
    layer_sum = jnp.dot(features, self_weight, preferred_element_type=F32)
    layer_sum += jnp.sum(inverse_parts.astype(F32), axis=0) + forward_sum
    return layer_sum.astype(BF16), coefficient_grads


def solution(mesh):
    return jax.shard_map(
        on_device,
        mesh=mesh,
        in_specs=(
            P(("prow", "pcol"), None),
            P(("prow", "pcol"), None),
            P(),
            P(),
            P(),
            P("prow", "pcol", None, None),
            P("prow", "pcol", None, None, None),
            P("prow", "pcol"),
        ),
        out_specs=(P(("prow", "pcol"), None), P()),
        check_vma=False,
    )
```

```python
import functools
import jax
import jax.numpy as jnp
from jax import lax
from jax.experimental import pallas as pl
from jax.experimental.pallas import tpu as pltpu
from jax.sharding import PartitionSpec as P

F32, BF16 = jnp.float32, jnp.bfloat16
VMEM = pl.BlockSpec(memory_space=pltpu.VMEM)
SMEM = pl.BlockSpec(memory_space=pltpu.SMEM)
ANY = pl.BlockSpec(memory_space=pl.ANY)
HBM = pl.BlockSpec(memory_space=pltpu.HBM)
LANES = 128
DIAGONAL = 16
PAYLOAD = 48


def params(mib):
    return pltpu.CompilerParams(vmem_limit_bytes=mib * 1024 * 1024)


def cost(flops, moved):
    return pl.CostEstimate(flops=flops, bytes_accessed=moved, transcendentals=0)


def split(wide):
    high = wide.astype(BF16)
    return high, (wide - high.astype(F32)).astype(BF16)


def iota(shape, dim):
    return lax.broadcasted_iota(jnp.int32, shape, dim)


def weights_kernel(parts, row_ref, coefficient_ref, basis_ref, weight_ref, spread, basis, weight, in_sems, out_sems):
    bases, named = coefficient_ref.shape
    sides = row_ref.shape[1]
    depth, width = basis.shape[1:]
    size = depth // parts
    tall, wide = sides * DIAGONAL, bases * DIAGONAL
    arrive, leave = [], []
    for part in range(parts):
        rows = pl.ds(part * size, size)
        arrive.append(pltpu.make_async_copy(basis_ref.at[:, rows, :], basis.at[:, rows, :], in_sems.at[part]))
        leave.append(pltpu.make_async_copy(weight.at[:, rows, :], weight_ref.at[:, rows, :], out_sems.at[part]))
    for copy in arrive:
        copy.start()
    chosen = (iota((named, sides), 0) == row_ref[...]).astype(F32).astype(BF16)
    rows = (iota((tall, sides), 0) // DIAGONAL == iota((tall, sides), 1)).astype(F32).astype(BF16)
    columns = (iota((bases, wide), 1) // DIAGONAL == iota((bases, wide), 0)).astype(F32).astype(BF16)
    same = iota((tall, wide), 0) % DIAGONAL == iota((tall, wide), 1) % DIAGONAL
    for index, part in enumerate(split(coefficient_ref[...])):
        picked = jnp.dot(part, chosen, preferred_element_type=F32).astype(BF16)
        tower = lax.dot_general(rows, picked, (((1,), (1,)), ((), ())), preferred_element_type=F32).astype(BF16)
        full = jnp.dot(tower, columns, preferred_element_type=F32)
        spread[index] = jnp.where(same, full, 0.0).astype(BF16)
    for start in range(0, depth, DIAGONAL):
        if start % size == 0:
            arrive[start // size].wait()
        part = basis[:, start : start + DIAGONAL, :].reshape(wide, width)
        total = jnp.dot(spread[0], part, preferred_element_type=F32)
        total += jnp.dot(spread[1], part, preferred_element_type=F32)
        weight[:, start : start + DIAGONAL, :] = total.astype(BF16).reshape(sides, DIAGONAL, width)
        if (start + DIAGONAL) % size == 0:
            leave[start // size].start()
    for copy in leave:
        copy.wait()


def relation_weights(rows_named, coefficients_t, basis, parts=4):
    bases, depth, width = basis.shape
    sides = rows_named.shape[1]
    return pl.pallas_call(
        functools.partial(weights_kernel, parts),
        out_shape=jax.ShapeDtypeStruct((sides, depth, width), BF16),
        in_specs=[VMEM, VMEM, HBM],
        out_specs=HBM,
        scratch_shapes=[
            pltpu.VMEM((2, sides * DIAGONAL, bases * DIAGONAL), BF16),
            pltpu.VMEM(basis.shape, BF16),
            pltpu.VMEM((sides, depth, width), BF16),
            pltpu.SemaphoreType.DMA((parts,)),
            pltpu.SemaphoreType.DMA((parts,)),
        ],
        compiler_params=params(56),
        cost_estimate=cost(4 * 10**9, 2 * basis.size * 2),
        name="relation_weights",
    )(rows_named, coefficients_t, basis)


def normalised(mask, rows, dim):
    over = (((dim,), (0,)), ((), ()))
    summed = lax.dot_general(mask, rows, over, preferred_element_type=F32)
    degree = lax.dot_general(mask, jnp.ones((mask.shape[dim], LANES), BF16), over, preferred_element_type=F32)
    scale = (1.0 / (1.0 + degree)).astype(BF16).astype(F32)
    return (summed * jnp.concatenate([scale] * (rows.shape[1] // LANES), axis=1)).astype(BF16)


def copies_into(target, refs, sems):
    copies, at = [], 0
    for index, ref in enumerate(refs):
        size = ref.shape[0]
        copies.append(pltpu.make_async_copy(ref, target.at[pl.ds(at, size)], sems.at[index]))
        at += size
    for copy in copies:
        copy.start()
    return copies


def block_at(index, size):
    return pl.ds(pl.multiple_of(index * size, size), size)


def inverse_kernel(pieces, entry_ref, live_ref, mask_ref, weights_ref, *refs):
    rows_ref, near_ref, far_ref, *send_refs, total, row, weight, row_sems, sem = refs[pieces:]
    tiles, block, _ = mask_ref.shape
    arrive = copies_into(row, refs[:pieces], row_sems)
    copy = pltpu.make_async_copy(weights_ref.at[pl.ds(tiles, tiles)], weight, sem)
    copy.start()
    total[...] = jnp.zeros_like(total)
    for part in arrive:
        part.wait()
    for tile in range(tiles):
        rows = row[entry_ref[2, tile], :block, :]
        rows_ref[tile] = normalised(mask_ref[tile].astype(F32).astype(BF16), rows, 0)
    copy.wait()
    for tile in range(tiles):
        weighting = (tile < live_ref[0, 0]).astype(F32)
        message = jnp.dot(rows_ref[tile], weight[tile], preferred_element_type=F32) * weighting
        total[block_at(entry_ref[4, tile], block), :] += message
    half = near_ref.shape[0]
    near_ref[...] = total[:half, :]
    far_ref[...] = total[half : 2 * half, :]
    quarter = half // 2
    for index, ref in enumerate(send_refs):
        start = 2 * half + index * quarter
        ref[...] = total[start : start + quarter, :].astype(BF16)


def inverse_messages(entries, live, mask, row_pieces, weights, row_count):
    tiles, block, _ = mask.shape
    width = row_pieces[0].shape[2]
    half = row_count * block // 2
    columns = sum(piece.shape[0] for piece in row_pieces)
    return pl.pallas_call(
        functools.partial(inverse_kernel, len(row_pieces)),
        out_shape=(
            jax.ShapeDtypeStruct((tiles, block, width), BF16),
            jax.ShapeDtypeStruct((half // 2, width), F32),
            jax.ShapeDtypeStruct((half // 2, width), F32),
        )
        + (jax.ShapeDtypeStruct((half // 4, width), BF16),) * 4,
        in_specs=[SMEM, SMEM, VMEM, HBM] + [ANY] * len(row_pieces),
        out_specs=(VMEM,) * 7,
        scratch_shapes=[
            pltpu.VMEM((2 * half, width), F32),
            pltpu.VMEM((columns,) + row_pieces[0].shape[1:], BF16),
            pltpu.VMEM((tiles, width, width), BF16),
            pltpu.SemaphoreType.DMA((len(row_pieces),)),
            pltpu.SemaphoreType.DMA,
        ],
        compiler_params=params(52),
        cost_estimate=cost(0, 1000),
        name="inverse_messages",
    )(entries, live, mask, weights, *row_pieces)


def forward_kernel(entry_ref, live_ref, rows_ref, weights_ref, keep_ref, *refs):
    send_refs, (total, weight, sem) = refs[:-3], refs[-3:]
    tiles, block, _ = rows_ref.shape
    copy = pltpu.make_async_copy(weights_ref.at[pl.ds(0, tiles)], weight, sem)
    copy.start()
    total[...] = jnp.zeros_like(total)
    copy.wait()
    for tile in range(tiles):
        weighting = (tile < live_ref[0, 0]).astype(F32)
        message = jnp.dot(rows_ref[tile], weight[tile], preferred_element_type=F32) * weighting
        total[entry_ref[5, tile]] += message
    pair = keep_ref.shape[0]
    keep_ref[...] = total[:pair]
    for index, ref in enumerate(send_refs):
        ref[...] = total[pair * (index + 1) : pair * (index + 2)].astype(BF16)


def forward_messages(entries, live, rows, weights):
    tiles, block, width = rows.shape
    shape = (X_LO, block, width)
    return pl.pallas_call(
        forward_kernel,
        out_shape=(jax.ShapeDtypeStruct(shape, F32),) + (jax.ShapeDtypeStruct(shape, BF16),) * (Y - 1),
        in_specs=[SMEM, SMEM, VMEM, HBM],
        out_specs=(VMEM,) * Y,
        scratch_shapes=[
            pltpu.VMEM((Y * X_LO, block, width), F32),
            pltpu.VMEM((tiles, width, width), BF16),
            pltpu.SemaphoreType.DMA,
        ],
        compiler_params=params(56),
        cost_estimate=cost(10**9, 4 * 10**6),
        name="forward_messages",
    )(entries, live, rows, weights)


def gradient_kernel(pieces, row_pieces, entry_ref, live_ref, core_ref, mask_ref, inverse_ref, basis_ref, *refs):
    column_refs, row_refs, refs = refs[:pieces], refs[pieces : pieces + row_pieces], refs[pieces + row_pieces :]
    rows_ref, mine_ref, other_ref, column, row, basis, moments, total, column_sem, row_sem, basis_sem = refs
    tiles, block, _ = mask_ref.shape
    bases, depth, width = basis.shape
    sides = 2 * tiles
    copies = copies_into(column, column_refs, column_sem) + copies_into(row, row_refs, row_sem)
    basis_copy = pltpu.make_async_copy(basis_ref, basis, basis_sem)
    basis_copy.start()
    for copy in copies:
        copy.wait()
    for tile in range(tiles):
        rows = column[entry_ref[1, tile], :block, :]
        rows_ref[tile] = normalised(mask_ref[tile].astype(F32).astype(BF16), rows, 1)
    over = (((0,), (0,)), ((), ()))
    for tile in range(tiles):
        target = row[entry_ref[2, tile], block:, :]
        source = column[entry_ref[1, tile], block:, :]
        moments[tile] = lax.dot_general(rows_ref[tile], target, over, preferred_element_type=F32).astype(BF16)
        moments[tiles + tile] = lax.dot_general(
            inverse_ref[tile], source, over, preferred_element_type=F32
        ).astype(BF16)
    basis_copy.wait()
    tall, wide = bases * DIAGONAL, sides * DIAGONAL
    for start in range(0, depth, DIAGONAL):
        left = basis[:, start : start + DIAGONAL, :].reshape(tall, width)
        right = moments[:, start : start + DIAGONAL, :].reshape(wide, width)
        product = lax.dot_general(left, right, (((1,), (1,)), ((), ())), preferred_element_type=F32)
        if start == 0:
            total[...] = product
        else:
            total[...] += product
    same = iota((tall, wide), 0) % DIAGONAL == iota((tall, wide), 1) % DIAGONAL
    rows = (iota((bases, tall), 1) // DIAGONAL == iota((bases, tall), 0)).astype(BF16)
    columns = (iota((wide, sides), 0) // DIAGONAL == iota((wide, sides), 1)).astype(BF16)
    tower = jnp.zeros((bases, wide), F32)
    for part in split(jnp.where(same, total[...], 0.0)):
        tower += jnp.dot(rows, part, preferred_element_type=F32)
    per_tile = jnp.zeros((bases, sides), F32)
    for part in split(tower):
        per_tile += jnp.dot(part, columns, preferred_element_type=F32)
    live = live_ref[0, 0]
    per_tile = jnp.where(iota((bases, sides), 1) % tiles < live, per_tile, 0.0)
    first = core_ref[0] == 0
    forward, inverse = per_tile[:, :tiles], per_tile[:, tiles:]
    names = iota((PAYLOAD - bases, tiles), 0)
    lane = iota((PAYLOAD - bases, tiles), 1)
    for ref, chosen in ((mine_ref, first), (other_ref, jnp.logical_not(first))):
        ref[:bases, :] = jnp.where(chosen, forward, inverse).astype(BF16)
        named = jnp.zeros((PAYLOAD - bases, tiles), jnp.int32)
        for tile in range(tiles):
            name = entry_ref[0, tile] + jnp.where(chosen, 0, entry_ref[3, tile])
            digits = jnp.where(names == 0, name // LANES, jnp.where(names == 1, name % LANES, 0))
            named = jnp.where(lane == tile, digits, named)
        ref[bases:, :] = named.astype(F32).astype(BF16)


def gradients(entries, live, core, mask, row_pieces, inverse_rows, basis, columns):
    tiles, block, _ = mask.shape
    bases, depth, width = basis.shape
    payload = jax.ShapeDtypeStruct((PAYLOAD, tiles), BF16)

    def room(pieces):
        return pltpu.VMEM((sum(piece.shape[0] for piece in pieces), 2 * block, width), BF16)

    return pl.pallas_call(
        functools.partial(gradient_kernel, len(columns), len(row_pieces)),
        out_shape=(jax.ShapeDtypeStruct((tiles, block, width), BF16), payload, payload),
        in_specs=[SMEM, SMEM, SMEM, VMEM, VMEM, HBM] + [ANY] * (len(columns) + len(row_pieces)),
        out_specs=(VMEM, VMEM, VMEM),
        scratch_shapes=[
            room(columns),
            room(row_pieces),
            pltpu.VMEM(basis.shape, BF16),
            pltpu.VMEM((2 * tiles, depth, width), BF16),
            pltpu.VMEM((bases * DIAGONAL, 2 * tiles * DIAGONAL), F32),
            pltpu.SemaphoreType.DMA((len(columns),)),
            pltpu.SemaphoreType.DMA((len(row_pieces),)),
            pltpu.SemaphoreType.DMA,
        ],
        compiler_params=params(50),
        cost_estimate=cost(4 * 10**9, 12 * 10**6),
        name="gradients",
    )(entries, live, core, mask, inverse_rows, basis, *columns, *row_pieces)


def place_kernel(entry_ref, out_ref, total):
    bases, window = out_ref.shape
    count, _, span = entry_ref.shape
    for index in range(count):
        values = entry_ref[index, :bases, :].astype(F32)
        names = entry_ref[index, bases:, :].astype(F32)
        high, low = names[:1], names[1:2]
        chosen = (iota((LANES, span), 0).astype(F32) == low).astype(F32).astype(BF16)
        spread = [jnp.where(high == part, values, 0.0).astype(BF16) for part in range(window // LANES)]
        product = lax.dot_general(
            jnp.concatenate(spread, axis=0), chosen, (((1,), (1,)), ((), ())), preferred_element_type=F32
        )
        if index == 0:
            total[...] = product
        else:
            total[...] += product
    for part in range(window // LANES):
        out_ref[:, part * LANES : part * LANES + LANES] = total[part * bases : part * bases + bases, :]


def place_rows(entries, bases, window):
    return pl.pallas_call(
        place_kernel,
        out_shape=jax.ShapeDtypeStruct((bases, window), F32),
        in_specs=[VMEM],
        out_specs=VMEM,
        scratch_shapes=[pltpu.VMEM((window // LANES * bases, LANES), F32)],
        compiler_params=params(16),
        cost_estimate=cost(10**9, 10**6),
        name="place_rows",
    )(entries)


def join_kernel(plan, count, *refs):
    sems = refs[-1]
    copies = []
    for output, pieces in enumerate(plan):
        at = 0
        for source, start, size in pieces:
            copies.append(
                pltpu.make_async_copy(
                    refs[source].at[pl.ds(start, size)],
                    refs[count + output].at[pl.ds(at, size)],
                    sems.at[len(copies)],
                )
            )
            at += size
    for copy in copies:
        copy.start()
    for copy in copies:
        copy.wait()


def join(sources, plan):
    shape = sources[0].shape[1:]
    sizes = [sum(size for _, _, size in pieces) for pieces in plan]
    return pl.pallas_call(
        functools.partial(join_kernel, plan, len(sources)),
        out_shape=tuple(jax.ShapeDtypeStruct((size,) + shape, sources[0].dtype) for size in sizes),
        in_specs=[ANY] * len(sources),
        out_specs=tuple(ANY for _ in plan),
        scratch_shapes=[pltpu.SemaphoreType.DMA((sum(len(pieces) for pieces in plan),))],
        compiler_params=params(4),
        cost_estimate=cost(0, 10**6),
        name="join",
    )(*sources)


def finish_kernel(base, core_ref, own_ref, partner_ref, out_ref):
    window = own_ref.shape[1]
    shared = window - base
    last = out_ref.shape[1]
    first = core_ref[0] == 0
    out_ref[:, :base] = jnp.where(first, own_ref[:, :base], partner_ref[:, :base])
    out_ref[:, base:window] = jnp.where(first, own_ref[:, base:], partner_ref[:, base:]) + jnp.where(
        first, partner_ref[:, :shared], own_ref[:, :shared]
    )
    out_ref[:, window:] = jnp.where(
        first, partner_ref[:, shared : last - base], own_ref[:, shared : last - base]
    )


def finish(core, own, partner, base, relations):
    return pl.pallas_call(
        functools.partial(finish_kernel, base),
        out_shape=jax.ShapeDtypeStruct((own.shape[0], 2 * relations), F32),
        in_specs=[SMEM, VMEM, VMEM],
        out_specs=VMEM,
        compiler_params=params(8),
        cost_estimate=cost(0, 10**6),
        name="finish",
    )(core, own, partner)


def pack_kernel(feature_ref, cotangent_ref, own_ref, copies_ref, sems):
    block = feature_ref.shape[0]
    copies = [
        pltpu.make_async_copy(ref, own_ref.at[0, pl.ds(index * block, block), :], sems.at[index])
        for index, ref in enumerate((feature_ref, cotangent_ref))
    ]
    for copy in copies:
        copy.start()
    for copy in copies:
        copy.wait()
    for index in range(copies_ref.shape[0]):
        copies_ref[index] = own_ref[0]


def pack(features, cotangent, count):
    block, width = features.shape
    return pl.pallas_call(
        pack_kernel,
        out_shape=tuple(jax.ShapeDtypeStruct((blocks, 2 * block, width), BF16) for blocks in (1, count)),
        in_specs=[HBM, HBM],
        out_specs=(VMEM, VMEM),
        scratch_shapes=[pltpu.SemaphoreType.DMA((2,))],
        compiler_params=params(60),
        cost_estimate=cost(0, 10**6),
        name="pack",
    )(features, cotangent)


X_HI, RING, CORES = 2, 8, 2
Y, X_LO = 4, 2


def from_row(array, dx=0, dz=0, dk=0):
    pairs = []
    for x in range(X_HI):
        for z in range(RING):
            for k in range(CORES):
                source = ((x ^ dx) * RING + (z + dz) % RING) * CORES + (k ^ dk)
                pairs.append((source, (x * RING + z) * CORES + k))
    return lax.ppermute(array, "prow", pairs)


def from_column(array, dy=0, dx=0):
    pairs = []
    for y in range(Y):
        for x in range(X_LO):
            pairs.append((((y + dy) % Y) * X_LO + (x ^ dx), y * X_LO + x))
    return lax.ppermute(array, "pcol", pairs)


def tie(*arrays):
    return lax.optimization_barrier(arrays)


def coordinates():
    row = lax.axis_index("prow")
    column = lax.axis_index("pcol")
    return row // (RING * CORES), (row // CORES) % RING, row % CORES, column // X_LO, column % X_LO


def column_position(source, x, z, k):
    dx = (source // (RING * CORES)) ^ x
    dz = ((source // CORES) % RING - z) % RING
    dk = (source % CORES) ^ k
    even = dx * 4 + ((dz + 2) % RING) // 2
    odd = 8 + 4 * (dz // 4) + 2 * dx + (dz % 4) // 2
    return dk * 16 + jnp.where(dz % 2 == 0, even, odd)


def ordered(first, own, other, dim):
    return jnp.concatenate([jnp.where(first, own, other), jnp.where(first, other, own)], axis=dim)


def row_groups(apart):
    return [
        [(x * RING + z) * CORES + k for x in range(X_HI) for z in range(first, RING, apart)]
        for first in range(apart)
        for k in range(CORES)
    ]


def z_groups():
    return [
        [(x * RING + z) * CORES + k for z in range(RING)] for x in range(X_HI) for k in range(CORES)
    ]


def gather_gradients(mine, arrived, held, place):
    _, _, k, y, x_lo = place
    entries = ordered(k == 0, mine, arrived, 1)
    entries = ordered(x_lo == 0, entries, from_column(entries, dx=1), 1)
    around = [entries] + [from_column(entries, dy=dy) for dy in range(1, Y)]
    entries = jnp.concatenate(
        [functools.reduce(lambda a, dy: jnp.where(y == (at - dy) % Y, around[dy], a), range(1, Y), around[0]) for at in range(Y)],
        axis=1,
    )
    copies = jnp.broadcast_to(entries[None], (X_HI * RING,) + entries.shape)
    copies, *held = tie(copies, *held)
    gathered = lax.all_to_all(copies, "prow", 0, 0, tiled=True, axis_index_groups=row_groups(1))
    return gathered, held


def on_device(features, cotangent, self_weight, basis_weights, coefficients, tile_list, tile_mask, live_tiles):
    block, width = features.shape
    relations = coefficients.shape[0] // 2
    bases = coefficients.shape[1]
    rows_count = X_HI * RING * CORES
    place = coordinates()
    x, z, k, y, x_lo = place
    mask = tile_mask[0, 0]
    relation, source, target = tile_list[0, 0, :, 0], tile_list[0, 0, :, 1], tile_list[0, 0, :, 2]
    apart = ((source % CORES ^ k) * X_HI + (source // (RING * CORES) ^ x)) * RING + source // CORES % RING
    near = (target // X_LO - y) % Y * X_LO + (target % X_LO ^ x_lo)
    shift = jnp.full_like(relation, relations % LANES)
    entries = jnp.stack([relation, column_position(source, x, z, k), target, shift, apart, near])
    rows_named = jnp.concatenate([relation, relation + relations])[None]

    own, copies = pack(features, cotangent, Y * X_LO)
    ring = [from_row(own, dz=dz) for dz in (4, 2, 6)]
    row_blocks = lax.all_to_all(copies, "pcol", 0, 0, tiled=True)
    (even,) = join([ring[2], own, ring[1], ring[0]], (((0, 0, 1), (1, 0, 1), (2, 0, 1), (3, 0, 1)),))
    across = from_row(even, dx=1)
    even, rows_named = tie(even, rows_named)
    weights = relation_weights(rows_named, coefficients.T, basis_weights)
    across, weights = tie(across, weights)
    upward, downward = join([even, across], (((0, 1, 2), (1, 1, 2)), ((0, 0, 2), (1, 0, 2))))
    upward, downward, even, across = tie(upward, downward, even, across)
    near = (even, across, from_row(upward, dz=1), from_row(downward, dz=7))
    columns = near + tuple(from_row(piece, dk=1) for piece in near)
    columns = list(columns)
    columns[4], columns[5], weights = tie(columns[4], columns[5], weights)
    row_pieces = [row_blocks]
    inverse_rows, keep_near, keep_far, *sends = inverse_messages(
        entries, live_tiles, mask, row_pieces, weights, rows_count
    )
    swapped = [from_row(part, dk=1) for part in sends]
    crossing = (keep_far + jnp.concatenate(swapped[2:]).astype(F32)).astype(BF16)
    *columns, crossing = tie(*columns, crossing)
    inverse_sum = keep_near + jnp.concatenate(swapped[:2]).astype(F32) + from_row(crossing, dx=1).astype(F32)
    inverse_sum = inverse_sum.astype(BF16).reshape(RING, block, width)
    inverse_parts = lax.all_to_all(inverse_sum, "prow", 0, 0, tiled=True, axis_index_groups=z_groups())
    forward_rows, mine, other = gradients(
        entries, live_tiles, k.reshape(1), mask, row_pieces, inverse_rows, basis_weights, columns
    )
    arrived, forward_rows = tie(from_row(other, dk=1), forward_rows)
    gathered, (forward_rows, inverse_parts) = gather_gradients(mine, arrived, (forward_rows, inverse_parts), place)
    forward_pair, *sends = forward_messages(entries, live_tiles, forward_rows, weights)
    sends = [from_column(part, dy=Y - dy) for dy, part in enumerate(sends, 1)]
    base = relations // LANES * LANES
    window = -(-(2 * relations - base) // LANES) * LANES
    placed = place_rows(gathered, bases, window)
    coefficient_grads = finish(k.reshape(1), placed, from_row(placed, dk=1), base, relations).T
    _, *sends = tie(placed, *sends)
    for part in sends:
        forward_pair += part.astype(F32)
    forward_sum = forward_pair[0] + from_column(forward_pair[1].astype(BF16), dx=1).astype(F32)
    layer_sum = jnp.dot(features, self_weight, preferred_element_type=F32)
    layer_sum += jnp.sum(inverse_parts.astype(F32), axis=0) + forward_sum
    return layer_sum.astype(BF16), coefficient_grads


def solution(mesh):
    return jax.shard_map(
        on_device,
        mesh=mesh,
        in_specs=(
            P(("prow", "pcol"), None),
            P(("prow", "pcol"), None),
            P(),
            P(),
            P(),
            P("prow", "pcol", None, None),
            P("prow", "pcol", None, None, None),
            P("prow", "pcol"),
        ),
        out_specs=(P(("prow", "pcol"), None), P()),
        check_vma=False,
    )
```

```python
import functools
import jax
import jax.numpy as jnp
from jax import lax
from jax.experimental import pallas as pl
from jax.experimental.pallas import tpu as pltpu
from jax.sharding import PartitionSpec as P

F32, BF16 = jnp.float32, jnp.bfloat16
VMEM = pl.BlockSpec(memory_space=pltpu.VMEM)
SMEM = pl.BlockSpec(memory_space=pltpu.SMEM)
ANY = pl.BlockSpec(memory_space=pl.ANY)
HBM = pl.BlockSpec(memory_space=pltpu.HBM)
LANES = 128
DIAGONAL = 16
STEP = 64
PAYLOAD = 48


def params(mib):
    return pltpu.CompilerParams(vmem_limit_bytes=mib * 1024 * 1024)


def cost(flops, moved):
    return pl.CostEstimate(flops=flops, bytes_accessed=moved, transcendentals=0)


def split(wide):
    high = wide.astype(BF16)
    return high, (wide - high.astype(F32)).astype(BF16)


def iota(shape, dim):
    return lax.broadcasted_iota(jnp.int32, shape, dim)


def weights_kernel(parts, row_ref, coefficient_ref, basis_ref, weight_ref, spread, basis, weight, in_sems, out_sems):
    bases, named = coefficient_ref.shape
    sides = row_ref.shape[1]
    depth, width = basis.shape[1:]
    size = depth // parts
    tall, wide = sides * DIAGONAL, bases * DIAGONAL
    arrive, leave = [], []
    for part in range(parts):
        rows = pl.ds(part * size, size)
        arrive.append(pltpu.make_async_copy(basis_ref.at[:, rows, :], basis.at[:, rows, :], in_sems.at[part]))
        leave.append(pltpu.make_async_copy(weight.at[:, rows, :], weight_ref.at[:, rows, :], out_sems.at[part]))
    for copy in arrive:
        copy.start()
    chosen = (iota((named, sides), 0) == row_ref[...]).astype(F32).astype(BF16)
    rows = (iota((tall, sides), 0) // DIAGONAL == iota((tall, sides), 1)).astype(F32).astype(BF16)
    columns = (iota((bases, wide), 1) // DIAGONAL == iota((bases, wide), 0)).astype(F32).astype(BF16)
    same = iota((tall, wide), 0) % DIAGONAL == iota((tall, wide), 1) % DIAGONAL
    for index, part in enumerate(split(coefficient_ref[...])):
        picked = jnp.dot(part, chosen, preferred_element_type=F32).astype(BF16)
        tower = lax.dot_general(rows, picked, (((1,), (1,)), ((), ())), preferred_element_type=F32).astype(BF16)
        full = jnp.dot(tower, columns, preferred_element_type=F32)
        spread[index] = jnp.where(same, full, 0.0).astype(BF16)
    for start in range(0, depth, DIAGONAL):
        if start % size == 0:
            arrive[start // size].wait()
        part = basis[:, start : start + DIAGONAL, :].reshape(wide, width)
        total = jnp.dot(spread[0], part, preferred_element_type=F32)
        total += jnp.dot(spread[1], part, preferred_element_type=F32)
        weight[:, start : start + DIAGONAL, :] = total.astype(BF16).reshape(sides, DIAGONAL, width)
        if (start + DIAGONAL) % size == 0:
            leave[start // size].start()
    for copy in leave:
        copy.wait()


def relation_weights(rows_named, coefficients_t, basis, parts=4):
    bases, depth, width = basis.shape
    sides = rows_named.shape[1]
    return pl.pallas_call(
        functools.partial(weights_kernel, parts),
        out_shape=jax.ShapeDtypeStruct((sides, depth, width), BF16),
        in_specs=[VMEM, VMEM, HBM],
        out_specs=HBM,
        scratch_shapes=[
            pltpu.VMEM((2, sides * DIAGONAL, bases * DIAGONAL), BF16),
            pltpu.VMEM(basis.shape, BF16),
            pltpu.VMEM((sides, depth, width), BF16),
            pltpu.SemaphoreType.DMA((parts,)),
            pltpu.SemaphoreType.DMA((parts,)),
        ],
        compiler_params=params(56),
        cost_estimate=cost(4 * 10**9, 2 * basis.size * 2),
        name="relation_weights",
    )(rows_named, coefficients_t, basis)


def normalised(mask, rows, dim):
    over = (((dim,), (0,)), ((), ()))
    summed = lax.dot_general(mask, rows, over, preferred_element_type=F32)
    degree = lax.dot_general(mask, jnp.ones((mask.shape[dim], LANES), BF16), over, preferred_element_type=F32)
    scale = (1.0 / (1.0 + degree)).astype(BF16).astype(F32)
    return (summed * jnp.concatenate([scale] * (rows.shape[1] // LANES), axis=1)).astype(BF16)


def copies_into(target, refs, sems):
    copies, at = [], 0
    for index, ref in enumerate(refs):
        size = ref.shape[0]
        copies.append(pltpu.make_async_copy(ref, target.at[pl.ds(at, size)], sems.at[index]))
        at += size
    for copy in copies:
        copy.start()
    return copies


def block_at(index, size):
    return pl.ds(pl.multiple_of(index * size, size), size)


def inverse_kernel(pieces, entry_ref, live_ref, mask_ref, weights_ref, *refs):
    rows_ref, keep_ref, send_ref, total, row, weight, row_sems, sem = refs[pieces:]
    tiles, block, _ = mask_ref.shape
    arrive = copies_into(row, refs[:pieces], row_sems)
    copy = pltpu.make_async_copy(weights_ref, weight, sem)
    copy.start()
    total[...] = jnp.zeros_like(total)
    for part in arrive:
        part.wait()
    for tile in range(tiles):
        rows = row[entry_ref[2, tile], :block, :]
        rows_ref[tile] = normalised(mask_ref[tile].astype(F32).astype(BF16), rows, 0)
    copy.wait()
    for tile in range(tiles):
        weighting = (tile < live_ref[0, 0]).astype(F32)
        message = jnp.dot(rows_ref[tile], weight[tile], preferred_element_type=F32) * weighting
        total[block_at(entry_ref[4, tile], block), :] += message
    half = keep_ref.shape[0]
    keep_ref[...] = total[:half, :]
    send_ref[...] = total[half:, :].astype(BF16)


def inverse_messages(entries, live, mask, row_pieces, weights, row_count):
    tiles, block, _ = mask.shape
    width = row_pieces[0].shape[2]
    half = row_count * block // 2
    columns = sum(piece.shape[0] for piece in row_pieces)
    return pl.pallas_call(
        functools.partial(inverse_kernel, len(row_pieces)),
        out_shape=(
            jax.ShapeDtypeStruct((tiles, block, width), BF16),
            jax.ShapeDtypeStruct((half, width), F32),
            jax.ShapeDtypeStruct((half, width), BF16),
        ),
        in_specs=[SMEM, SMEM, VMEM, HBM] + [ANY] * len(row_pieces),
        out_specs=(VMEM, VMEM, VMEM),
        scratch_shapes=[
            pltpu.VMEM((2 * half, width), F32),
            pltpu.VMEM((columns,) + row_pieces[0].shape[1:], BF16),
            pltpu.VMEM((tiles, width, width), BF16),
            pltpu.SemaphoreType.DMA((len(row_pieces),)),
            pltpu.SemaphoreType.DMA,
        ],
        compiler_params=params(52),
        cost_estimate=cost(10**9, 8 * 10**6),
        name="inverse_messages",
    )(entries, live, mask, weights, *row_pieces)


def forward_kernel(entry_ref, live_ref, rows_ref, weights_ref, keep_ref, *refs):
    send_refs, (total, rows, weight, sems) = refs[:-4], refs[-4:]
    tiles, block, _ = rows.shape
    rows_copy = pltpu.make_async_copy(rows_ref, rows, sems.at[0])
    weight_copy = pltpu.make_async_copy(weights_ref, weight, sems.at[1])
    rows_copy.start()
    weight_copy.start()
    total[...] = jnp.zeros_like(total)
    rows_copy.wait()
    weight_copy.wait()
    for tile in range(tiles):
        weighting = (tile < live_ref[0, 0]).astype(F32)
        message = jnp.dot(rows[tile], weight[tile], preferred_element_type=F32) * weighting
        total[entry_ref[2, tile]] += message
    pair = keep_ref.shape[0]
    keep_ref[...] = total[:pair]
    for index, ref in enumerate(send_refs):
        ref[...] = total[pair * (index + 1) : pair * (index + 2)].astype(BF16)


def forward_messages(entries, live, rows, weights):
    tiles, block, width = rows.shape
    shape = (X_LO, block, width)
    return pl.pallas_call(
        forward_kernel,
        out_shape=(jax.ShapeDtypeStruct(shape, F32),) + (jax.ShapeDtypeStruct(shape, BF16),) * (Y - 1),
        in_specs=[SMEM, SMEM, ANY, HBM],
        out_specs=(VMEM,) * Y,
        scratch_shapes=[
            pltpu.VMEM((Y * X_LO, block, width), F32),
            pltpu.VMEM(rows.shape, BF16),
            pltpu.VMEM((tiles, width, width), BF16),
            pltpu.SemaphoreType.DMA((2,)),
        ],
        compiler_params=params(56),
        cost_estimate=cost(10**9, 4 * 10**6),
        name="forward_messages",
    )(entries, live, rows, weights)


def gradient_kernel(pieces, row_pieces, entry_ref, live_ref, core_ref, mask_ref, inverse_ref, basis_ref, *refs):
    column_refs, row_refs, refs = refs[:pieces], refs[pieces : pieces + row_pieces], refs[pieces + row_pieces :]
    rows_ref, mine_ref, other_ref, *refs = refs
    column, row, mask, inverse, forward, basis, moments, total, column_sem, row_sem, sems = refs
    tiles, block, _ = mask.shape
    bases, depth, width = basis.shape
    sides = 2 * tiles
    mask_copy = pltpu.make_async_copy(mask_ref, mask, sems.at[0])
    inverse_copy = pltpu.make_async_copy(inverse_ref, inverse, sems.at[1])
    basis_copy = pltpu.make_async_copy(basis_ref, basis, sems.at[2])
    forward_copy = pltpu.make_async_copy(forward, rows_ref, sems.at[3])
    mask_copy.start()
    copies = copies_into(column, column_refs, column_sem) + copies_into(row, row_refs, row_sem)
    inverse_copy.start()
    basis_copy.start()
    mask_copy.wait()
    for copy in copies:
        copy.wait()
    for tile in range(tiles):
        rows = column[entry_ref[1, tile], :block, :]
        forward[tile] = normalised(mask[tile].astype(F32).astype(BF16), rows, 1)
    forward_copy.start()
    inverse_copy.wait()
    over = (((0,), (0,)), ((), ()))
    for tile in range(tiles):
        target = row[entry_ref[2, tile], block:, :]
        source = column[entry_ref[1, tile], block:, :]
        moments[tile] = lax.dot_general(forward[tile], target, over, preferred_element_type=F32).astype(BF16)
        moments[tiles + tile] = lax.dot_general(
            inverse[tile], source, over, preferred_element_type=F32
        ).astype(BF16)
    basis_copy.wait()
    tall, wide = bases * DIAGONAL, sides * DIAGONAL
    for start in range(0, depth, STEP):
        rows = range(start, start + STEP, DIAGONAL)
        left = jnp.concatenate([basis[:, at : at + DIAGONAL, :].reshape(tall, width) for at in rows], axis=1)
        right = jnp.concatenate([moments[:, at : at + DIAGONAL, :].reshape(wide, width) for at in rows], axis=1)
        product = lax.dot_general(left, right, (((1,), (1,)), ((), ())), preferred_element_type=F32)
        if start == 0:
            total[...] = product
        else:
            total[...] += product
    same = iota((tall, wide), 0) % DIAGONAL == iota((tall, wide), 1) % DIAGONAL
    rows = (iota((bases, tall), 1) // DIAGONAL == iota((bases, tall), 0)).astype(BF16)
    columns = (iota((wide, sides), 0) // DIAGONAL == iota((wide, sides), 1)).astype(BF16)
    tower = jnp.zeros((bases, wide), F32)
    for part in split(jnp.where(same, total[...], 0.0)):
        tower += jnp.dot(rows, part, preferred_element_type=F32)
    per_tile = jnp.zeros((bases, sides), F32)
    for part in split(tower):
        per_tile += jnp.dot(part, columns, preferred_element_type=F32)
    live = live_ref[0, 0]
    per_tile = jnp.where(iota((bases, sides), 1) % tiles < live, per_tile, 0.0)
    first = core_ref[0] == 0
    forward, inverse = per_tile[:, :tiles], per_tile[:, tiles:]
    names = iota((PAYLOAD - bases, tiles), 0)
    lane = iota((PAYLOAD - bases, tiles), 1)
    for ref, chosen in ((mine_ref, first), (other_ref, jnp.logical_not(first))):
        ref[:bases, :] = jnp.where(chosen, forward, inverse).astype(BF16)
        named = jnp.zeros((PAYLOAD - bases, tiles), jnp.int32)
        for tile in range(tiles):
            name = entry_ref[0, tile] + jnp.where(chosen, 0, entry_ref[3, tile])
            digits = jnp.where(names == 0, name // LANES, jnp.where(names == 1, name % LANES, 0))
            named = jnp.where(lane == tile, digits, named)
        ref[bases:, :] = named.astype(F32).astype(BF16)
    forward_copy.wait()


def gradients(entries, live, core, mask, row_pieces, inverse_rows, basis, columns):
    tiles, block, _ = mask.shape
    bases, depth, width = basis.shape
    payload = jax.ShapeDtypeStruct((PAYLOAD, tiles), BF16)

    def room(pieces):
        return pltpu.VMEM((sum(piece.shape[0] for piece in pieces), 2 * block, width), BF16)

    return pl.pallas_call(
        functools.partial(gradient_kernel, len(columns), len(row_pieces)),
        out_shape=(jax.ShapeDtypeStruct((tiles, block, width), BF16), payload, payload),
        in_specs=[SMEM, SMEM, SMEM, ANY, ANY, HBM] + [ANY] * (len(columns) + len(row_pieces)),
        out_specs=(ANY, VMEM, VMEM),
        scratch_shapes=[
            room(columns),
            room(row_pieces),
            pltpu.VMEM(mask.shape, jnp.int32),
            pltpu.VMEM(inverse_rows.shape, BF16),
            pltpu.VMEM(inverse_rows.shape, BF16),
            pltpu.VMEM(basis.shape, BF16),
            pltpu.VMEM((2 * tiles, depth, width), BF16),
            pltpu.VMEM((bases * DIAGONAL, 2 * tiles * DIAGONAL), F32),
            pltpu.SemaphoreType.DMA((len(columns),)),
            pltpu.SemaphoreType.DMA((len(row_pieces),)),
            pltpu.SemaphoreType.DMA((4,)),
        ],
        compiler_params=params(56),
        cost_estimate=cost(0, 1000),
        name="gradients",
    )(entries, live, core, mask, inverse_rows, basis, *columns, *row_pieces)


def place_kernel(entry_ref, out_ref, total):
    bases, window = out_ref.shape
    count, _, span = entry_ref.shape
    for index in range(count):
        values = entry_ref[index, :bases, :].astype(F32)
        names = entry_ref[index, bases:, :].astype(F32)
        high, low = names[:1], names[1:2]
        chosen = (iota((LANES, span), 0).astype(F32) == low).astype(F32).astype(BF16)
        spread = [jnp.where(high == part, values, 0.0).astype(BF16) for part in range(window // LANES)]
        product = lax.dot_general(
            jnp.concatenate(spread, axis=0), chosen, (((1,), (1,)), ((), ())), preferred_element_type=F32
        )
        if index == 0:
            total[...] = product
        else:
            total[...] += product
    for part in range(window // LANES):
        out_ref[:, part * LANES : part * LANES + LANES] = total[part * bases : part * bases + bases, :]


def place_rows(entries, bases, window):
    return pl.pallas_call(
        place_kernel,
        out_shape=jax.ShapeDtypeStruct((bases, window), F32),
        in_specs=[VMEM],
        out_specs=VMEM,
        scratch_shapes=[pltpu.VMEM((window // LANES * bases, LANES), F32)],
        compiler_params=params(16),
        cost_estimate=cost(10**9, 10**6),
        name="place_rows",
    )(entries)


def join_kernel(plan, count, *refs):
    sems = refs[-1]
    copies = []
    for output, pieces in enumerate(plan):
        at = 0
        for source, start, size in pieces:
            copies.append(
                pltpu.make_async_copy(
                    refs[source].at[pl.ds(start, size)],
                    refs[count + output].at[pl.ds(at, size)],
                    sems.at[len(copies)],
                )
            )
            at += size
    for copy in copies:
        copy.start()
    for copy in copies:
        copy.wait()


def join(sources, plan):
    shape = sources[0].shape[1:]
    sizes = [sum(size for _, _, size in pieces) for pieces in plan]
    return pl.pallas_call(
        functools.partial(join_kernel, plan, len(sources)),
        out_shape=tuple(jax.ShapeDtypeStruct((size,) + shape, sources[0].dtype) for size in sizes),
        in_specs=[ANY] * len(sources),
        out_specs=tuple(ANY for _ in plan),
        scratch_shapes=[pltpu.SemaphoreType.DMA((sum(len(pieces) for pieces in plan),))],
        compiler_params=params(4),
        cost_estimate=cost(0, 10**6),
        name="join",
    )(*sources)


def finish_kernel(base, core_ref, own_ref, partner_ref, out_ref):
    window = own_ref.shape[1]
    shared = window - base
    last = out_ref.shape[1]
    first = core_ref[0] == 0
    out_ref[:, :base] = jnp.where(first, own_ref[:, :base], partner_ref[:, :base])
    out_ref[:, base:window] = jnp.where(first, own_ref[:, base:], partner_ref[:, base:]) + jnp.where(
        first, partner_ref[:, :shared], own_ref[:, :shared]
    )
    out_ref[:, window:] = jnp.where(
        first, partner_ref[:, shared : last - base], own_ref[:, shared : last - base]
    )


def finish(core, own, partner, base, relations):
    return pl.pallas_call(
        functools.partial(finish_kernel, base),
        out_shape=jax.ShapeDtypeStruct((own.shape[0], 2 * relations), F32),
        in_specs=[SMEM, VMEM, VMEM],
        out_specs=VMEM,
        compiler_params=params(8),
        cost_estimate=cost(0, 10**6),
        name="finish",
    )(core, own, partner)


def pack_kernel(feature_ref, cotangent_ref, own_ref, sems):
    block = feature_ref.shape[0]
    copies = [
        pltpu.make_async_copy(ref, own_ref.at[0, pl.ds(index * block, block), :], sems.at[index])
        for index, ref in enumerate((feature_ref, cotangent_ref))
    ]
    for copy in copies:
        copy.start()
    for copy in copies:
        copy.wait()


def pack(features, cotangent):
    block, width = features.shape
    return pl.pallas_call(
        pack_kernel,
        out_shape=jax.ShapeDtypeStruct((1, 2 * block, width), BF16),
        in_specs=[HBM, HBM],
        out_specs=VMEM,
        scratch_shapes=[pltpu.SemaphoreType.DMA((2,))],
        compiler_params=params(60),
        cost_estimate=cost(0, 10**6),
        name="pack",
    )(features, cotangent)


X_HI, RING, CORES = 2, 8, 2
Y, X_LO = 4, 2


def from_row(array, dx=0, dz=0, dk=0):
    pairs = []
    for x in range(X_HI):
        for z in range(RING):
            for k in range(CORES):
                source = ((x ^ dx) * RING + (z + dz) % RING) * CORES + (k ^ dk)
                pairs.append((source, (x * RING + z) * CORES + k))
    return lax.ppermute(array, "prow", pairs)


def from_column(array, dy=0, dx=0):
    pairs = []
    for y in range(Y):
        for x in range(X_LO):
            pairs.append((((y + dy) % Y) * X_LO + (x ^ dx), y * X_LO + x))
    return lax.ppermute(array, "pcol", pairs)


def tie(*arrays):
    return lax.optimization_barrier(arrays)


def coordinates():
    row = lax.axis_index("prow")
    column = lax.axis_index("pcol")
    return row // (RING * CORES), (row // CORES) % RING, row % CORES, column // X_LO, column % X_LO


def column_position(source, x, z, k):
    dx = (source // (RING * CORES)) ^ x
    dz = ((source // CORES) % RING - z) % RING
    dk = (source % CORES) ^ k
    even = dx * 4 + ((dz + 2) % RING) // 2
    odd = 8 + 4 * (dz // 4) + 2 * dx + (dz % 4) // 2
    return dk * 16 + jnp.where(dz % 2 == 0, even, odd)


def ordered(first, own, other, dim):
    return jnp.concatenate([jnp.where(first, own, other), jnp.where(first, other, own)], axis=dim)


def row_groups(apart):
    return [
        [(x * RING + z) * CORES + k for x in range(X_HI) for z in range(first, RING, apart)]
        for first in range(apart)
        for k in range(CORES)
    ]


def gather_gradients(mine, arrived, held, place):
    _, _, k, y, x_lo = place
    entries = ordered(k == 0, mine, arrived, 1)
    entries = ordered(x_lo == 0, entries, from_column(entries, dx=1), 1)
    around = [entries] + [from_column(entries, dy=dy) for dy in range(1, Y)]
    entries = jnp.concatenate(
        [functools.reduce(lambda a, dy: jnp.where(y == (at - dy) % Y, around[dy], a), range(1, Y), around[0]) for at in range(Y)],
        axis=1,
    )
    copies = jnp.broadcast_to(entries[None], (X_HI * RING,) + entries.shape)
    copies, *held = tie(copies, *held)
    gathered = lax.all_to_all(copies, "prow", 0, 0, tiled=True, axis_index_groups=row_groups(1))
    return gathered, held


def on_device(features, cotangent, self_weight, basis_weights, coefficients, tile_list, tile_mask, live_tiles):
    block, width = features.shape
    relations = coefficients.shape[0] // 2
    bases = coefficients.shape[1]
    rows_count = X_HI * RING * CORES
    place = coordinates()
    x, z, k, y, x_lo = place
    mask = tile_mask[0, 0]
    relation, source, target = tile_list[0, 0, :, 0], tile_list[0, 0, :, 1], tile_list[0, 0, :, 2]
    apart = (source % CORES ^ k) * (X_HI * RING) + source // CORES
    near = (target // X_LO - y) % Y * X_LO + (target % X_LO ^ x_lo)
    shift = jnp.full_like(relation, relations % LANES)
    entries = jnp.stack([relation, column_position(source, x, z, k), near, shift, apart])
    forward_named, inverse_named = relation[None], relation[None] + relations

    own = pack(features, cotangent)
    ring = [from_row(own, dz=dz) for dz in (4, 2, 6)]
    (pair,) = join([own, from_column(own, dx=1)], (((0, 0, 1), (1, 0, 1)),))
    row_pieces = [pair] + [from_column(pair, dy=dy) for dy in range(1, Y)]
    (even,) = join([ring[2], own, ring[1], ring[0]], (((0, 0, 1), (1, 0, 1), (2, 0, 1), (3, 0, 1)),))
    across = from_row(even, dx=1)
    even, inverse_named = tie(even, inverse_named)
    weights = relation_weights(inverse_named, coefficients.T, basis_weights)
    inverse_rows, keep, send = inverse_messages(entries, live_tiles, mask, row_pieces, weights, rows_count)
    across, inverse_rows, keep, send, forward_named = tie(across, inverse_rows, keep, send, forward_named)
    upward, downward = join([even, across], (((0, 1, 2), (1, 1, 2)), ((0, 0, 2), (1, 0, 2))))
    near = (even, across, from_row(upward, dz=1), from_row(downward, dz=7))
    columns = near + tuple(from_row(piece, dk=1) for piece in near)
    weights = relation_weights(forward_named, coefficients.T, basis_weights)
    inverse_part = (keep + from_row(send, dk=1).astype(F32)).astype(BF16).reshape(X_HI * RING, block, width)
    *columns, inverse_part, weights = tie(*columns, inverse_part, weights)
    inverse_parts = lax.all_to_all(inverse_part, "prow", 0, 0, tiled=True, axis_index_groups=row_groups(1))
    forward_rows, mine, other = gradients(
        entries, live_tiles, k.reshape(1), mask, row_pieces, inverse_rows, basis_weights, columns
    )
    arrived, forward_rows = tie(from_row(other, dk=1), forward_rows)
    gathered, (forward_rows, inverse_parts) = gather_gradients(mine, arrived, (forward_rows, inverse_parts), place)
    forward_pair, *sends = forward_messages(entries, live_tiles, forward_rows, weights)
    sends = [from_column(part, dy=Y - dy) for dy, part in enumerate(sends, 1)]
    for part in sends:
        forward_pair += part.astype(F32)
    beyond = forward_pair[1].astype(BF16)
    inverse_total = jnp.sum(inverse_parts.astype(F32), axis=0)
    gathered, beyond, inverse_total = tie(gathered, beyond, inverse_total)
    base = relations // LANES * LANES
    window = -(-(2 * relations - base) // LANES) * LANES
    placed = place_rows(gathered, bases, window)
    coefficient_grads = finish(k.reshape(1), placed, from_row(placed, dk=1), base, relations).T
    forward_sum = forward_pair[0] + from_column(beyond, dx=1).astype(F32)
    layer_sum = jnp.dot(features, self_weight, preferred_element_type=F32)
    layer_sum += inverse_total + forward_sum
    return layer_sum.astype(BF16), coefficient_grads


def solution(mesh):
    return jax.shard_map(
        on_device,
        mesh=mesh,
        in_specs=(
            P(("prow", "pcol"), None),
            P(("prow", "pcol"), None),
            P(),
            P(),
            P(),
            P("prow", "pcol", None, None),
            P("prow", "pcol", None, None, None),
            P("prow", "pcol"),
        ),
        out_specs=(P(("prow", "pcol"), None), P()),
        check_vma=False,
    )
```

```python
import functools
import jax
import jax.numpy as jnp
from jax import lax
from jax.experimental import pallas as pl
from jax.experimental.pallas import tpu as pltpu
from jax.sharding import PartitionSpec as P

F32, BF16 = jnp.float32, jnp.bfloat16
VMEM = pl.BlockSpec(memory_space=pltpu.VMEM)
SMEM = pl.BlockSpec(memory_space=pltpu.SMEM)
ANY = pl.BlockSpec(memory_space=pl.ANY)
HBM = pl.BlockSpec(memory_space=pltpu.HBM)
LANES = 128
DIAGONAL = 16
PAYLOAD = 48


def params(mib):
    return pltpu.CompilerParams(vmem_limit_bytes=mib * 1024 * 1024)


def cost(flops, moved):
    return pl.CostEstimate(flops=flops, bytes_accessed=moved, transcendentals=0)


def split(wide):
    high = wide.astype(BF16)
    return high, (wide - high.astype(F32)).astype(BF16)


def iota(shape, dim):
    return lax.broadcasted_iota(jnp.int32, shape, dim)


def weights_kernel(parts, row_ref, coefficient_ref, basis_ref, weight_ref, spread, basis, weight, in_sems, out_sems):
    bases, named = coefficient_ref.shape
    sides = row_ref.shape[1]
    depth, width = basis.shape[1:]
    size = depth // parts
    tall, wide = sides * DIAGONAL, bases * DIAGONAL
    arrive, leave = [], []
    for part in range(parts):
        rows = pl.ds(part * size, size)
        arrive.append(pltpu.make_async_copy(basis_ref.at[:, rows, :], basis.at[:, rows, :], in_sems.at[part]))
        leave.append(pltpu.make_async_copy(weight.at[:, rows, :], weight_ref.at[:, rows, :], out_sems.at[part]))
    for copy in arrive:
        copy.start()
    chosen = (iota((named, sides), 0) == row_ref[...]).astype(F32).astype(BF16)
    rows = (iota((tall, sides), 0) // DIAGONAL == iota((tall, sides), 1)).astype(F32).astype(BF16)
    columns = (iota((bases, wide), 1) // DIAGONAL == iota((bases, wide), 0)).astype(F32).astype(BF16)
    same = iota((tall, wide), 0) % DIAGONAL == iota((tall, wide), 1) % DIAGONAL
    for index, part in enumerate(split(coefficient_ref[...])):
        picked = jnp.dot(part, chosen, preferred_element_type=F32).astype(BF16)
        tower = lax.dot_general(rows, picked, (((1,), (1,)), ((), ())), preferred_element_type=F32).astype(BF16)
        full = jnp.dot(tower, columns, preferred_element_type=F32)
        spread[index] = jnp.where(same, full, 0.0).astype(BF16)
    for start in range(0, depth, DIAGONAL):
        if start % size == 0:
            arrive[start // size].wait()
        part = basis[:, start : start + DIAGONAL, :].reshape(wide, width)
        total = jnp.dot(spread[0], part, preferred_element_type=F32)
        total += jnp.dot(spread[1], part, preferred_element_type=F32)
        weight[:, start : start + DIAGONAL, :] = total.astype(BF16).reshape(sides, DIAGONAL, width)
        if (start + DIAGONAL) % size == 0:
            leave[start // size].start()
    for copy in leave:
        copy.wait()


def relation_weights(rows_named, coefficients_t, basis, parts=4):
    bases, depth, width = basis.shape
    sides = rows_named.shape[1]
    return pl.pallas_call(
        functools.partial(weights_kernel, parts),
        out_shape=jax.ShapeDtypeStruct((sides, depth, width), BF16),
        in_specs=[VMEM, VMEM, HBM],
        out_specs=HBM,
        scratch_shapes=[
            pltpu.VMEM((2, sides * DIAGONAL, bases * DIAGONAL), BF16),
            pltpu.VMEM(basis.shape, BF16),
            pltpu.VMEM((sides, depth, width), BF16),
            pltpu.SemaphoreType.DMA((parts,)),
            pltpu.SemaphoreType.DMA((parts,)),
        ],
        compiler_params=params(56),
        cost_estimate=cost(4 * 10**9, 2 * basis.size * 2),
        name="relation_weights",
    )(rows_named, coefficients_t, basis)


def normalised(mask, rows, dim):
    over = (((dim,), (0,)), ((), ()))
    summed = lax.dot_general(mask, rows, over, preferred_element_type=F32)
    degree = lax.dot_general(mask, jnp.ones((mask.shape[dim], LANES), BF16), over, preferred_element_type=F32)
    scale = (1.0 / (1.0 + degree)).astype(BF16).astype(F32)
    return (summed * jnp.concatenate([scale] * (rows.shape[1] // LANES), axis=1)).astype(BF16)


def copies_into(target, refs, sems):
    copies, at = [], 0
    for index, ref in enumerate(refs):
        size = ref.shape[0]
        copies.append(pltpu.make_async_copy(ref, target.at[pl.ds(at, size)], sems.at[index]))
        at += size
    for copy in copies:
        copy.start()
    return copies


def block_at(index, size):
    return pl.ds(pl.multiple_of(index * size, size), size)


def inverse_kernel(pieces, entry_ref, live_ref, mask_ref, weights_ref, *refs):
    rows_ref, keep_ref, *send_refs, total, row, weight, row_sems, sem = refs[pieces:]
    tiles, block, _ = mask_ref.shape
    arrive = copies_into(row, refs[:pieces], row_sems)
    copy = pltpu.make_async_copy(weights_ref.at[pl.ds(tiles, tiles)], weight, sem)
    copy.start()
    total[...] = jnp.zeros_like(total)
    for part in arrive:
        part.wait()
    for tile in range(tiles):
        rows = row[entry_ref[2, tile]]
        rows_ref[tile] = normalised(mask_ref[tile].astype(F32).astype(BF16), rows, 0)
    copy.wait()
    for tile in range(tiles):
        weighting = (tile < live_ref[0, 0]).astype(F32)
        message = jnp.dot(rows_ref[tile], weight[tile], preferred_element_type=F32) * weighting
        total[block_at(entry_ref[4, tile], block), :] += message
    half = keep_ref.shape[0]
    keep_ref[...] = total[:half, :]
    for index, ref in enumerate(send_refs):
        start = half + index * ref.shape[0]
        ref[...] = total[start : start + ref.shape[0], :].astype(BF16)


def inverse_messages(entries, live, mask, row_pieces, weights, row_count):
    tiles, block, _ = mask.shape
    width = row_pieces[0].shape[2]
    half = row_count * block // 2
    columns = sum(piece.shape[0] for piece in row_pieces)
    return pl.pallas_call(
        functools.partial(inverse_kernel, len(row_pieces)),
        out_shape=(
            jax.ShapeDtypeStruct((tiles, block, width), BF16),
            jax.ShapeDtypeStruct((half, width), F32),
        )
        + (jax.ShapeDtypeStruct((half // 4, width), BF16),) * 4,
        in_specs=[SMEM, SMEM, VMEM, HBM] + [ANY] * len(row_pieces),
        out_specs=(VMEM,) * 6,
        scratch_shapes=[
            pltpu.VMEM((2 * half, width), F32),
            pltpu.VMEM((columns,) + row_pieces[0].shape[1:], BF16),
            pltpu.VMEM((tiles, width, width), BF16),
            pltpu.SemaphoreType.DMA((len(row_pieces),)),
            pltpu.SemaphoreType.DMA,
        ],
        compiler_params=params(52),
        cost_estimate=cost(0, 1000),
        name="inverse_messages",
    )(entries, live, mask, weights, *row_pieces)


def forward_kernel(entry_ref, live_ref, rows_ref, weights_ref, keep_ref, *refs):
    send_refs, (total, weight, sem) = refs[:-3], refs[-3:]
    tiles, block, _ = rows_ref.shape
    copy = pltpu.make_async_copy(weights_ref.at[pl.ds(0, tiles)], weight, sem)
    copy.start()
    total[...] = jnp.zeros_like(total)
    copy.wait()
    for tile in range(tiles):
        weighting = (tile < live_ref[0, 0]).astype(F32)
        message = jnp.dot(rows_ref[tile], weight[tile], preferred_element_type=F32) * weighting
        total[entry_ref[5, tile]] += message
    pair = keep_ref.shape[0]
    keep_ref[...] = total[:pair]
    for index, ref in enumerate(send_refs):
        ref[...] = total[pair * (index + 1) : pair * (index + 2)].astype(BF16)


def forward_messages(entries, live, rows, weights):
    tiles, block, width = rows.shape
    shape = (X_LO, block, width)
    return pl.pallas_call(
        forward_kernel,
        out_shape=(jax.ShapeDtypeStruct(shape, F32),) + (jax.ShapeDtypeStruct(shape, BF16),) * (Y - 1),
        in_specs=[SMEM, SMEM, VMEM, HBM],
        out_specs=(VMEM,) * Y,
        scratch_shapes=[
            pltpu.VMEM((Y * X_LO, block, width), F32),
            pltpu.VMEM((tiles, width, width), BF16),
            pltpu.SemaphoreType.DMA,
        ],
        compiler_params=params(56),
        cost_estimate=cost(10**9, 4 * 10**6),
        name="forward_messages",
    )(entries, live, rows, weights)


def gradient_kernel(pieces, row_pieces, entry_ref, live_ref, core_ref, mask_ref, inverse_ref, basis_ref, *refs):
    column_refs, row_refs, refs = refs[:pieces], refs[pieces : pieces + row_pieces], refs[pieces + row_pieces :]
    rows_ref, mine_ref, other_ref, column, row, basis, moments, total, column_sem, row_sem, basis_sem = refs
    tiles, block, _ = mask_ref.shape
    bases, depth, width = basis.shape
    sides = 2 * tiles
    copies = copies_into(column, column_refs, column_sem) + copies_into(row, row_refs, row_sem)
    basis_copy = pltpu.make_async_copy(basis_ref, basis, basis_sem)
    basis_copy.start()
    for copy in copies:
        copy.wait()
    for tile in range(tiles):
        rows = column[entry_ref[1, tile], :block, :]
        rows_ref[tile] = normalised(mask_ref[tile].astype(F32).astype(BF16), rows, 1)
    over = (((0,), (0,)), ((), ()))
    for tile in range(tiles):
        target = row[entry_ref[2, tile]]
        source = column[entry_ref[1, tile], block:, :]
        moments[tile] = lax.dot_general(rows_ref[tile], target, over, preferred_element_type=F32).astype(BF16)
        moments[tiles + tile] = lax.dot_general(
            inverse_ref[tile], source, over, preferred_element_type=F32
        ).astype(BF16)
    basis_copy.wait()
    tall, wide = bases * DIAGONAL, sides * DIAGONAL
    for start in range(0, depth, DIAGONAL):
        left = basis[:, start : start + DIAGONAL, :].reshape(tall, width)
        right = moments[:, start : start + DIAGONAL, :].reshape(wide, width)
        product = lax.dot_general(left, right, (((1,), (1,)), ((), ())), preferred_element_type=F32)
        if start == 0:
            total[...] = product
        else:
            total[...] += product
    same = iota((tall, wide), 0) % DIAGONAL == iota((tall, wide), 1) % DIAGONAL
    rows = (iota((bases, tall), 1) // DIAGONAL == iota((bases, tall), 0)).astype(BF16)
    columns = (iota((wide, sides), 0) // DIAGONAL == iota((wide, sides), 1)).astype(BF16)
    tower = jnp.zeros((bases, wide), F32)
    for part in split(jnp.where(same, total[...], 0.0)):
        tower += jnp.dot(rows, part, preferred_element_type=F32)
    per_tile = jnp.zeros((bases, sides), F32)
    for part in split(tower):
        per_tile += jnp.dot(part, columns, preferred_element_type=F32)
    live = live_ref[0, 0]
    per_tile = jnp.where(iota((bases, sides), 1) % tiles < live, per_tile, 0.0)
    first = core_ref[0] == 0
    forward, inverse = per_tile[:, :tiles], per_tile[:, tiles:]
    names = iota((PAYLOAD - bases, tiles), 0)
    lane = iota((PAYLOAD - bases, tiles), 1)
    for ref, chosen in ((mine_ref, first), (other_ref, jnp.logical_not(first))):
        ref[:bases, :] = jnp.where(chosen, forward, inverse).astype(BF16)
        named = jnp.zeros((PAYLOAD - bases, tiles), jnp.int32)
        for tile in range(tiles):
            name = entry_ref[0, tile] + jnp.where(chosen, 0, entry_ref[3, tile])
            digits = jnp.where(names == 0, name // LANES, jnp.where(names == 1, name % LANES, 0))
            named = jnp.where(lane == tile, digits, named)
        ref[bases:, :] = named.astype(F32).astype(BF16)


def gradients(entries, live, core, mask, row_pieces, inverse_rows, basis, columns):
    tiles, block, _ = mask.shape
    bases, depth, width = basis.shape
    payload = jax.ShapeDtypeStruct((PAYLOAD, tiles), BF16)

    def room(pieces):
        return pltpu.VMEM((sum(piece.shape[0] for piece in pieces),) + pieces[0].shape[1:], BF16)

    return pl.pallas_call(
        functools.partial(gradient_kernel, len(columns), len(row_pieces)),
        out_shape=(jax.ShapeDtypeStruct((tiles, block, width), BF16), payload, payload),
        in_specs=[SMEM, SMEM, SMEM, VMEM, VMEM, HBM] + [ANY] * (len(columns) + len(row_pieces)),
        out_specs=(VMEM, VMEM, VMEM),
        scratch_shapes=[
            room(columns),
            room(row_pieces),
            pltpu.VMEM(basis.shape, BF16),
            pltpu.VMEM((2 * tiles, depth, width), BF16),
            pltpu.VMEM((bases * DIAGONAL, 2 * tiles * DIAGONAL), F32),
            pltpu.SemaphoreType.DMA((len(columns),)),
            pltpu.SemaphoreType.DMA((len(row_pieces),)),
            pltpu.SemaphoreType.DMA,
        ],
        compiler_params=params(50),
        cost_estimate=cost(0, 1000),
        name="gradients",
    )(entries, live, core, mask, inverse_rows, basis, *columns, *row_pieces)


def place_kernel(entry_ref, out_ref, total):
    bases, window = out_ref.shape
    count, _, span = entry_ref.shape
    for index in range(count):
        values = entry_ref[index, :bases, :].astype(F32)
        names = entry_ref[index, bases:, :].astype(F32)
        high, low = names[:1], names[1:2]
        chosen = (iota((LANES, span), 0).astype(F32) == low).astype(F32).astype(BF16)
        spread = [jnp.where(high == part, values, 0.0).astype(BF16) for part in range(window // LANES)]
        product = lax.dot_general(
            jnp.concatenate(spread, axis=0), chosen, (((1,), (1,)), ((), ())), preferred_element_type=F32
        )
        if index == 0:
            total[...] = product
        else:
            total[...] += product
    for part in range(window // LANES):
        out_ref[:, part * LANES : part * LANES + LANES] = total[part * bases : part * bases + bases, :]


def place_rows(entries, bases, window):
    return pl.pallas_call(
        place_kernel,
        out_shape=jax.ShapeDtypeStruct((bases, window), F32),
        in_specs=[VMEM],
        out_specs=VMEM,
        scratch_shapes=[pltpu.VMEM((window // LANES * bases, LANES), F32)],
        compiler_params=params(16),
        cost_estimate=cost(10**9, 10**6),
        name="place_rows",
    )(entries)


def join_kernel(plan, count, *refs):
    sems = refs[-1]
    copies = []
    for output, pieces in enumerate(plan):
        at = 0
        for source, start, size in pieces:
            copies.append(
                pltpu.make_async_copy(
                    refs[source].at[pl.ds(start, size)],
                    refs[count + output].at[pl.ds(at, size)],
                    sems.at[len(copies)],
                )
            )
            at += size
    for copy in copies:
        copy.start()
    for copy in copies:
        copy.wait()


def join(sources, plan):
    shape = sources[0].shape[1:]
    sizes = [sum(size for _, _, size in pieces) for pieces in plan]
    return pl.pallas_call(
        functools.partial(join_kernel, plan, len(sources)),
        out_shape=tuple(jax.ShapeDtypeStruct((size,) + shape, sources[0].dtype) for size in sizes),
        in_specs=[ANY] * len(sources),
        out_specs=tuple(ANY for _ in plan),
        scratch_shapes=[pltpu.SemaphoreType.DMA((sum(len(pieces) for pieces in plan),))],
        compiler_params=params(4),
        cost_estimate=cost(0, 10**6),
        name="join",
    )(*sources)


def finish_kernel(base, core_ref, own_ref, partner_ref, out_ref):
    window = own_ref.shape[1]
    shared = window - base
    last = out_ref.shape[1]
    first = core_ref[0] == 0
    out_ref[:, :base] = jnp.where(first, own_ref[:, :base], partner_ref[:, :base])
    out_ref[:, base:window] = jnp.where(first, own_ref[:, base:], partner_ref[:, base:]) + jnp.where(
        first, partner_ref[:, :shared], own_ref[:, :shared]
    )
    out_ref[:, window:] = jnp.where(
        first, partner_ref[:, shared : last - base], own_ref[:, shared : last - base]
    )


def finish(core, own, partner, base, relations):
    return pl.pallas_call(
        functools.partial(finish_kernel, base),
        out_shape=jax.ShapeDtypeStruct((own.shape[0], 2 * relations), F32),
        in_specs=[SMEM, VMEM, VMEM],
        out_specs=VMEM,
        compiler_params=params(8),
        cost_estimate=cost(0, 10**6),
        name="finish",
    )(core, own, partner)


def pack_kernel(feature_ref, cotangent_ref, own_ref, sems):
    block = feature_ref.shape[0]
    copies = [
        pltpu.make_async_copy(ref, own_ref.at[0, pl.ds(index * block, block), :], sems.at[index])
        for index, ref in enumerate((feature_ref, cotangent_ref))
    ]
    for copy in copies:
        copy.start()
    for copy in copies:
        copy.wait()


def pack(features, cotangent):
    block, width = features.shape
    return pl.pallas_call(
        pack_kernel,
        out_shape=jax.ShapeDtypeStruct((1, 2 * block, width), BF16),
        in_specs=[HBM, HBM],
        out_specs=VMEM,
        scratch_shapes=[pltpu.SemaphoreType.DMA((2,))],
        compiler_params=params(60),
        cost_estimate=cost(0, 10**6),
        name="pack",
    )(features, cotangent)


X_HI, RING, CORES = 2, 8, 2
Y, X_LO = 4, 2


def from_row(array, dx=0, dz=0, dk=0):
    pairs = []
    for x in range(X_HI):
        for z in range(RING):
            for k in range(CORES):
                source = ((x ^ dx) * RING + (z + dz) % RING) * CORES + (k ^ dk)
                pairs.append((source, (x * RING + z) * CORES + k))
    return lax.ppermute(array, "prow", pairs)


def from_column(array, dy=0, dx=0):
    pairs = []
    for y in range(Y):
        for x in range(X_LO):
            pairs.append((((y + dy) % Y) * X_LO + (x ^ dx), y * X_LO + x))
    return lax.ppermute(array, "pcol", pairs)


def tie(*arrays):
    return lax.optimization_barrier(arrays)


def coordinates():
    row = lax.axis_index("prow")
    column = lax.axis_index("pcol")
    return row // (RING * CORES), (row // CORES) % RING, row % CORES, column // X_LO, column % X_LO


def column_position(source, x, z, k):
    dx = (source // (RING * CORES)) ^ x
    dz = ((source // CORES) % RING - z) % RING
    dk = (source % CORES) ^ k
    even = dx * 4 + ((dz + 2) % RING) // 2
    odd = 8 + 4 * (dz // 4) + 2 * dx + (dz % 4) // 2
    return dk * 16 + jnp.where(dz % 2 == 0, even, odd)


def ordered(first, own, other, dim):
    return jnp.concatenate([jnp.where(first, own, other), jnp.where(first, other, own)], axis=dim)


def row_groups(apart):
    return [
        [(x * RING + z) * CORES + k for x in range(X_HI) for z in range(first, RING, apart)]
        for first in range(apart)
        for k in range(CORES)
    ]


def gather_gradients(mine, arrived, held, place):
    _, _, k, y, x_lo = place
    entries = ordered(k == 0, mine, arrived, 1)
    entries = ordered(x_lo == 0, entries, from_column(entries, dx=1), 1)
    around = [entries] + [from_column(entries, dy=dy) for dy in range(1, Y)]
    entries = jnp.concatenate(
        [functools.reduce(lambda a, dy: jnp.where(y == (at - dy) % Y, around[dy], a), range(1, Y), around[0]) for at in range(Y)],
        axis=1,
    )
    copies = jnp.broadcast_to(entries[None], (X_HI * RING,) + entries.shape)
    copies, *held = tie(copies, *held)
    gathered = lax.all_to_all(copies, "prow", 0, 0, tiled=True, axis_index_groups=row_groups(1))
    return gathered, held


def on_device(features, cotangent, self_weight, basis_weights, coefficients, tile_list, tile_mask, live_tiles):
    block, width = features.shape
    relations = coefficients.shape[0] // 2
    bases = coefficients.shape[1]
    rows_count = X_HI * RING * CORES
    place = coordinates()
    x, z, k, y, x_lo = place
    mask = tile_mask[0, 0]
    relation, source, target = tile_list[0, 0, :, 0], tile_list[0, 0, :, 1], tile_list[0, 0, :, 2]
    apart = (source % CORES ^ k) * (X_HI * RING) + source // CORES
    near = (target // X_LO - y) % Y * X_LO + (target % X_LO ^ x_lo)
    shift = jnp.full_like(relation, relations % LANES)
    entries = jnp.stack([relation, column_position(source, x, z, k), target, shift, apart, near])
    rows_named = jnp.concatenate([relation, relation + relations])[None]

    own = pack(features, cotangent)
    ring = [from_row(own, dz=dz) for dz in (4, 2, 6)]
    copies = jnp.broadcast_to(features, (Y * X_LO,) + features.shape)
    row_features = lax.all_to_all(copies, "pcol", 0, 0, tiled=True)
    (even,) = join([ring[2], own, ring[1], ring[0]], (((0, 0, 1), (1, 0, 1), (2, 0, 1), (3, 0, 1)),))
    across = from_row(even, dx=1)
    even, rows_named = tie(even, rows_named)
    weights = relation_weights(rows_named, coefficients.T, basis_weights)
    across, weights, row_features = tie(across, weights, row_features)
    upward, downward = join([even, across], (((0, 1, 2), (1, 1, 2)), ((0, 0, 2), (1, 0, 2))))
    upward, downward, even, across = tie(upward, downward, even, across)
    cotangent, _ = tie(cotangent, upward)
    copies = jnp.broadcast_to(cotangent, (Y * X_LO,) + cotangent.shape)
    row_cotangent = lax.all_to_all(copies, "pcol", 0, 0, tiled=True)
    up, down = from_row(upward, dz=1), from_row(downward, dz=7)
    swapped = [from_row(even, dk=1), from_row(across, dk=1)]
    *swapped, weights = tie(*swapped, weights)
    up, down, row_cotangent = tie(up, down, row_cotangent)
    columns = [even, across, up, down, *swapped, from_row(up, dk=1), from_row(down, dk=1)]
    inverse_rows, keep, *sends = inverse_messages(
        entries, live_tiles, mask, [row_features], weights, rows_count
    )
    sends = [from_row(part, dk=1) for part in sends]
    inverse_part = (keep + jnp.concatenate(sends).astype(F32)).astype(BF16).reshape(X_HI * RING, block, width)
    *columns, inverse_part = tie(*columns, inverse_part)
    inverse_parts = lax.all_to_all(inverse_part, "prow", 0, 0, tiled=True, axis_index_groups=row_groups(1))
    forward_rows, mine, other = gradients(
        entries, live_tiles, k.reshape(1), mask, [row_cotangent], inverse_rows, basis_weights, columns
    )
    arrived, forward_rows = tie(from_row(other, dk=1), forward_rows)
    gathered, (forward_rows, inverse_parts) = gather_gradients(mine, arrived, (forward_rows, inverse_parts), place)
    forward_pair, *sends = forward_messages(entries, live_tiles, forward_rows, weights)
    sends = [from_column(part, dy=Y - dy) for dy, part in enumerate(sends, 1)]
    for part in sends:
        forward_pair += part.astype(F32)
    beyond = forward_pair[1].astype(BF16)
    inverse_total = jnp.sum(inverse_parts.astype(F32), axis=0)
    gathered, beyond, inverse_total = tie(gathered, beyond, inverse_total)
    base = relations // LANES * LANES
    window = -(-(2 * relations - base) // LANES) * LANES
    placed = place_rows(gathered, bases, window)
    coefficient_grads = finish(k.reshape(1), placed, from_row(placed, dk=1), base, relations).T
    forward_sum = forward_pair[0] + from_column(beyond, dx=1).astype(F32)
    layer_sum = jnp.dot(features, self_weight, preferred_element_type=F32)
    layer_sum += inverse_total + forward_sum
    return layer_sum.astype(BF16), coefficient_grads


def solution(mesh):
    return jax.shard_map(
        on_device,
        mesh=mesh,
        in_specs=(
            P(("prow", "pcol"), None),
            P(("prow", "pcol"), None),
            P(),
            P(),
            P(),
            P("prow", "pcol", None, None),
            P("prow", "pcol", None, None, None),
            P("prow", "pcol"),
        ),
        out_specs=(P(("prow", "pcol"), None), P()),
        check_vma=False,
    )
```

```python
import functools
import jax
import jax.numpy as jnp
from jax import lax
from jax.experimental import pallas as pl
from jax.experimental.pallas import tpu as pltpu
from jax.sharding import PartitionSpec as P

F32, BF16 = jnp.float32, jnp.bfloat16
VMEM = pl.BlockSpec(memory_space=pltpu.VMEM)
SMEM = pl.BlockSpec(memory_space=pltpu.SMEM)
ANY = pl.BlockSpec(memory_space=pl.ANY)
HBM = pl.BlockSpec(memory_space=pltpu.HBM)
LANES = 128
DIAGONAL = 16
PAYLOAD = 48


def params(mib):
    return pltpu.CompilerParams(vmem_limit_bytes=mib * 1024 * 1024)


def cost(flops, moved):
    return pl.CostEstimate(flops=flops, bytes_accessed=moved, transcendentals=0)


def split(wide):
    high = wide.astype(BF16)
    return high, (wide - high.astype(F32)).astype(BF16)


def iota(shape, dim):
    return lax.broadcasted_iota(jnp.int32, shape, dim)


def weights_kernel(parts, row_ref, coefficient_ref, basis_ref, weight_ref, spread, basis, weight, in_sems, out_sems):
    bases, named = coefficient_ref.shape
    sides = row_ref.shape[1]
    depth, width = basis.shape[1:]
    size = depth // parts
    tall, wide = sides * DIAGONAL, bases * DIAGONAL
    arrive, leave = [], []
    for part in range(parts):
        rows = pl.ds(part * size, size)
        arrive.append(pltpu.make_async_copy(basis_ref.at[:, rows, :], basis.at[:, rows, :], in_sems.at[part]))
        leave.append(pltpu.make_async_copy(weight.at[:, rows, :], weight_ref.at[:, rows, :], out_sems.at[part]))
    for copy in arrive:
        copy.start()
    chosen = (iota((named, sides), 0) == row_ref[...]).astype(F32).astype(BF16)
    rows = (iota((tall, sides), 0) // DIAGONAL == iota((tall, sides), 1)).astype(F32).astype(BF16)
    columns = (iota((bases, wide), 1) // DIAGONAL == iota((bases, wide), 0)).astype(F32).astype(BF16)
    same = iota((tall, wide), 0) % DIAGONAL == iota((tall, wide), 1) % DIAGONAL
    for index, part in enumerate(split(coefficient_ref[...])):
        picked = jnp.dot(part, chosen, preferred_element_type=F32).astype(BF16)
        tower = lax.dot_general(rows, picked, (((1,), (1,)), ((), ())), preferred_element_type=F32).astype(BF16)
        full = jnp.dot(tower, columns, preferred_element_type=F32)
        spread[index] = jnp.where(same, full, 0.0).astype(BF16)
    for start in range(0, depth, DIAGONAL):
        if start % size == 0:
            arrive[start // size].wait()
        part = basis[:, start : start + DIAGONAL, :].reshape(wide, width)
        total = jnp.dot(spread[0], part, preferred_element_type=F32)
        total += jnp.dot(spread[1], part, preferred_element_type=F32)
        weight[:, start : start + DIAGONAL, :] = total.astype(BF16).reshape(sides, DIAGONAL, width)
        if (start + DIAGONAL) % size == 0:
            leave[start // size].start()
    for copy in leave:
        copy.wait()


def relation_weights(rows_named, coefficients_t, basis, parts=4):
    bases, depth, width = basis.shape
    sides = rows_named.shape[1]
    return pl.pallas_call(
        functools.partial(weights_kernel, parts),
        out_shape=jax.ShapeDtypeStruct((sides, depth, width), BF16),
        in_specs=[VMEM, VMEM, HBM],
        out_specs=HBM,
        scratch_shapes=[
            pltpu.VMEM((2, sides * DIAGONAL, bases * DIAGONAL), BF16),
            pltpu.VMEM(basis.shape, BF16),
            pltpu.VMEM((sides, depth, width), BF16),
            pltpu.SemaphoreType.DMA((parts,)),
            pltpu.SemaphoreType.DMA((parts,)),
        ],
        compiler_params=params(56),
        cost_estimate=cost(4 * 10**9, 2 * basis.size * 2),
        name="relation_weights",
    )(rows_named, coefficients_t, basis)


def normalised(mask, rows, dim):
    over = (((dim,), (0,)), ((), ()))
    summed = lax.dot_general(mask, rows, over, preferred_element_type=F32)
    degree = lax.dot_general(mask, jnp.ones((mask.shape[dim], LANES), BF16), over, preferred_element_type=F32)
    scale = (1.0 / (1.0 + degree)).astype(BF16).astype(F32)
    return (summed * jnp.concatenate([scale] * (rows.shape[1] // LANES), axis=1)).astype(BF16)


def copies_into(target, refs, sems):
    copies, at = [], 0
    for index, ref in enumerate(refs):
        size = ref.shape[0]
        copies.append(pltpu.make_async_copy(ref, target.at[pl.ds(at, size)], sems.at[index]))
        at += size
    for copy in copies:
        copy.start()
    return copies


def block_at(index, size):
    return pl.ds(pl.multiple_of(index * size, size), size)


def inverse_kernel(pieces, entry_ref, live_ref, mask_ref, weights_ref, *refs):
    rows_ref, keep_ref, *send_refs, total, row, weight, row_sems, sem = refs[pieces:]
    tiles, block, _ = mask_ref.shape
    arrive = copies_into(row, refs[:pieces], row_sems)
    copy = pltpu.make_async_copy(weights_ref.at[pl.ds(tiles, tiles)], weight, sem)
    copy.start()
    total[...] = jnp.zeros_like(total)
    for part in arrive:
        part.wait()
    for tile in range(tiles):
        rows = row[entry_ref[2, tile]]
        rows_ref[tile] = normalised(mask_ref[tile].astype(F32).astype(BF16), rows, 0)
    copy.wait()
    for tile in range(tiles):
        weighting = (tile < live_ref[0, 0]).astype(F32)
        message = jnp.dot(rows_ref[tile], weight[tile], preferred_element_type=F32) * weighting
        total[block_at(entry_ref[4, tile], block), :] += message
    half = keep_ref.shape[0]
    keep_ref[...] = total[:half, :]
    for index, ref in enumerate(send_refs):
        start = half + index * ref.shape[0]
        ref[...] = total[start : start + ref.shape[0], :].astype(BF16)


def inverse_messages(entries, live, mask, row_pieces, weights, row_count):
    tiles, block, _ = mask.shape
    width = row_pieces[0].shape[2]
    half = row_count * block // 2
    columns = sum(piece.shape[0] for piece in row_pieces)
    return pl.pallas_call(
        functools.partial(inverse_kernel, len(row_pieces)),
        out_shape=(
            jax.ShapeDtypeStruct((tiles, block, width), BF16),
            jax.ShapeDtypeStruct((half, width), F32),
        )
        + (jax.ShapeDtypeStruct((half // 4, width), BF16),) * 4,
        in_specs=[SMEM, SMEM, VMEM, HBM] + [ANY] * len(row_pieces),
        out_specs=(VMEM,) * 6,
        scratch_shapes=[
            pltpu.VMEM((2 * half, width), F32),
            pltpu.VMEM((columns,) + row_pieces[0].shape[1:], BF16),
            pltpu.VMEM((tiles, width, width), BF16),
            pltpu.SemaphoreType.DMA((len(row_pieces),)),
            pltpu.SemaphoreType.DMA,
        ],
        compiler_params=params(52),
        cost_estimate=cost(0, 1000),
        name="inverse_messages",
    )(entries, live, mask, weights, *row_pieces)


def forward_kernel(entry_ref, live_ref, rows_ref, weights_ref, keep_ref, *refs):
    send_refs, (total, weight, sem) = refs[:-3], refs[-3:]
    tiles, block, _ = rows_ref.shape
    copy = pltpu.make_async_copy(weights_ref.at[pl.ds(0, tiles)], weight, sem)
    copy.start()
    total[...] = jnp.zeros_like(total)
    copy.wait()
    for tile in range(tiles):
        weighting = (tile < live_ref[0, 0]).astype(F32)
        message = jnp.dot(rows_ref[tile], weight[tile], preferred_element_type=F32) * weighting
        total[entry_ref[5, tile]] += message
    pair = keep_ref.shape[0]
    keep_ref[...] = total[:pair]
    for index, ref in enumerate(send_refs):
        ref[...] = total[pair * (index + 1) : pair * (index + 2)].astype(BF16)


def forward_messages(entries, live, rows, weights):
    tiles, block, width = rows.shape
    shape = (X_LO, block, width)
    return pl.pallas_call(
        forward_kernel,
        out_shape=(jax.ShapeDtypeStruct(shape, F32),) + (jax.ShapeDtypeStruct(shape, BF16),) * (Y - 1),
        in_specs=[SMEM, SMEM, VMEM, HBM],
        out_specs=(VMEM,) * Y,
        scratch_shapes=[
            pltpu.VMEM((Y * X_LO, block, width), F32),
            pltpu.VMEM((tiles, width, width), BF16),
            pltpu.SemaphoreType.DMA,
        ],
        compiler_params=params(56),
        cost_estimate=cost(10**9, 4 * 10**6),
        name="forward_messages",
    )(entries, live, rows, weights)


def gradient_kernel(pieces, row_pieces, entry_ref, live_ref, core_ref, mask_ref, inverse_ref, basis_ref, *refs):
    column_refs, row_refs, refs = refs[:pieces], refs[pieces : pieces + row_pieces], refs[pieces + row_pieces :]
    rows_ref, mine_ref, other_ref, column, row, basis, moments, total, column_sem, row_sem, basis_sem = refs
    tiles, block, _ = mask_ref.shape
    bases, depth, width = basis.shape
    sides = 2 * tiles
    copies = copies_into(column, column_refs, column_sem) + copies_into(row, row_refs, row_sem)
    basis_copy = pltpu.make_async_copy(basis_ref, basis, basis_sem)
    basis_copy.start()
    for copy in copies:
        copy.wait()
    for tile in range(tiles):
        rows = column[entry_ref[1, tile], :block, :]
        rows_ref[tile] = normalised(mask_ref[tile].astype(F32).astype(BF16), rows, 1)
    over = (((0,), (0,)), ((), ()))
    for tile in range(tiles):
        target = row[entry_ref[2, tile]]
        source = column[entry_ref[1, tile], block:, :]
        moments[tile] = lax.dot_general(rows_ref[tile], target, over, preferred_element_type=F32).astype(BF16)
        moments[tiles + tile] = lax.dot_general(
            inverse_ref[tile], source, over, preferred_element_type=F32
        ).astype(BF16)
    basis_copy.wait()
    tall, wide = bases * DIAGONAL, sides * DIAGONAL
    for start in range(0, depth, DIAGONAL):
        left = basis[:, start : start + DIAGONAL, :].reshape(tall, width)
        right = moments[:, start : start + DIAGONAL, :].reshape(wide, width)
        product = lax.dot_general(left, right, (((1,), (1,)), ((), ())), preferred_element_type=F32)
        if start == 0:
            total[...] = product
        else:
            total[...] += product
    same = iota((tall, wide), 0) % DIAGONAL == iota((tall, wide), 1) % DIAGONAL
    rows = (iota((bases, tall), 1) // DIAGONAL == iota((bases, tall), 0)).astype(BF16)
    columns = (iota((wide, sides), 0) // DIAGONAL == iota((wide, sides), 1)).astype(BF16)
    tower = jnp.zeros((bases, wide), F32)
    for part in split(jnp.where(same, total[...], 0.0)):
        tower += jnp.dot(rows, part, preferred_element_type=F32)
    per_tile = jnp.zeros((bases, sides), F32)
    for part in split(tower):
        per_tile += jnp.dot(part, columns, preferred_element_type=F32)
    live = live_ref[0, 0]
    per_tile = jnp.where(iota((bases, sides), 1) % tiles < live, per_tile, 0.0)
    first = core_ref[0] == 0
    forward, inverse = per_tile[:, :tiles], per_tile[:, tiles:]
    names = iota((PAYLOAD - bases, tiles), 0)
    lane = iota((PAYLOAD - bases, tiles), 1)
    for ref, chosen in ((mine_ref, first), (other_ref, jnp.logical_not(first))):
        ref[:bases, :] = jnp.where(chosen, forward, inverse).astype(BF16)
        named = jnp.zeros((PAYLOAD - bases, tiles), jnp.int32)
        for tile in range(tiles):
            name = entry_ref[0, tile] + jnp.where(chosen, 0, entry_ref[3, tile])
            digits = jnp.where(names == 0, name // LANES, jnp.where(names == 1, name % LANES, 0))
            named = jnp.where(lane == tile, digits, named)
        ref[bases:, :] = named.astype(F32).astype(BF16)


def gradients(entries, live, core, mask, row_pieces, inverse_rows, basis, columns):
    tiles, block, _ = mask.shape
    bases, depth, width = basis.shape
    payload = jax.ShapeDtypeStruct((PAYLOAD, tiles), BF16)

    def room(pieces):
        return pltpu.VMEM((sum(piece.shape[0] for piece in pieces),) + pieces[0].shape[1:], BF16)

    return pl.pallas_call(
        functools.partial(gradient_kernel, len(columns), len(row_pieces)),
        out_shape=(jax.ShapeDtypeStruct((tiles, block, width), BF16), payload, payload),
        in_specs=[SMEM, SMEM, SMEM, VMEM, VMEM, HBM] + [ANY] * (len(columns) + len(row_pieces)),
        out_specs=(VMEM, VMEM, VMEM),
        scratch_shapes=[
            room(columns),
            room(row_pieces),
            pltpu.VMEM(basis.shape, BF16),
            pltpu.VMEM((2 * tiles, depth, width), BF16),
            pltpu.VMEM((bases * DIAGONAL, 2 * tiles * DIAGONAL), F32),
            pltpu.SemaphoreType.DMA((len(columns),)),
            pltpu.SemaphoreType.DMA((len(row_pieces),)),
            pltpu.SemaphoreType.DMA,
        ],
        compiler_params=params(50),
        cost_estimate=cost(0, 1000),
        name="gradients",
    )(entries, live, core, mask, inverse_rows, basis, *columns, *row_pieces)


def place_kernel(entry_ref, out_ref, total):
    bases, window = out_ref.shape
    count, _, span = entry_ref.shape
    for index in range(count):
        values = entry_ref[index, :bases, :].astype(F32)
        names = entry_ref[index, bases:, :].astype(F32)
        high, low = names[:1], names[1:2]
        chosen = (iota((LANES, span), 0).astype(F32) == low).astype(F32).astype(BF16)
        spread = [jnp.where(high == part, values, 0.0).astype(BF16) for part in range(window // LANES)]
        product = lax.dot_general(
            jnp.concatenate(spread, axis=0), chosen, (((1,), (1,)), ((), ())), preferred_element_type=F32
        )
        if index == 0:
            total[...] = product
        else:
            total[...] += product
    for part in range(window // LANES):
        out_ref[:, part * LANES : part * LANES + LANES] = total[part * bases : part * bases + bases, :]


def place_rows(entries, bases, window):
    return pl.pallas_call(
        place_kernel,
        out_shape=jax.ShapeDtypeStruct((bases, window), F32),
        in_specs=[VMEM],
        out_specs=VMEM,
        scratch_shapes=[pltpu.VMEM((window // LANES * bases, LANES), F32)],
        compiler_params=params(16),
        cost_estimate=cost(10**9, 10**6),
        name="place_rows",
    )(entries)


def join_kernel(plan, count, *refs):
    sems = refs[-1]
    copies = []
    for output, pieces in enumerate(plan):
        at = 0
        for source, start, size in pieces:
            copies.append(
                pltpu.make_async_copy(
                    refs[source].at[pl.ds(start, size)],
                    refs[count + output].at[pl.ds(at, size)],
                    sems.at[len(copies)],
                )
            )
            at += size
    for copy in copies:
        copy.start()
    for copy in copies:
        copy.wait()


def join(sources, plan):
    shape = sources[0].shape[1:]
    sizes = [sum(size for _, _, size in pieces) for pieces in plan]
    return pl.pallas_call(
        functools.partial(join_kernel, plan, len(sources)),
        out_shape=tuple(jax.ShapeDtypeStruct((size,) + shape, sources[0].dtype) for size in sizes),
        in_specs=[ANY] * len(sources),
        out_specs=tuple(ANY for _ in plan),
        scratch_shapes=[pltpu.SemaphoreType.DMA((sum(len(pieces) for pieces in plan),))],
        compiler_params=params(4),
        cost_estimate=cost(0, 10**6),
        name="join",
    )(*sources)


def finish_kernel(base, core_ref, own_ref, partner_ref, out_ref):
    window = own_ref.shape[1]
    shared = window - base
    last = out_ref.shape[1]
    first = core_ref[0] == 0
    out_ref[:, :base] = jnp.where(first, own_ref[:, :base], partner_ref[:, :base])
    out_ref[:, base:window] = jnp.where(first, own_ref[:, base:], partner_ref[:, base:]) + jnp.where(
        first, partner_ref[:, :shared], own_ref[:, :shared]
    )
    out_ref[:, window:] = jnp.where(
        first, partner_ref[:, shared : last - base], own_ref[:, shared : last - base]
    )


def finish(core, own, partner, base, relations):
    return pl.pallas_call(
        functools.partial(finish_kernel, base),
        out_shape=jax.ShapeDtypeStruct((own.shape[0], 2 * relations), F32),
        in_specs=[SMEM, VMEM, VMEM],
        out_specs=VMEM,
        compiler_params=params(8),
        cost_estimate=cost(0, 10**6),
        name="finish",
    )(core, own, partner)


def pack_kernel(feature_ref, cotangent_ref, own_ref, sems):
    block = feature_ref.shape[0]
    copies = [
        pltpu.make_async_copy(ref, own_ref.at[0, pl.ds(index * block, block), :], sems.at[index])
        for index, ref in enumerate((feature_ref, cotangent_ref))
    ]
    for copy in copies:
        copy.start()
    for copy in copies:
        copy.wait()


def pack(features, cotangent):
    block, width = features.shape
    return pl.pallas_call(
        pack_kernel,
        out_shape=jax.ShapeDtypeStruct((1, 2 * block, width), BF16),
        in_specs=[HBM, HBM],
        out_specs=VMEM,
        scratch_shapes=[pltpu.SemaphoreType.DMA((2,))],
        compiler_params=params(60),
        cost_estimate=cost(0, 10**6),
        name="pack",
    )(features, cotangent)


X_HI, RING, CORES = 2, 8, 2
Y, X_LO = 4, 2


def from_row(array, dx=0, dz=0, dk=0):
    pairs = []
    for x in range(X_HI):
        for z in range(RING):
            for k in range(CORES):
                source = ((x ^ dx) * RING + (z + dz) % RING) * CORES + (k ^ dk)
                pairs.append((source, (x * RING + z) * CORES + k))
    return lax.ppermute(array, "prow", pairs)


def from_column(array, dy=0, dx=0):
    pairs = []
    for y in range(Y):
        for x in range(X_LO):
            pairs.append((((y + dy) % Y) * X_LO + (x ^ dx), y * X_LO + x))
    return lax.ppermute(array, "pcol", pairs)


def tie(*arrays):
    return lax.optimization_barrier(arrays)


def coordinates():
    row = lax.axis_index("prow")
    column = lax.axis_index("pcol")
    return row // (RING * CORES), (row // CORES) % RING, row % CORES, column // X_LO, column % X_LO


def column_position(source, x, z, k):
    dx = (source // (RING * CORES)) ^ x
    dz = ((source // CORES) % RING - z) % RING
    dk = (source % CORES) ^ k
    even = dx * 4 + ((dz + 2) % RING) // 2
    odd = 8 + 4 * (dz // 4) + 2 * dx + (dz % 4) // 2
    return dk * 16 + jnp.where(dz % 2 == 0, even, odd)


def ordered(first, own, other, dim):
    return jnp.concatenate([jnp.where(first, own, other), jnp.where(first, other, own)], axis=dim)


def row_groups(apart):
    return [
        [(x * RING + z) * CORES + k for x in range(X_HI) for z in range(first, RING, apart)]
        for first in range(apart)
        for k in range(CORES)
    ]


def gather_gradients(mine, arrived, held, place):
    _, _, k, y, x_lo = place
    entries = ordered(k == 0, mine, arrived, 1)
    entries = ordered(x_lo == 0, entries, from_column(entries, dx=1), 1)
    around = [entries] + [from_column(entries, dy=dy) for dy in range(1, Y)]
    entries = jnp.concatenate(
        [functools.reduce(lambda a, dy: jnp.where(y == (at - dy) % Y, around[dy], a), range(1, Y), around[0]) for at in range(Y)],
        axis=1,
    )
    copies = jnp.broadcast_to(entries[None], (X_HI * RING,) + entries.shape)
    copies, *held = tie(copies, *held)
    gathered = lax.all_to_all(copies, "prow", 0, 0, tiled=True, axis_index_groups=row_groups(1))
    return gathered, held


def on_device(features, cotangent, self_weight, basis_weights, coefficients, tile_list, tile_mask, live_tiles):
    block, width = features.shape
    relations = coefficients.shape[0] // 2
    bases = coefficients.shape[1]
    rows_count = X_HI * RING * CORES
    place = coordinates()
    x, z, k, y, x_lo = place
    mask = tile_mask[0, 0]
    relation, source, target = tile_list[0, 0, :, 0], tile_list[0, 0, :, 1], tile_list[0, 0, :, 2]
    apart = (source % CORES ^ k) * (X_HI * RING) + source // CORES
    near = (target // X_LO - y) % Y * X_LO + (target % X_LO ^ x_lo)
    shift = jnp.full_like(relation, relations % LANES)
    entries = jnp.stack([relation, column_position(source, x, z, k), target, shift, apart, near])
    rows_named = jnp.concatenate([relation, relation + relations])[None]

    own = pack(features, cotangent)
    ring = [from_row(own, dz=dz) for dz in (4, 2, 6)]
    copies = jnp.broadcast_to(features, (Y * X_LO,) + features.shape)
    row_features = lax.all_to_all(copies, "pcol", 0, 0, tiled=True)
    (even,) = join([ring[2], own, ring[1], ring[0]], (((0, 0, 1), (1, 0, 1), (2, 0, 1), (3, 0, 1)),))
    across = from_row(even, dx=1)
    even, rows_named = tie(even, rows_named)
    weights = relation_weights(rows_named, coefficients.T, basis_weights)
    across, weights, row_features = tie(across, weights, row_features)
    upward, downward = join([even, across], (((0, 1, 2), (1, 1, 2)), ((0, 0, 2), (1, 0, 2))))
    upward, downward, even, across = tie(upward, downward, even, across)
    cotangent, _ = tie(cotangent, upward)
    copies = jnp.broadcast_to(cotangent, (Y * X_LO,) + cotangent.shape)
    row_cotangent = lax.all_to_all(copies, "pcol", 0, 0, tiled=True)
    up, down = from_row(upward, dz=1), from_row(downward, dz=7)
    swapped = [from_row(even, dk=1), from_row(across, dk=1)]
    *swapped, weights = tie(*swapped, weights)
    up, down, row_cotangent = tie(up, down, row_cotangent)
    columns = [even, across, up, down, *swapped, from_row(up, dk=1), from_row(down, dk=1)]
    inverse_rows, keep, *sends = inverse_messages(
        entries, live_tiles, mask, [row_features], weights, rows_count
    )
    sends = [from_row(part, dk=1) for part in sends]
    inverse_part = (keep + jnp.concatenate(sends).astype(F32)).astype(BF16).reshape(X_HI * RING, block, width)
    *columns, inverse_part = tie(*columns, inverse_part)
    inverse_parts = lax.all_to_all(inverse_part, "prow", 0, 0, tiled=True, axis_index_groups=row_groups(1))
    forward_rows, mine, other = gradients(
        entries, live_tiles, k.reshape(1), mask, [row_cotangent], inverse_rows, basis_weights, columns
    )
    arrived, forward_rows = tie(from_row(other, dk=1), forward_rows)
    held = forward_messages(entries, live_tiles, forward_rows, weights)
    gathered, (forward_pair, *sends, inverse_parts) = gather_gradients(mine, arrived, (*held, inverse_parts), place)
    sends = [from_column(part, dy=Y - dy) for dy, part in enumerate(sends, 1)]
    for part in sends:
        forward_pair += part.astype(F32)
    beyond = forward_pair[1].astype(BF16)
    inverse_total = jnp.sum(inverse_parts.astype(F32), axis=0)
    gathered, beyond, inverse_total = tie(gathered, beyond, inverse_total)
    base = relations // LANES * LANES
    window = -(-(2 * relations - base) // LANES) * LANES
    placed = place_rows(gathered, bases, window)
    coefficient_grads = finish(k.reshape(1), placed, from_row(placed, dk=1), base, relations).T
    forward_sum = forward_pair[0] + from_column(beyond, dx=1).astype(F32)
    layer_sum = jnp.dot(features, self_weight, preferred_element_type=F32)
    layer_sum += inverse_total + forward_sum
    return layer_sum.astype(BF16), coefficient_grads


def solution(mesh):
    return jax.shard_map(
        on_device,
        mesh=mesh,
        in_specs=(
            P(("prow", "pcol"), None),
            P(("prow", "pcol"), None),
            P(),
            P(),
            P(),
            P("prow", "pcol", None, None),
            P("prow", "pcol", None, None, None),
            P("prow", "pcol"),
        ),
        out_specs=(P(("prow", "pcol"), None), P()),
        check_vma=False,
    )
```

```python
import functools
import jax
import jax.numpy as jnp
from jax import lax
from jax.experimental import pallas as pl
from jax.experimental.pallas import tpu as pltpu
from jax.sharding import PartitionSpec as P

F32, BF16 = jnp.float32, jnp.bfloat16
VMEM = pl.BlockSpec(memory_space=pltpu.VMEM)
SMEM = pl.BlockSpec(memory_space=pltpu.SMEM)
ANY = pl.BlockSpec(memory_space=pl.ANY)
HBM = pl.BlockSpec(memory_space=pltpu.HBM)
LANES = 128
DIAGONAL = 16
PAYLOAD = 48


def params(mib):
    return pltpu.CompilerParams(vmem_limit_bytes=mib * 1024 * 1024)


def cost(flops, moved):
    return pl.CostEstimate(flops=flops, bytes_accessed=moved, transcendentals=0)


def split(wide):
    high = wide.astype(BF16)
    return high, (wide - high.astype(F32)).astype(BF16)


def iota(shape, dim):
    return lax.broadcasted_iota(jnp.int32, shape, dim)


def weights_kernel(parts, row_ref, coefficient_ref, basis_ref, weight_ref, spread, basis, weight, in_sems, out_sems):
    bases, named = coefficient_ref.shape
    sides = row_ref.shape[1]
    depth, width = basis.shape[1:]
    size = depth // parts
    tall, wide = sides * DIAGONAL, bases * DIAGONAL
    arrive, leave = [], []
    for part in range(parts):
        rows = pl.ds(part * size, size)
        arrive.append(pltpu.make_async_copy(basis_ref.at[:, rows, :], basis.at[:, rows, :], in_sems.at[part]))
        leave.append(pltpu.make_async_copy(weight.at[:, rows, :], weight_ref.at[:, rows, :], out_sems.at[part]))
    for copy in arrive:
        copy.start()
    chosen = (iota((named, sides), 0) == row_ref[...]).astype(F32).astype(BF16)
    rows = (iota((tall, sides), 0) // DIAGONAL == iota((tall, sides), 1)).astype(F32).astype(BF16)
    columns = (iota((bases, wide), 1) // DIAGONAL == iota((bases, wide), 0)).astype(F32).astype(BF16)
    same = iota((tall, wide), 0) % DIAGONAL == iota((tall, wide), 1) % DIAGONAL
    for index, part in enumerate(split(coefficient_ref[...])):
        picked = jnp.dot(part, chosen, preferred_element_type=F32).astype(BF16)
        tower = lax.dot_general(rows, picked, (((1,), (1,)), ((), ())), preferred_element_type=F32).astype(BF16)
        full = jnp.dot(tower, columns, preferred_element_type=F32)
        spread[index] = jnp.where(same, full, 0.0).astype(BF16)
    for start in range(0, depth, DIAGONAL):
        if start % size == 0:
            arrive[start // size].wait()
        part = basis[:, start : start + DIAGONAL, :].reshape(wide, width)
        total = jnp.dot(spread[0], part, preferred_element_type=F32)
        total += jnp.dot(spread[1], part, preferred_element_type=F32)
        weight[:, start : start + DIAGONAL, :] = total.astype(BF16).reshape(sides, DIAGONAL, width)
        if (start + DIAGONAL) % size == 0:
            leave[start // size].start()
    for copy in leave:
        copy.wait()


def relation_weights(rows_named, coefficients_t, basis, parts=4):
    bases, depth, width = basis.shape
    sides = rows_named.shape[1]
    return pl.pallas_call(
        functools.partial(weights_kernel, parts),
        out_shape=jax.ShapeDtypeStruct((sides, depth, width), BF16),
        in_specs=[VMEM, VMEM, HBM],
        out_specs=HBM,
        scratch_shapes=[
            pltpu.VMEM((2, sides * DIAGONAL, bases * DIAGONAL), BF16),
            pltpu.VMEM(basis.shape, BF16),
            pltpu.VMEM((sides, depth, width), BF16),
            pltpu.SemaphoreType.DMA((parts,)),
            pltpu.SemaphoreType.DMA((parts,)),
        ],
        compiler_params=params(56),
        cost_estimate=cost(4 * 10**9, 2 * basis.size * 2),
        name="relation_weights",
    )(rows_named, coefficients_t, basis)


def normalised(mask, rows, dim):
    over = (((dim,), (0,)), ((), ()))
    summed = lax.dot_general(mask, rows, over, preferred_element_type=F32)
    degree = lax.dot_general(mask, jnp.ones((mask.shape[dim], LANES), BF16), over, preferred_element_type=F32)
    scale = (1.0 / (1.0 + degree)).astype(BF16).astype(F32)
    return (summed * jnp.concatenate([scale] * (rows.shape[1] // LANES), axis=1)).astype(BF16)


def copies_into(target, refs, sems):
    copies, at = [], 0
    for index, ref in enumerate(refs):
        size = ref.shape[0]
        copies.append(pltpu.make_async_copy(ref, target.at[pl.ds(at, size)], sems.at[index]))
        at += size
    for copy in copies:
        copy.start()
    return copies


def block_at(index, size):
    return pl.ds(pl.multiple_of(index * size, size), size)


def inverse_kernel(pieces, entry_ref, live_ref, mask_ref, weights_ref, *refs):
    rows_ref, keep_ref, *send_refs, total, row, weight, row_sems, sem = refs[pieces:]
    tiles, block, _ = mask_ref.shape
    arrive = copies_into(row, refs[:pieces], row_sems)
    copy = pltpu.make_async_copy(weights_ref.at[pl.ds(tiles, tiles)], weight, sem)
    copy.start()
    total[...] = jnp.zeros_like(total)
    for part in arrive:
        part.wait()
    for tile in range(tiles):
        rows = row[entry_ref[2, tile]]
        rows_ref[tile] = normalised(mask_ref[tile].astype(F32).astype(BF16), rows, 0)
    copy.wait()
    for tile in range(tiles):
        weighting = (tile < live_ref[0, 0]).astype(F32)
        message = jnp.dot(rows_ref[tile], weight[tile], preferred_element_type=F32) * weighting
        total[block_at(entry_ref[4, tile], block), :] += message
    half = keep_ref.shape[0]
    keep_ref[...] = total[:half, :]
    for index, ref in enumerate(send_refs):
        start = half + index * ref.shape[0]
        ref[...] = total[start : start + ref.shape[0], :].astype(BF16)


def inverse_messages(entries, live, mask, row_pieces, weights, row_count):
    tiles, block, _ = mask.shape
    width = row_pieces[0].shape[2]
    half = row_count * block // 2
    columns = sum(piece.shape[0] for piece in row_pieces)
    return pl.pallas_call(
        functools.partial(inverse_kernel, len(row_pieces)),
        out_shape=(
            jax.ShapeDtypeStruct((tiles, block, width), BF16),
            jax.ShapeDtypeStruct((half, width), F32),
        )
        + (jax.ShapeDtypeStruct((half // 4, width), BF16),) * 4,
        in_specs=[SMEM, SMEM, VMEM, HBM] + [ANY] * len(row_pieces),
        out_specs=(VMEM,) * 6,
        scratch_shapes=[
            pltpu.VMEM((2 * half, width), F32),
            pltpu.VMEM((columns,) + row_pieces[0].shape[1:], BF16),
            pltpu.VMEM((tiles, width, width), BF16),
            pltpu.SemaphoreType.DMA((len(row_pieces),)),
            pltpu.SemaphoreType.DMA,
        ],
        compiler_params=params(52),
        cost_estimate=cost(0, 1000),
        name="inverse_messages",
    )(entries, live, mask, weights, *row_pieces)


def forward_kernel(entry_ref, live_ref, rows_ref, weights_ref, keep_ref, *refs):
    send_refs, (total, weight, sem) = refs[:-3], refs[-3:]
    tiles, block, _ = rows_ref.shape
    copy = pltpu.make_async_copy(weights_ref.at[pl.ds(0, tiles)], weight, sem)
    copy.start()
    total[...] = jnp.zeros_like(total)
    copy.wait()
    for tile in range(tiles):
        weighting = (tile < live_ref[0, 0]).astype(F32)
        message = jnp.dot(rows_ref[tile], weight[tile], preferred_element_type=F32) * weighting
        total[entry_ref[5, tile]] += message
    pair = keep_ref.shape[0]
    keep_ref[...] = total[:pair]
    for index, ref in enumerate(send_refs):
        ref[...] = total[pair * (index + 1) : pair * (index + 2)].astype(BF16)


def forward_messages(entries, live, rows, weights):
    tiles, block, width = rows.shape
    shape = (X_LO, block, width)
    return pl.pallas_call(
        forward_kernel,
        out_shape=(jax.ShapeDtypeStruct(shape, F32),) + (jax.ShapeDtypeStruct(shape, BF16),) * (Y - 1),
        in_specs=[SMEM, SMEM, VMEM, HBM],
        out_specs=(VMEM,) * Y,
        scratch_shapes=[
            pltpu.VMEM((Y * X_LO, block, width), F32),
            pltpu.VMEM((tiles, width, width), BF16),
            pltpu.SemaphoreType.DMA,
        ],
        compiler_params=params(56),
        cost_estimate=cost(10**9, 4 * 10**6),
        name="forward_messages",
    )(entries, live, rows, weights)


def gradient_kernel(pieces, row_pieces, entry_ref, live_ref, core_ref, mask_ref, inverse_ref, basis_ref, *refs):
    column_refs, row_refs, refs = refs[:pieces], refs[pieces : pieces + row_pieces], refs[pieces + row_pieces :]
    rows_ref, mine_ref, other_ref, column, row, basis, moments, total, column_sem, row_sem, basis_sem = refs
    tiles, block, _ = mask_ref.shape
    bases, depth, width = basis.shape
    sides = 2 * tiles
    copies = copies_into(column, column_refs, column_sem) + copies_into(row, row_refs, row_sem)
    basis_copy = pltpu.make_async_copy(basis_ref, basis, basis_sem)
    basis_copy.start()
    for copy in copies:
        copy.wait()
    for tile in range(tiles):
        rows = column[entry_ref[1, tile], :block, :]
        rows_ref[tile] = normalised(mask_ref[tile].astype(F32).astype(BF16), rows, 1)
    over = (((0,), (0,)), ((), ()))
    for tile in range(tiles):
        target = row[entry_ref[2, tile]]
        source = column[entry_ref[1, tile], block:, :]
        moments[tile] = lax.dot_general(rows_ref[tile], target, over, preferred_element_type=F32).astype(BF16)
        moments[tiles + tile] = lax.dot_general(
            inverse_ref[tile], source, over, preferred_element_type=F32
        ).astype(BF16)
    basis_copy.wait()
    tall, wide = bases * DIAGONAL, sides * DIAGONAL
    for start in range(0, depth, DIAGONAL):
        left = basis[:, start : start + DIAGONAL, :].reshape(tall, width)
        right = moments[:, start : start + DIAGONAL, :].reshape(wide, width)
        product = lax.dot_general(left, right, (((1,), (1,)), ((), ())), preferred_element_type=F32)
        if start == 0:
            total[...] = product
        else:
            total[...] += product
    same = iota((tall, wide), 0) % DIAGONAL == iota((tall, wide), 1) % DIAGONAL
    rows = (iota((bases, tall), 1) // DIAGONAL == iota((bases, tall), 0)).astype(BF16)
    columns = (iota((wide, sides), 0) // DIAGONAL == iota((wide, sides), 1)).astype(BF16)
    tower = jnp.zeros((bases, wide), F32)
    for part in split(jnp.where(same, total[...], 0.0)):
        tower += jnp.dot(rows, part, preferred_element_type=F32)
    per_tile = jnp.zeros((bases, sides), F32)
    for part in split(tower):
        per_tile += jnp.dot(part, columns, preferred_element_type=F32)
    live = live_ref[0, 0]
    per_tile = jnp.where(iota((bases, sides), 1) % tiles < live, per_tile, 0.0)
    first = core_ref[0] == 0
    forward, inverse = per_tile[:, :tiles], per_tile[:, tiles:]
    names = iota((PAYLOAD - bases, tiles), 0)
    lane = iota((PAYLOAD - bases, tiles), 1)
    for ref, chosen in ((mine_ref, first), (other_ref, jnp.logical_not(first))):
        ref[:bases, :] = jnp.where(chosen, forward, inverse).astype(BF16)
        named = jnp.zeros((PAYLOAD - bases, tiles), jnp.int32)
        for tile in range(tiles):
            name = entry_ref[0, tile] + jnp.where(chosen, 0, entry_ref[3, tile])
            digits = jnp.where(names == 0, name // LANES, jnp.where(names == 1, name % LANES, 0))
            named = jnp.where(lane == tile, digits, named)
        ref[bases:, :] = named.astype(F32).astype(BF16)


def gradients(entries, live, core, mask, row_pieces, inverse_rows, basis, columns):
    tiles, block, _ = mask.shape
    bases, depth, width = basis.shape
    payload = jax.ShapeDtypeStruct((PAYLOAD, tiles), BF16)

    def room(pieces):
        return pltpu.VMEM((sum(piece.shape[0] for piece in pieces),) + pieces[0].shape[1:], BF16)

    return pl.pallas_call(
        functools.partial(gradient_kernel, len(columns), len(row_pieces)),
        out_shape=(jax.ShapeDtypeStruct((tiles, block, width), BF16), payload, payload),
        in_specs=[SMEM, SMEM, SMEM, VMEM, VMEM, HBM] + [ANY] * (len(columns) + len(row_pieces)),
        out_specs=(VMEM, VMEM, VMEM),
        scratch_shapes=[
            room(columns),
            room(row_pieces),
            pltpu.VMEM(basis.shape, BF16),
            pltpu.VMEM((2 * tiles, depth, width), BF16),
            pltpu.VMEM((bases * DIAGONAL, 2 * tiles * DIAGONAL), F32),
            pltpu.SemaphoreType.DMA((len(columns),)),
            pltpu.SemaphoreType.DMA((len(row_pieces),)),
            pltpu.SemaphoreType.DMA,
        ],
        compiler_params=params(54),
        cost_estimate=cost(0, 1000),
        name="gradients",
    )(entries, live, core, mask, inverse_rows, basis, *columns, *row_pieces)


def place_kernel(entry_ref, out_ref, total):
    bases, window = out_ref.shape
    count, _, span = entry_ref.shape
    for index in range(count):
        values = entry_ref[index, :bases, :].astype(F32)
        names = entry_ref[index, bases:, :].astype(F32)
        high, low = names[:1], names[1:2]
        chosen = (iota((LANES, span), 0).astype(F32) == low).astype(F32).astype(BF16)
        spread = [jnp.where(high == part, values, 0.0).astype(BF16) for part in range(window // LANES)]
        product = lax.dot_general(
            jnp.concatenate(spread, axis=0), chosen, (((1,), (1,)), ((), ())), preferred_element_type=F32
        )
        if index == 0:
            total[...] = product
        else:
            total[...] += product
    for part in range(window // LANES):
        out_ref[:, part * LANES : part * LANES + LANES] = total[part * bases : part * bases + bases, :]


def place_rows(entries, bases, window):
    return pl.pallas_call(
        place_kernel,
        out_shape=jax.ShapeDtypeStruct((bases, window), F32),
        in_specs=[VMEM],
        out_specs=VMEM,
        scratch_shapes=[pltpu.VMEM((window // LANES * bases, LANES), F32)],
        compiler_params=params(16),
        cost_estimate=cost(10**9, 10**6),
        name="place_rows",
    )(entries)


def join_kernel(plan, count, *refs):
    sems = refs[-1]
    copies = []
    for output, pieces in enumerate(plan):
        at = 0
        for source, start, size in pieces:
            copies.append(
                pltpu.make_async_copy(
                    refs[source].at[pl.ds(start, size)],
                    refs[count + output].at[pl.ds(at, size)],
                    sems.at[len(copies)],
                )
            )
            at += size
    for copy in copies:
        copy.start()
    for copy in copies:
        copy.wait()


def join(sources, plan):
    shape = sources[0].shape[1:]
    sizes = [sum(size for _, _, size in pieces) for pieces in plan]
    return pl.pallas_call(
        functools.partial(join_kernel, plan, len(sources)),
        out_shape=tuple(jax.ShapeDtypeStruct((size,) + shape, sources[0].dtype) for size in sizes),
        in_specs=[ANY] * len(sources),
        out_specs=tuple(ANY for _ in plan),
        scratch_shapes=[pltpu.SemaphoreType.DMA((sum(len(pieces) for pieces in plan),))],
        compiler_params=params(4),
        cost_estimate=cost(0, 10**6),
        name="join",
    )(*sources)


def finish_kernel(base, core_ref, own_ref, partner_ref, out_ref):
    window = own_ref.shape[1]
    shared = window - base
    last = out_ref.shape[1]
    first = core_ref[0] == 0
    out_ref[:, :base] = jnp.where(first, own_ref[:, :base], partner_ref[:, :base])
    out_ref[:, base:window] = jnp.where(first, own_ref[:, base:], partner_ref[:, base:]) + jnp.where(
        first, partner_ref[:, :shared], own_ref[:, :shared]
    )
    out_ref[:, window:] = jnp.where(
        first, partner_ref[:, shared : last - base], own_ref[:, shared : last - base]
    )


def finish(core, own, partner, base, relations):
    return pl.pallas_call(
        functools.partial(finish_kernel, base),
        out_shape=jax.ShapeDtypeStruct((own.shape[0], 2 * relations), F32),
        in_specs=[SMEM, VMEM, VMEM],
        out_specs=VMEM,
        compiler_params=params(8),
        cost_estimate=cost(0, 10**6),
        name="finish",
    )(core, own, partner)


def pack_kernel(feature_ref, cotangent_ref, own_ref, sems):
    block = feature_ref.shape[0]
    copies = [
        pltpu.make_async_copy(ref, own_ref.at[0, pl.ds(index * block, block), :], sems.at[index])
        for index, ref in enumerate((feature_ref, cotangent_ref))
    ]
    for copy in copies:
        copy.start()
    for copy in copies:
        copy.wait()


def pack(features, cotangent):
    block, width = features.shape
    return pl.pallas_call(
        pack_kernel,
        out_shape=jax.ShapeDtypeStruct((1, 2 * block, width), BF16),
        in_specs=[HBM, HBM],
        out_specs=VMEM,
        scratch_shapes=[pltpu.SemaphoreType.DMA((2,))],
        compiler_params=params(60),
        cost_estimate=cost(0, 10**6),
        name="pack",
    )(features, cotangent)


X_HI, RING, CORES = 2, 8, 2
Y, X_LO = 4, 2


def from_row(array, dx=0, dz=0, dk=0):
    pairs = []
    for x in range(X_HI):
        for z in range(RING):
            for k in range(CORES):
                source = ((x ^ dx) * RING + (z + dz) % RING) * CORES + (k ^ dk)
                pairs.append((source, (x * RING + z) * CORES + k))
    return lax.ppermute(array, "prow", pairs)


def from_column(array, dy=0, dx=0):
    pairs = []
    for y in range(Y):
        for x in range(X_LO):
            pairs.append((((y + dy) % Y) * X_LO + (x ^ dx), y * X_LO + x))
    return lax.ppermute(array, "pcol", pairs)


def tie(*arrays):
    return lax.optimization_barrier(arrays)


def coordinates():
    row = lax.axis_index("prow")
    column = lax.axis_index("pcol")
    return row // (RING * CORES), (row // CORES) % RING, row % CORES, column // X_LO, column % X_LO


def column_position(source, x, z, k):
    dx = (source // (RING * CORES)) ^ x
    dz = ((source // CORES) % RING - z) % RING
    dk = (source % CORES) ^ k
    even = dx * 4 + ((dz + 2) % RING) // 2
    odd = 8 + 4 * (dz // 4) + 2 * dx + (dz % 4) // 2
    return dk * 16 + jnp.where(dz % 2 == 0, even, odd)


def ordered(first, own, other, dim):
    return jnp.concatenate([jnp.where(first, own, other), jnp.where(first, other, own)], axis=dim)


def row_groups(apart):
    return [
        [(x * RING + z) * CORES + k for x in range(X_HI) for z in range(first, RING, apart)]
        for first in range(apart)
        for k in range(CORES)
    ]


def gather_gradients(mine, arrived, held, place):
    _, _, k, y, x_lo = place
    entries = ordered(k == 0, mine, arrived, 1)
    entries = ordered(x_lo == 0, entries, from_column(entries, dx=1), 1)
    around = [entries] + [from_column(entries, dy=dy) for dy in range(1, Y)]
    entries = jnp.concatenate(
        [functools.reduce(lambda a, dy: jnp.where(y == (at - dy) % Y, around[dy], a), range(1, Y), around[0]) for at in range(Y)],
        axis=1,
    )
    copies = jnp.broadcast_to(entries[None], (X_HI * RING,) + entries.shape)
    copies, *held = tie(copies, *held)
    gathered = lax.all_to_all(copies, "prow", 0, 0, tiled=True, axis_index_groups=row_groups(1))
    return gathered, held


def on_device(features, cotangent, self_weight, basis_weights, coefficients, tile_list, tile_mask, live_tiles):
    block, width = features.shape
    relations = coefficients.shape[0] // 2
    bases = coefficients.shape[1]
    rows_count = X_HI * RING * CORES
    place = coordinates()
    x, z, k, y, x_lo = place
    mask = tile_mask[0, 0]
    relation, source, target = tile_list[0, 0, :, 0], tile_list[0, 0, :, 1], tile_list[0, 0, :, 2]
    apart = (source % CORES ^ k) * (X_HI * RING) + source // CORES
    near = (target // X_LO - y) % Y * X_LO + (target % X_LO ^ x_lo)
    shift = jnp.full_like(relation, relations % LANES)
    entries = jnp.stack([relation, column_position(source, x, z, k), target, shift, apart, near])
    rows_named = jnp.concatenate([relation, relation + relations])[None]

    own = pack(features, cotangent)
    ring = [from_row(own, dz=dz) for dz in (4, 2, 6)]
    copies = jnp.broadcast_to(features, (Y * X_LO,) + features.shape)
    row_features = lax.all_to_all(copies, "pcol", 0, 0, tiled=True)
    (even,) = join([ring[2], own, ring[1], ring[0]], (((0, 0, 1), (1, 0, 1), (2, 0, 1), (3, 0, 1)),))
    across = from_row(even, dx=1)
    even, rows_named = tie(even, rows_named)
    weights = relation_weights(rows_named, coefficients.T, basis_weights)
    inverse_rows, keep, *sends = inverse_messages(
        entries, live_tiles, mask, [row_features], weights, rows_count
    )
    across, inverse_rows, keep, *sends = tie(across, inverse_rows, keep, *sends)
    upward, downward = join([even, across], (((0, 1, 2), (1, 1, 2)), ((0, 0, 2), (1, 0, 2))))
    upward, downward, even, across = tie(upward, downward, even, across)
    cotangent, _ = tie(cotangent, upward)
    copies = jnp.broadcast_to(cotangent, (Y * X_LO,) + cotangent.shape)
    row_cotangent = lax.all_to_all(copies, "pcol", 0, 0, tiled=True)
    up, down = from_row(upward, dz=1), from_row(downward, dz=7)
    swapped = [from_row(even, dk=1), from_row(across, dk=1)]
    sends = [from_row(part, dk=1) for part in sends]
    inverse_part = (keep + jnp.concatenate(sends).astype(F32)).astype(BF16).reshape(X_HI * RING, block, width)
    up, down, row_cotangent, *swapped = tie(up, down, row_cotangent, *swapped)
    columns = [even, across, up, down, *swapped, from_row(up, dk=1), from_row(down, dk=1)]
    *columns, inverse_part = tie(*columns, inverse_part)
    inverse_parts = lax.all_to_all(inverse_part, "prow", 0, 0, tiled=True, axis_index_groups=row_groups(1))
    forward_rows, mine, other = gradients(
        entries, live_tiles, k.reshape(1), mask, [row_cotangent], inverse_rows, basis_weights, columns
    )
    arrived, forward_rows = tie(from_row(other, dk=1), forward_rows)
    held = forward_messages(entries, live_tiles, forward_rows, weights)
    gathered, (forward_pair, *sends, inverse_parts) = gather_gradients(mine, arrived, (*held, inverse_parts), place)
    sends = [from_column(part, dy=Y - dy) for dy, part in enumerate(sends, 1)]
    for part in sends:
        forward_pair += part.astype(F32)
    beyond = forward_pair[1].astype(BF16)
    inverse_total = jnp.sum(inverse_parts.astype(F32), axis=0)
    gathered, beyond, inverse_total = tie(gathered, beyond, inverse_total)
    base = relations // LANES * LANES
    window = -(-(2 * relations - base) // LANES) * LANES
    placed = place_rows(gathered, bases, window)
    coefficient_grads = finish(k.reshape(1), placed, from_row(placed, dk=1), base, relations).T
    forward_sum = forward_pair[0] + from_column(beyond, dx=1).astype(F32)
    layer_sum = jnp.dot(features, self_weight, preferred_element_type=F32)
    layer_sum += inverse_total + forward_sum
    return layer_sum.astype(BF16), coefficient_grads


def solution(mesh):
    return jax.shard_map(
        on_device,
        mesh=mesh,
        in_specs=(
            P(("prow", "pcol"), None),
            P(("prow", "pcol"), None),
            P(),
            P(),
            P(),
            P("prow", "pcol", None, None),
            P("prow", "pcol", None, None, None),
            P("prow", "pcol"),
        ),
        out_specs=(P(("prow", "pcol"), None), P()),
        check_vma=False,
    )
```

```python
import functools
import jax
import jax.numpy as jnp
from jax import lax
from jax.experimental import pallas as pl
from jax.experimental.pallas import tpu as pltpu
from jax.sharding import PartitionSpec as P

F32, BF16 = jnp.float32, jnp.bfloat16
VMEM = pl.BlockSpec(memory_space=pltpu.VMEM)
SMEM = pl.BlockSpec(memory_space=pltpu.SMEM)
ANY = pl.BlockSpec(memory_space=pl.ANY)
HBM = pl.BlockSpec(memory_space=pltpu.HBM)
LANES = 128
DIAGONAL = 16
PAYLOAD = 48


def params(mib):
    return pltpu.CompilerParams(vmem_limit_bytes=mib * 1024 * 1024)


def cost(flops, moved):
    return pl.CostEstimate(flops=flops, bytes_accessed=moved, transcendentals=0)


def split(wide):
    high = wide.astype(BF16)
    return high, (wide - high.astype(F32)).astype(BF16)


def iota(shape, dim):
    return lax.broadcasted_iota(jnp.int32, shape, dim)


def weights_kernel(parts, row_ref, coefficient_ref, basis_ref, weight_ref, spread, basis, weight, in_sems, out_sems):
    bases, named = coefficient_ref.shape
    sides = row_ref.shape[1]
    depth, width = basis.shape[1:]
    size = depth // parts
    tall, wide = sides * DIAGONAL, bases * DIAGONAL
    arrive, leave = [], []
    for part in range(parts):
        rows = pl.ds(part * size, size)
        arrive.append(pltpu.make_async_copy(basis_ref.at[:, rows, :], basis.at[:, rows, :], in_sems.at[part]))
        leave.append(pltpu.make_async_copy(weight.at[:, rows, :], weight_ref.at[:, rows, :], out_sems.at[part]))
    for copy in arrive:
        copy.start()
    chosen = (iota((named, sides), 0) == row_ref[...]).astype(F32).astype(BF16)
    rows = (iota((tall, sides), 0) // DIAGONAL == iota((tall, sides), 1)).astype(F32).astype(BF16)
    columns = (iota((bases, wide), 1) // DIAGONAL == iota((bases, wide), 0)).astype(F32).astype(BF16)
    same = iota((tall, wide), 0) % DIAGONAL == iota((tall, wide), 1) % DIAGONAL
    for index, part in enumerate(split(coefficient_ref[...])):
        picked = jnp.dot(part, chosen, preferred_element_type=F32).astype(BF16)
        tower = lax.dot_general(rows, picked, (((1,), (1,)), ((), ())), preferred_element_type=F32).astype(BF16)
        full = jnp.dot(tower, columns, preferred_element_type=F32)
        spread[index] = jnp.where(same, full, 0.0).astype(BF16)
    for start in range(0, depth, DIAGONAL):
        if start % size == 0:
            arrive[start // size].wait()
        part = basis[:, start : start + DIAGONAL, :].reshape(wide, width)
        total = jnp.dot(spread[0], part, preferred_element_type=F32)
        total += jnp.dot(spread[1], part, preferred_element_type=F32)
        weight[:, start : start + DIAGONAL, :] = total.astype(BF16).reshape(sides, DIAGONAL, width)
        if (start + DIAGONAL) % size == 0:
            leave[start // size].start()
    for copy in leave:
        copy.wait()


def relation_weights(rows_named, coefficients_t, basis, parts=4):
    bases, depth, width = basis.shape
    sides = rows_named.shape[1]
    return pl.pallas_call(
        functools.partial(weights_kernel, parts),
        out_shape=jax.ShapeDtypeStruct((sides, depth, width), BF16),
        in_specs=[VMEM, VMEM, HBM],
        out_specs=HBM,
        scratch_shapes=[
            pltpu.VMEM((2, sides * DIAGONAL, bases * DIAGONAL), BF16),
            pltpu.VMEM(basis.shape, BF16),
            pltpu.VMEM((sides, depth, width), BF16),
            pltpu.SemaphoreType.DMA((parts,)),
            pltpu.SemaphoreType.DMA((parts,)),
        ],
        compiler_params=params(56),
        cost_estimate=cost(4 * 10**9, 2 * basis.size * 2),
        name="relation_weights",
    )(rows_named, coefficients_t, basis)


def normalised(mask, rows, dim):
    over = (((dim,), (0,)), ((), ()))
    summed = lax.dot_general(mask, rows, over, preferred_element_type=F32)
    degree = lax.dot_general(mask, jnp.ones((mask.shape[dim], LANES), BF16), over, preferred_element_type=F32)
    scale = (1.0 / (1.0 + degree)).astype(BF16).astype(F32)
    return (summed * jnp.concatenate([scale] * (rows.shape[1] // LANES), axis=1)).astype(BF16)


def copies_into(target, refs, sems):
    copies, at = [], 0
    for index, ref in enumerate(refs):
        size = ref.shape[0]
        copies.append(pltpu.make_async_copy(ref, target.at[pl.ds(at, size)], sems.at[index]))
        at += size
    for copy in copies:
        copy.start()
    return copies


def block_at(index, size):
    return pl.ds(pl.multiple_of(index * size, size), size)


def inverse_kernel(pieces, entry_ref, live_ref, mask_ref, weights_ref, *refs):
    rows_ref, keep_ref, send_ref, total, row, weight, row_sems, sem = refs[pieces:]
    tiles, block, _ = mask_ref.shape
    arrive = copies_into(row, refs[:pieces], row_sems)
    copy = pltpu.make_async_copy(weights_ref.at[pl.ds(tiles, tiles)], weight, sem)
    copy.start()
    total[...] = jnp.zeros_like(total)
    for part in arrive:
        part.wait()
    for tile in range(tiles):
        rows = row[entry_ref[2, tile], :block, :]
        rows_ref[tile] = normalised(mask_ref[tile].astype(F32).astype(BF16), rows, 0)
    copy.wait()
    for tile in range(tiles):
        weighting = (tile < live_ref[0, 0]).astype(F32)
        message = jnp.dot(rows_ref[tile], weight[tile], preferred_element_type=F32) * weighting
        total[block_at(entry_ref[4, tile], block), :] += message
    half = keep_ref.shape[0]
    keep_ref[...] = total[:half, :]
    send_ref[...] = total[half:, :].astype(BF16)


def inverse_messages(entries, live, mask, row_pieces, weights, row_count):
    tiles, block, _ = mask.shape
    width = row_pieces[0].shape[2]
    half = row_count * block // 2
    columns = sum(piece.shape[0] for piece in row_pieces)
    return pl.pallas_call(
        functools.partial(inverse_kernel, len(row_pieces)),
        out_shape=(
            jax.ShapeDtypeStruct((tiles, block, width), BF16),
            jax.ShapeDtypeStruct((half, width), F32),
            jax.ShapeDtypeStruct((half, width), BF16),
        ),
        in_specs=[SMEM, SMEM, VMEM, HBM] + [ANY] * len(row_pieces),
        out_specs=(VMEM, VMEM, VMEM),
        scratch_shapes=[
            pltpu.VMEM((2 * half, width), F32),
            pltpu.VMEM((columns,) + row_pieces[0].shape[1:], BF16),
            pltpu.VMEM((tiles, width, width), BF16),
            pltpu.SemaphoreType.DMA((len(row_pieces),)),
            pltpu.SemaphoreType.DMA,
        ],
        compiler_params=params(52),
        cost_estimate=cost(10**9, 8 * 10**6),
        name="inverse_messages",
    )(entries, live, mask, weights, *row_pieces)


def forward_kernel(entry_ref, live_ref, rows_ref, weights_ref, keep_ref, *refs):
    send_refs, (total, weight, sem) = refs[:-3], refs[-3:]
    tiles, block, _ = rows_ref.shape
    copy = pltpu.make_async_copy(weights_ref.at[pl.ds(0, tiles)], weight, sem)
    copy.start()
    total[...] = jnp.zeros_like(total)
    copy.wait()
    for tile in range(tiles):
        weighting = (tile < live_ref[0, 0]).astype(F32)
        message = jnp.dot(rows_ref[tile], weight[tile], preferred_element_type=F32) * weighting
        total[entry_ref[5, tile]] += message
    pair = keep_ref.shape[0]
    keep_ref[...] = total[:pair]
    for index, ref in enumerate(send_refs):
        ref[...] = total[pair * (index + 1) : pair * (index + 2)].astype(BF16)


def forward_messages(entries, live, rows, weights):
    tiles, block, width = rows.shape
    shape = (X_LO, block, width)
    return pl.pallas_call(
        forward_kernel,
        out_shape=(jax.ShapeDtypeStruct(shape, F32),) + (jax.ShapeDtypeStruct(shape, BF16),) * (Y - 1),
        in_specs=[SMEM, SMEM, VMEM, HBM],
        out_specs=(VMEM,) * Y,
        scratch_shapes=[
            pltpu.VMEM((Y * X_LO, block, width), F32),
            pltpu.VMEM((tiles, width, width), BF16),
            pltpu.SemaphoreType.DMA,
        ],
        compiler_params=params(56),
        cost_estimate=cost(10**9, 4 * 10**6),
        name="forward_messages",
    )(entries, live, rows, weights)


def gradient_kernel(pieces, row_pieces, entry_ref, live_ref, core_ref, mask_ref, inverse_ref, basis_ref, *refs):
    column_refs, row_refs, refs = refs[:pieces], refs[pieces : pieces + row_pieces], refs[pieces + row_pieces :]
    rows_ref, mine_ref, other_ref, column, row, basis, moments, total, column_sem, row_sem, basis_sem = refs
    tiles, block, _ = mask_ref.shape
    bases, depth, width = basis.shape
    sides = 2 * tiles
    copies = copies_into(column, column_refs, column_sem) + copies_into(row, row_refs, row_sem)
    basis_copy = pltpu.make_async_copy(basis_ref, basis, basis_sem)
    basis_copy.start()
    for copy in copies:
        copy.wait()
    for tile in range(tiles):
        rows = column[entry_ref[1, tile], :block, :]
        rows_ref[tile] = normalised(mask_ref[tile].astype(F32).astype(BF16), rows, 1)
    over = (((0,), (0,)), ((), ()))
    for tile in range(tiles):
        target = row[entry_ref[2, tile], block:, :]
        source = column[entry_ref[1, tile], block:, :]
        moments[tile] = lax.dot_general(rows_ref[tile], target, over, preferred_element_type=F32).astype(BF16)
        moments[tiles + tile] = lax.dot_general(
            inverse_ref[tile], source, over, preferred_element_type=F32
        ).astype(BF16)
    basis_copy.wait()
    tall, wide = bases * DIAGONAL, sides * DIAGONAL
    for start in range(0, depth, DIAGONAL):
        left = basis[:, start : start + DIAGONAL, :].reshape(tall, width)
        right = moments[:, start : start + DIAGONAL, :].reshape(wide, width)
        product = lax.dot_general(left, right, (((1,), (1,)), ((), ())), preferred_element_type=F32)
        if start == 0:
            total[...] = product
        else:
            total[...] += product
    same = iota((tall, wide), 0) % DIAGONAL == iota((tall, wide), 1) % DIAGONAL
    rows = (iota((bases, tall), 1) // DIAGONAL == iota((bases, tall), 0)).astype(BF16)
    columns = (iota((wide, sides), 0) // DIAGONAL == iota((wide, sides), 1)).astype(BF16)
    tower = jnp.zeros((bases, wide), F32)
    for part in split(jnp.where(same, total[...], 0.0)):
        tower += jnp.dot(rows, part, preferred_element_type=F32)
    per_tile = jnp.zeros((bases, sides), F32)
    for part in split(tower):
        per_tile += jnp.dot(part, columns, preferred_element_type=F32)
    live = live_ref[0, 0]
    per_tile = jnp.where(iota((bases, sides), 1) % tiles < live, per_tile, 0.0)
    first = core_ref[0] == 0
    forward, inverse = per_tile[:, :tiles], per_tile[:, tiles:]
    names = iota((PAYLOAD - bases, tiles), 0)
    lane = iota((PAYLOAD - bases, tiles), 1)
    for ref, chosen in ((mine_ref, first), (other_ref, jnp.logical_not(first))):
        ref[:bases, :] = jnp.where(chosen, forward, inverse).astype(BF16)
        named = jnp.zeros((PAYLOAD - bases, tiles), jnp.int32)
        for tile in range(tiles):
            name = entry_ref[0, tile] + jnp.where(chosen, 0, entry_ref[3, tile])
            digits = jnp.where(names == 0, name // LANES, jnp.where(names == 1, name % LANES, 0))
            named = jnp.where(lane == tile, digits, named)
        ref[bases:, :] = named.astype(F32).astype(BF16)


def gradients(entries, live, core, mask, row_pieces, inverse_rows, basis, columns):
    tiles, block, _ = mask.shape
    bases, depth, width = basis.shape
    payload = jax.ShapeDtypeStruct((PAYLOAD, tiles), BF16)

    def room(pieces):
        return pltpu.VMEM((sum(piece.shape[0] for piece in pieces), 2 * block, width), BF16)

    return pl.pallas_call(
        functools.partial(gradient_kernel, len(columns), len(row_pieces)),
        out_shape=(jax.ShapeDtypeStruct((tiles, block, width), BF16), payload, payload),
        in_specs=[SMEM, SMEM, SMEM, VMEM, VMEM, HBM] + [ANY] * (len(columns) + len(row_pieces)),
        out_specs=(VMEM, VMEM, VMEM),
        scratch_shapes=[
            room(columns),
            room(row_pieces),
            pltpu.VMEM(basis.shape, BF16),
            pltpu.VMEM((2 * tiles, depth, width), BF16),
            pltpu.VMEM((bases * DIAGONAL, 2 * tiles * DIAGONAL), F32),
            pltpu.SemaphoreType.DMA((len(columns),)),
            pltpu.SemaphoreType.DMA((len(row_pieces),)),
            pltpu.SemaphoreType.DMA,
        ],
        compiler_params=params(50),
        cost_estimate=cost(4 * 10**9, 12 * 10**6),
        name="gradients",
    )(entries, live, core, mask, inverse_rows, basis, *columns, *row_pieces)


def place_kernel(entry_ref, out_ref, total):
    bases, window = out_ref.shape
    count, _, span = entry_ref.shape
    for index in range(count):
        values = entry_ref[index, :bases, :].astype(F32)
        names = entry_ref[index, bases:, :].astype(F32)
        high, low = names[:1], names[1:2]
        chosen = (iota((LANES, span), 0).astype(F32) == low).astype(F32).astype(BF16)
        spread = [jnp.where(high == part, values, 0.0).astype(BF16) for part in range(window // LANES)]
        product = lax.dot_general(
            jnp.concatenate(spread, axis=0), chosen, (((1,), (1,)), ((), ())), preferred_element_type=F32
        )
        if index == 0:
            total[...] = product
        else:
            total[...] += product
    for part in range(window // LANES):
        out_ref[:, part * LANES : part * LANES + LANES] = total[part * bases : part * bases + bases, :]


def place_rows(entries, bases, window):
    return pl.pallas_call(
        place_kernel,
        out_shape=jax.ShapeDtypeStruct((bases, window), F32),
        in_specs=[VMEM],
        out_specs=VMEM,
        scratch_shapes=[pltpu.VMEM((window // LANES * bases, LANES), F32)],
        compiler_params=params(16),
        cost_estimate=cost(10**9, 10**6),
        name="place_rows",
    )(entries)


def join_kernel(plan, count, *refs):
    sems = refs[-1]
    copies = []
    for output, pieces in enumerate(plan):
        at = 0
        for source, start, size in pieces:
            copies.append(
                pltpu.make_async_copy(
                    refs[source].at[pl.ds(start, size)],
                    refs[count + output].at[pl.ds(at, size)],
                    sems.at[len(copies)],
                )
            )
            at += size
    for copy in copies:
        copy.start()
    for copy in copies:
        copy.wait()


def join(sources, plan):
    shape = sources[0].shape[1:]
    sizes = [sum(size for _, _, size in pieces) for pieces in plan]
    return pl.pallas_call(
        functools.partial(join_kernel, plan, len(sources)),
        out_shape=tuple(jax.ShapeDtypeStruct((size,) + shape, sources[0].dtype) for size in sizes),
        in_specs=[ANY] * len(sources),
        out_specs=tuple(ANY for _ in plan),
        scratch_shapes=[pltpu.SemaphoreType.DMA((sum(len(pieces) for pieces in plan),))],
        compiler_params=params(4),
        cost_estimate=cost(0, 10**6),
        name="join",
    )(*sources)


def finish_kernel(base, core_ref, own_ref, partner_ref, out_ref):
    window = own_ref.shape[1]
    shared = window - base
    last = out_ref.shape[1]
    first = core_ref[0] == 0
    out_ref[:, :base] = jnp.where(first, own_ref[:, :base], partner_ref[:, :base])
    out_ref[:, base:window] = jnp.where(first, own_ref[:, base:], partner_ref[:, base:]) + jnp.where(
        first, partner_ref[:, :shared], own_ref[:, :shared]
    )
    out_ref[:, window:] = jnp.where(
        first, partner_ref[:, shared : last - base], own_ref[:, shared : last - base]
    )


def finish(core, own, partner, base, relations):
    return pl.pallas_call(
        functools.partial(finish_kernel, base),
        out_shape=jax.ShapeDtypeStruct((own.shape[0], 2 * relations), F32),
        in_specs=[SMEM, VMEM, VMEM],
        out_specs=VMEM,
        compiler_params=params(8),
        cost_estimate=cost(0, 10**6),
        name="finish",
    )(core, own, partner)


def pack_kernel(feature_ref, cotangent_ref, own_ref, copies_ref, sems):
    block = feature_ref.shape[0]
    copies = [
        pltpu.make_async_copy(ref, own_ref.at[0, pl.ds(index * block, block), :], sems.at[index])
        for index, ref in enumerate((feature_ref, cotangent_ref))
    ]
    for copy in copies:
        copy.start()
    for copy in copies:
        copy.wait()
    for index in range(copies_ref.shape[0]):
        copies_ref[index] = own_ref[0]


def pack(features, cotangent, count):
    block, width = features.shape
    return pl.pallas_call(
        pack_kernel,
        out_shape=tuple(jax.ShapeDtypeStruct((blocks, 2 * block, width), BF16) for blocks in (1, count)),
        in_specs=[HBM, HBM],
        out_specs=(VMEM, VMEM),
        scratch_shapes=[pltpu.SemaphoreType.DMA((2,))],
        compiler_params=params(60),
        cost_estimate=cost(0, 10**6),
        name="pack",
    )(features, cotangent)


X_HI, RING, CORES = 2, 8, 2
Y, X_LO = 4, 2


def from_row(array, dx=0, dz=0, dk=0):
    pairs = []
    for x in range(X_HI):
        for z in range(RING):
            for k in range(CORES):
                source = ((x ^ dx) * RING + (z + dz) % RING) * CORES + (k ^ dk)
                pairs.append((source, (x * RING + z) * CORES + k))
    return lax.ppermute(array, "prow", pairs)


def from_column(array, dy=0, dx=0):
    pairs = []
    for y in range(Y):
        for x in range(X_LO):
            pairs.append((((y + dy) % Y) * X_LO + (x ^ dx), y * X_LO + x))
    return lax.ppermute(array, "pcol", pairs)


def tie(*arrays):
    return lax.optimization_barrier(arrays)


def coordinates():
    row = lax.axis_index("prow")
    column = lax.axis_index("pcol")
    return row // (RING * CORES), (row // CORES) % RING, row % CORES, column // X_LO, column % X_LO


def column_position(source, x, z, k):
    dx = (source // (RING * CORES)) ^ x
    dz = ((source // CORES) % RING - z) % RING
    dk = (source % CORES) ^ k
    even = dx * 4 + ((dz + 2) % RING) // 2
    odd = 8 + 4 * (dz // 4) + 2 * dx + (dz % 4) // 2
    return dk * 16 + jnp.where(dz % 2 == 0, even, odd)


def ordered(first, own, other, dim):
    return jnp.concatenate([jnp.where(first, own, other), jnp.where(first, other, own)], axis=dim)


def row_groups(apart):
    return [
        [(x * RING + z) * CORES + k for x in range(X_HI) for z in range(first, RING, apart)]
        for first in range(apart)
        for k in range(CORES)
    ]


def gather_gradients(mine, arrived, held, place):
    _, _, k, y, x_lo = place
    entries = ordered(k == 0, mine, arrived, 1)
    entries = ordered(x_lo == 0, entries, from_column(entries, dx=1), 1)
    around = [entries] + [from_column(entries, dy=dy) for dy in range(1, Y)]
    entries = jnp.concatenate(
        [functools.reduce(lambda a, dy: jnp.where(y == (at - dy) % Y, around[dy], a), range(1, Y), around[0]) for at in range(Y)],
        axis=1,
    )
    copies = jnp.broadcast_to(entries[None], (X_HI * RING,) + entries.shape)
    copies, *held = tie(copies, *held)
    gathered = lax.all_to_all(copies, "prow", 0, 0, tiled=True, axis_index_groups=row_groups(1))
    return gathered, held


def on_device(features, cotangent, self_weight, basis_weights, coefficients, tile_list, tile_mask, live_tiles):
    block, width = features.shape
    relations = coefficients.shape[0] // 2
    bases = coefficients.shape[1]
    rows_count = X_HI * RING * CORES
    place = coordinates()
    x, z, k, y, x_lo = place
    mask = tile_mask[0, 0]
    relation, source, target = tile_list[0, 0, :, 0], tile_list[0, 0, :, 1], tile_list[0, 0, :, 2]
    apart = ((source % CORES) ^ k) * (X_HI * RING) + source // CORES
    near = (target // X_LO - y) % Y * X_LO + (target % X_LO ^ x_lo)
    shift = jnp.full_like(relation, relations % LANES)
    entries = jnp.stack([relation, column_position(source, x, z, k), target, shift, apart, near])
    rows_named = jnp.concatenate([relation, relation + relations])[None]

    own, copies = pack(features, cotangent, Y * X_LO)
    ring = [from_row(own, dz=dz) for dz in (4, 2, 6)]
    row_blocks = lax.all_to_all(copies, "pcol", 0, 0, tiled=True)
    (even,) = join([ring[2], own, ring[1], ring[0]], (((0, 0, 1), (1, 0, 1), (2, 0, 1), (3, 0, 1)),))
    across = from_row(even, dx=1)
    even, rows_named = tie(even, rows_named)
    weights = relation_weights(rows_named, coefficients.T, basis_weights)
    row_pieces = [row_blocks]
    inverse_rows, keep, send = inverse_messages(entries, live_tiles, mask, row_pieces, weights, rows_count)
    across, inverse_rows, keep, send = tie(across, inverse_rows, keep, send)
    upward, downward = join([even, across], (((0, 1, 2), (1, 1, 2)), ((0, 0, 2), (1, 0, 2))))
    up, down = from_row(upward, dz=1), from_row(downward, dz=7)
    swapped = [from_row(even, dk=1), from_row(across, dk=1)]
    inverse_part = (keep + from_row(send, dk=1).astype(F32)).astype(BF16).reshape(X_HI * RING, block, width)
    up, down, inverse_part, *swapped = tie(up, down, inverse_part, *swapped)
    columns = [even, across, up, down, *swapped, from_row(up, dk=1), from_row(down, dk=1)]
    inverse_parts = lax.all_to_all(inverse_part, "prow", 0, 0, tiled=True, axis_index_groups=row_groups(1))
    forward_rows, mine, other = gradients(
        entries, live_tiles, k.reshape(1), mask, row_pieces, inverse_rows, basis_weights, columns
    )
    arrived, forward_rows = tie(from_row(other, dk=1), forward_rows)
    gathered, (forward_rows, inverse_parts) = gather_gradients(mine, arrived, (forward_rows, inverse_parts), place)
    forward_pair, *sends = forward_messages(entries, live_tiles, forward_rows, weights)
    sends = [from_column(part, dy=Y - dy) for dy, part in enumerate(sends, 1)]
    base = relations // LANES * LANES
    window = -(-(2 * relations - base) // LANES) * LANES
    placed = place_rows(gathered, bases, window)
    coefficient_grads = finish(k.reshape(1), placed, from_row(placed, dk=1), base, relations).T
    _, *sends = tie(placed, *sends)
    for part in sends:
        forward_pair += part.astype(F32)
    forward_sum = forward_pair[0] + from_column(forward_pair[1].astype(BF16), dx=1).astype(F32)
    layer_sum = jnp.dot(features, self_weight, preferred_element_type=F32)
    layer_sum += jnp.sum(inverse_parts.astype(F32), axis=0) + forward_sum
    return layer_sum.astype(BF16), coefficient_grads


def solution(mesh):
    return jax.shard_map(
        on_device,
        mesh=mesh,
        in_specs=(
            P(("prow", "pcol"), None),
            P(("prow", "pcol"), None),
            P(),
            P(),
            P(),
            P("prow", "pcol", None, None),
            P("prow", "pcol", None, None, None),
            P("prow", "pcol"),
        ),
        out_specs=(P(("prow", "pcol"), None), P()),
        check_vma=False,
    )
```

```python
import functools
import jax
import jax.numpy as jnp
from jax import lax
from jax.experimental import pallas as pl
from jax.experimental.pallas import tpu as pltpu
from jax.sharding import PartitionSpec as P

F32, BF16 = jnp.float32, jnp.bfloat16
VMEM = pl.BlockSpec(memory_space=pltpu.VMEM)
SMEM = pl.BlockSpec(memory_space=pltpu.SMEM)
ANY = pl.BlockSpec(memory_space=pl.ANY)
HBM = pl.BlockSpec(memory_space=pltpu.HBM)
LANES = 128
DIAGONAL = 16
PAYLOAD = 48


def params(mib):
    return pltpu.CompilerParams(vmem_limit_bytes=mib * 1024 * 1024)


def cost(flops, moved):
    return pl.CostEstimate(flops=flops, bytes_accessed=moved, transcendentals=0)


def split(wide):
    high = wide.astype(BF16)
    return high, (wide - high.astype(F32)).astype(BF16)


def iota(shape, dim):
    return lax.broadcasted_iota(jnp.int32, shape, dim)


def weights_kernel(parts, row_ref, coefficient_ref, basis_ref, weight_ref, spread, basis, weight, in_sems, out_sems):
    bases, named = coefficient_ref.shape
    sides = row_ref.shape[1]
    depth, width = basis.shape[1:]
    size = depth // parts
    tall, wide = sides * DIAGONAL, bases * DIAGONAL
    arrive, leave = [], []
    for part in range(parts):
        rows = pl.ds(part * size, size)
        arrive.append(pltpu.make_async_copy(basis_ref.at[:, rows, :], basis.at[:, rows, :], in_sems.at[part]))
        leave.append(pltpu.make_async_copy(weight.at[:, rows, :], weight_ref.at[:, rows, :], out_sems.at[part]))
    for copy in arrive:
        copy.start()
    chosen = (iota((named, sides), 0) == row_ref[...]).astype(F32).astype(BF16)
    rows = (iota((tall, sides), 0) // DIAGONAL == iota((tall, sides), 1)).astype(F32).astype(BF16)
    columns = (iota((bases, wide), 1) // DIAGONAL == iota((bases, wide), 0)).astype(F32).astype(BF16)
    same = iota((tall, wide), 0) % DIAGONAL == iota((tall, wide), 1) % DIAGONAL
    for index, part in enumerate(split(coefficient_ref[...])):
        picked = jnp.dot(part, chosen, preferred_element_type=F32).astype(BF16)
        tower = lax.dot_general(rows, picked, (((1,), (1,)), ((), ())), preferred_element_type=F32).astype(BF16)
        full = jnp.dot(tower, columns, preferred_element_type=F32)
        spread[index] = jnp.where(same, full, 0.0).astype(BF16)
    for start in range(0, depth, DIAGONAL):
        if start % size == 0:
            arrive[start // size].wait()
        part = basis[:, start : start + DIAGONAL, :].reshape(wide, width)
        total = jnp.dot(spread[0], part, preferred_element_type=F32)
        total += jnp.dot(spread[1], part, preferred_element_type=F32)
        weight[:, start : start + DIAGONAL, :] = total.astype(BF16).reshape(sides, DIAGONAL, width)
        if (start + DIAGONAL) % size == 0:
            leave[start // size].start()
    for copy in leave:
        copy.wait()


def relation_weights(rows_named, coefficients_t, basis, parts=4):
    bases, depth, width = basis.shape
    sides = rows_named.shape[1]
    return pl.pallas_call(
        functools.partial(weights_kernel, parts),
        out_shape=jax.ShapeDtypeStruct((sides, depth, width), BF16),
        in_specs=[VMEM, VMEM, HBM],
        out_specs=HBM,
        scratch_shapes=[
            pltpu.VMEM((2, sides * DIAGONAL, bases * DIAGONAL), BF16),
            pltpu.VMEM(basis.shape, BF16),
            pltpu.VMEM((sides, depth, width), BF16),
            pltpu.SemaphoreType.DMA((parts,)),
            pltpu.SemaphoreType.DMA((parts,)),
        ],
        compiler_params=params(56),
        cost_estimate=cost(4 * 10**9, 2 * basis.size * 2),
        name="relation_weights",
    )(rows_named, coefficients_t, basis)


def normalised(mask, rows, dim):
    over = (((dim,), (0,)), ((), ()))
    summed = lax.dot_general(mask, rows, over, preferred_element_type=F32)
    degree = lax.dot_general(mask, jnp.ones((mask.shape[dim], LANES), BF16), over, preferred_element_type=F32)
    scale = (1.0 / (1.0 + degree)).astype(BF16).astype(F32)
    return (summed * jnp.concatenate([scale] * (rows.shape[1] // LANES), axis=1)).astype(BF16)


def copies_into(target, refs, sems):
    copies, at = [], 0
    for index, ref in enumerate(refs):
        size = ref.shape[0]
        copies.append(pltpu.make_async_copy(ref, target.at[pl.ds(at, size)], sems.at[index]))
        at += size
    for copy in copies:
        copy.start()
    return copies


def block_at(index, size):
    return pl.ds(pl.multiple_of(index * size, size), size)


def inverse_kernel(pieces, entry_ref, live_ref, mask_ref, weights_ref, *refs):
    rows_ref, keep_ref, send_ref, total, row, weight, row_sems, sem = refs[pieces:]
    tiles, block, _ = mask_ref.shape
    arrive = copies_into(row, refs[:pieces], row_sems)
    copy = pltpu.make_async_copy(weights_ref.at[pl.ds(tiles, tiles)], weight, sem)
    copy.start()
    total[...] = jnp.zeros_like(total)
    for part in arrive:
        part.wait()
    for tile in range(tiles):
        rows = row[entry_ref[2, tile], :block, :]
        rows_ref[tile] = normalised(mask_ref[tile].astype(F32).astype(BF16), rows, 0)
    copy.wait()
    for tile in range(tiles):
        weighting = (tile < live_ref[0, 0]).astype(F32)
        message = jnp.dot(rows_ref[tile], weight[tile], preferred_element_type=F32) * weighting
        total[block_at(entry_ref[4, tile], block), :] += message
    half = keep_ref.shape[0]
    keep_ref[...] = total[:half, :]
    send_ref[...] = total[half:, :].astype(BF16)


def inverse_messages(entries, live, mask, row_pieces, weights, row_count):
    tiles, block, _ = mask.shape
    width = row_pieces[0].shape[2]
    half = row_count * block // 2
    columns = sum(piece.shape[0] for piece in row_pieces)
    return pl.pallas_call(
        functools.partial(inverse_kernel, len(row_pieces)),
        out_shape=(
            jax.ShapeDtypeStruct((tiles, block, width), BF16),
            jax.ShapeDtypeStruct((half, width), F32),
            jax.ShapeDtypeStruct((half, width), BF16),
        ),
        in_specs=[SMEM, SMEM, VMEM, HBM] + [ANY] * len(row_pieces),
        out_specs=(VMEM, VMEM, VMEM),
        scratch_shapes=[
            pltpu.VMEM((2 * half, width), F32),
            pltpu.VMEM((columns,) + row_pieces[0].shape[1:], BF16),
            pltpu.VMEM((tiles, width, width), BF16),
            pltpu.SemaphoreType.DMA((len(row_pieces),)),
            pltpu.SemaphoreType.DMA,
        ],
        compiler_params=params(52),
        cost_estimate=cost(10**9, 8 * 10**6),
        name="inverse_messages",
    )(entries, live, mask, weights, *row_pieces)


def forward_kernel(entry_ref, live_ref, rows_ref, weights_ref, keep_ref, *refs):
    send_refs, (total, weight, sem) = refs[:-3], refs[-3:]
    tiles, block, _ = rows_ref.shape
    copy = pltpu.make_async_copy(weights_ref.at[pl.ds(0, tiles)], weight, sem)
    copy.start()
    total[...] = jnp.zeros_like(total)
    copy.wait()
    for tile in range(tiles):
        weighting = (tile < live_ref[0, 0]).astype(F32)
        message = jnp.dot(rows_ref[tile], weight[tile], preferred_element_type=F32) * weighting
        total[entry_ref[5, tile]] += message
    pair = keep_ref.shape[0]
    keep_ref[...] = total[:pair]
    for index, ref in enumerate(send_refs):
        ref[...] = total[pair * (index + 1) : pair * (index + 2)].astype(BF16)


def forward_messages(entries, live, rows, weights):
    tiles, block, width = rows.shape
    shape = (X_LO, block, width)
    return pl.pallas_call(
        forward_kernel,
        out_shape=(jax.ShapeDtypeStruct(shape, F32),) + (jax.ShapeDtypeStruct(shape, BF16),) * (Y - 1),
        in_specs=[SMEM, SMEM, VMEM, HBM],
        out_specs=(VMEM,) * Y,
        scratch_shapes=[
            pltpu.VMEM((Y * X_LO, block, width), F32),
            pltpu.VMEM((tiles, width, width), BF16),
            pltpu.SemaphoreType.DMA,
        ],
        compiler_params=params(56),
        cost_estimate=cost(10**9, 4 * 10**6),
        name="forward_messages",
    )(entries, live, rows, weights)


def gradient_kernel(pieces, row_pieces, entry_ref, live_ref, core_ref, mask_ref, inverse_ref, basis_ref, *refs):
    column_refs, row_refs, refs = refs[:pieces], refs[pieces : pieces + row_pieces], refs[pieces + row_pieces :]
    rows_ref, mine_ref, other_ref, column, row, basis, moments, total, column_sem, row_sem, basis_sem = refs
    tiles, block, _ = mask_ref.shape
    bases, depth, width = basis.shape
    sides = 2 * tiles
    copies = copies_into(column, column_refs, column_sem) + copies_into(row, row_refs, row_sem)
    basis_copy = pltpu.make_async_copy(basis_ref, basis, basis_sem)
    basis_copy.start()
    for copy in copies:
        copy.wait()
    for tile in range(tiles):
        rows = column[entry_ref[1, tile], :block, :]
        rows_ref[tile] = normalised(mask_ref[tile].astype(F32).astype(BF16), rows, 1)
    over = (((0,), (0,)), ((), ()))
    for tile in range(tiles):
        target = row[entry_ref[2, tile], block:, :]
        source = column[entry_ref[1, tile], block:, :]
        moments[tile] = lax.dot_general(rows_ref[tile], target, over, preferred_element_type=F32).astype(BF16)
        moments[tiles + tile] = lax.dot_general(
            inverse_ref[tile], source, over, preferred_element_type=F32
        ).astype(BF16)
    basis_copy.wait()
    tall, wide = bases * DIAGONAL, sides * DIAGONAL
    for start in range(0, depth, DIAGONAL):
        left = basis[:, start : start + DIAGONAL, :].reshape(tall, width)
        right = moments[:, start : start + DIAGONAL, :].reshape(wide, width)
        product = lax.dot_general(left, right, (((1,), (1,)), ((), ())), preferred_element_type=F32)
        if start == 0:
            total[...] = product
        else:
            total[...] += product
    same = iota((tall, wide), 0) % DIAGONAL == iota((tall, wide), 1) % DIAGONAL
    rows = (iota((bases, tall), 1) // DIAGONAL == iota((bases, tall), 0)).astype(BF16)
    columns = (iota((wide, sides), 0) // DIAGONAL == iota((wide, sides), 1)).astype(BF16)
    tower = jnp.zeros((bases, wide), F32)
    for part in split(jnp.where(same, total[...], 0.0)):
        tower += jnp.dot(rows, part, preferred_element_type=F32)
    per_tile = jnp.zeros((bases, sides), F32)
    for part in split(tower):
        per_tile += jnp.dot(part, columns, preferred_element_type=F32)
    live = live_ref[0, 0]
    per_tile = jnp.where(iota((bases, sides), 1) % tiles < live, per_tile, 0.0)
    first = core_ref[0] == 0
    forward, inverse = per_tile[:, :tiles], per_tile[:, tiles:]
    names = iota((PAYLOAD - bases, tiles), 0)
    lane = iota((PAYLOAD - bases, tiles), 1)
    for ref, chosen in ((mine_ref, first), (other_ref, jnp.logical_not(first))):
        ref[:bases, :] = jnp.where(chosen, forward, inverse).astype(BF16)
        named = jnp.zeros((PAYLOAD - bases, tiles), jnp.int32)
        for tile in range(tiles):
            name = entry_ref[0, tile] + jnp.where(chosen, 0, entry_ref[3, tile])
            digits = jnp.where(names == 0, name // LANES, jnp.where(names == 1, name % LANES, 0))
            named = jnp.where(lane == tile, digits, named)
        ref[bases:, :] = named.astype(F32).astype(BF16)


def gradients(entries, live, core, mask, row_pieces, inverse_rows, basis, columns):
    tiles, block, _ = mask.shape
    bases, depth, width = basis.shape
    payload = jax.ShapeDtypeStruct((PAYLOAD, tiles), BF16)

    def room(pieces):
        return pltpu.VMEM((sum(piece.shape[0] for piece in pieces), 2 * block, width), BF16)

    return pl.pallas_call(
        functools.partial(gradient_kernel, len(columns), len(row_pieces)),
        out_shape=(jax.ShapeDtypeStruct((tiles, block, width), BF16), payload, payload),
        in_specs=[SMEM, SMEM, SMEM, VMEM, VMEM, HBM] + [ANY] * (len(columns) + len(row_pieces)),
        out_specs=(VMEM, VMEM, VMEM),
        scratch_shapes=[
            room(columns),
            room(row_pieces),
            pltpu.VMEM(basis.shape, BF16),
            pltpu.VMEM((2 * tiles, depth, width), BF16),
            pltpu.VMEM((bases * DIAGONAL, 2 * tiles * DIAGONAL), F32),
            pltpu.SemaphoreType.DMA((len(columns),)),
            pltpu.SemaphoreType.DMA((len(row_pieces),)),
            pltpu.SemaphoreType.DMA,
        ],
        compiler_params=params(50),
        cost_estimate=cost(4 * 10**9, 12 * 10**6),
        name="gradients",
    )(entries, live, core, mask, inverse_rows, basis, *columns, *row_pieces)


def place_kernel(entry_ref, out_ref, total):
    bases, window = out_ref.shape
    count, _, span = entry_ref.shape
    for index in range(count):
        values = entry_ref[index, :bases, :].astype(F32)
        names = entry_ref[index, bases:, :].astype(F32)
        high, low = names[:1], names[1:2]
        chosen = (iota((LANES, span), 0).astype(F32) == low).astype(F32).astype(BF16)
        spread = [jnp.where(high == part, values, 0.0).astype(BF16) for part in range(window // LANES)]
        product = lax.dot_general(
            jnp.concatenate(spread, axis=0), chosen, (((1,), (1,)), ((), ())), preferred_element_type=F32
        )
        if index == 0:
            total[...] = product
        else:
            total[...] += product
    for part in range(window // LANES):
        out_ref[:, part * LANES : part * LANES + LANES] = total[part * bases : part * bases + bases, :]


def place_rows(entries, bases, window):
    return pl.pallas_call(
        place_kernel,
        out_shape=jax.ShapeDtypeStruct((bases, window), F32),
        in_specs=[VMEM],
        out_specs=VMEM,
        scratch_shapes=[pltpu.VMEM((window // LANES * bases, LANES), F32)],
        compiler_params=params(16),
        cost_estimate=cost(10**9, 10**6),
        name="place_rows",
    )(entries)


def join_kernel(plan, count, *refs):
    sems = refs[-1]
    copies = []
    for output, pieces in enumerate(plan):
        at = 0
        for source, start, size in pieces:
            copies.append(
                pltpu.make_async_copy(
                    refs[source].at[pl.ds(start, size)],
                    refs[count + output].at[pl.ds(at, size)],
                    sems.at[len(copies)],
                )
            )
            at += size
    for copy in copies:
        copy.start()
    for copy in copies:
        copy.wait()


def join(sources, plan):
    shape = sources[0].shape[1:]
    sizes = [sum(size for _, _, size in pieces) for pieces in plan]
    return pl.pallas_call(
        functools.partial(join_kernel, plan, len(sources)),
        out_shape=tuple(jax.ShapeDtypeStruct((size,) + shape, sources[0].dtype) for size in sizes),
        in_specs=[ANY] * len(sources),
        out_specs=tuple(ANY for _ in plan),
        scratch_shapes=[pltpu.SemaphoreType.DMA((sum(len(pieces) for pieces in plan),))],
        compiler_params=params(4),
        cost_estimate=cost(0, 10**6),
        name="join",
    )(*sources)


def finish_kernel(base, core_ref, own_ref, partner_ref, out_ref):
    window = own_ref.shape[1]
    shared = window - base
    last = out_ref.shape[1]
    first = core_ref[0] == 0
    out_ref[:, :base] = jnp.where(first, own_ref[:, :base], partner_ref[:, :base])
    out_ref[:, base:window] = jnp.where(first, own_ref[:, base:], partner_ref[:, base:]) + jnp.where(
        first, partner_ref[:, :shared], own_ref[:, :shared]
    )
    out_ref[:, window:] = jnp.where(
        first, partner_ref[:, shared : last - base], own_ref[:, shared : last - base]
    )


def finish(core, own, partner, base, relations):
    return pl.pallas_call(
        functools.partial(finish_kernel, base),
        out_shape=jax.ShapeDtypeStruct((own.shape[0], 2 * relations), F32),
        in_specs=[SMEM, VMEM, VMEM],
        out_specs=VMEM,
        compiler_params=params(8),
        cost_estimate=cost(0, 10**6),
        name="finish",
    )(core, own, partner)


def pack_kernel(feature_ref, cotangent_ref, own_ref, copies_ref, sems):
    block = feature_ref.shape[0]
    copies = [
        pltpu.make_async_copy(ref, own_ref.at[0, pl.ds(index * block, block), :], sems.at[index])
        for index, ref in enumerate((feature_ref, cotangent_ref))
    ]
    for copy in copies:
        copy.start()
    for copy in copies:
        copy.wait()
    for index in range(copies_ref.shape[0]):
        copies_ref[index] = own_ref[0]


def pack(features, cotangent, count):
    block, width = features.shape
    return pl.pallas_call(
        pack_kernel,
        out_shape=tuple(jax.ShapeDtypeStruct((blocks, 2 * block, width), BF16) for blocks in (1, count)),
        in_specs=[HBM, HBM],
        out_specs=(VMEM, VMEM),
        scratch_shapes=[pltpu.SemaphoreType.DMA((2,))],
        compiler_params=params(60),
        cost_estimate=cost(0, 10**6),
        name="pack",
    )(features, cotangent)


X_HI, RING, CORES = 2, 8, 2
Y, X_LO = 4, 2


def from_row(array, dx=0, dz=0, dk=0):
    pairs = []
    for x in range(X_HI):
        for z in range(RING):
            for k in range(CORES):
                source = ((x ^ dx) * RING + (z + dz) % RING) * CORES + (k ^ dk)
                pairs.append((source, (x * RING + z) * CORES + k))
    return lax.ppermute(array, "prow", pairs)


def from_column(array, dy=0, dx=0):
    pairs = []
    for y in range(Y):
        for x in range(X_LO):
            pairs.append((((y + dy) % Y) * X_LO + (x ^ dx), y * X_LO + x))
    return lax.ppermute(array, "pcol", pairs)


def tie(*arrays):
    return lax.optimization_barrier(arrays)


def coordinates():
    row = lax.axis_index("prow")
    column = lax.axis_index("pcol")
    return row // (RING * CORES), (row // CORES) % RING, row % CORES, column // X_LO, column % X_LO


def column_position(source, x, z, k):
    dx = (source // (RING * CORES)) ^ x
    dz = ((source // CORES) % RING - z) % RING
    dk = (source % CORES) ^ k
    even = dx * 4 + ((dz + 2) % RING) // 2
    odd = 8 + 4 * (dz // 4) + 2 * dx + (dz % 4) // 2
    return dk * 16 + jnp.where(dz % 2 == 0, even, odd)


def ordered(first, own, other, dim):
    return jnp.concatenate([jnp.where(first, own, other), jnp.where(first, other, own)], axis=dim)


def row_groups(apart):
    return [
        [(x * RING + z) * CORES + k for x in range(X_HI) for z in range(first, RING, apart)]
        for first in range(apart)
        for k in range(CORES)
    ]


def gather_gradients(mine, arrived, held, place):
    _, _, k, y, x_lo = place
    entries = ordered(k == 0, mine, arrived, 1)
    entries = ordered(x_lo == 0, entries, from_column(entries, dx=1), 1)
    around = [entries] + [from_column(entries, dy=dy) for dy in range(1, Y)]
    entries = jnp.concatenate(
        [functools.reduce(lambda a, dy: jnp.where(y == (at - dy) % Y, around[dy], a), range(1, Y), around[0]) for at in range(Y)],
        axis=1,
    )
    copies = jnp.broadcast_to(entries[None], (X_HI * RING,) + entries.shape)
    copies, *held = tie(copies, *held)
    gathered = lax.all_to_all(copies, "prow", 0, 0, tiled=True, axis_index_groups=row_groups(1))
    return gathered, held


def on_device(features, cotangent, self_weight, basis_weights, coefficients, tile_list, tile_mask, live_tiles):
    block, width = features.shape
    relations = coefficients.shape[0] // 2
    bases = coefficients.shape[1]
    rows_count = X_HI * RING * CORES
    place = coordinates()
    x, z, k, y, x_lo = place
    mask = tile_mask[0, 0]
    relation, source, target = tile_list[0, 0, :, 0], tile_list[0, 0, :, 1], tile_list[0, 0, :, 2]
    apart = ((source % CORES) ^ k) * (X_HI * RING) + source // CORES
    near = (target // X_LO - y) % Y * X_LO + (target % X_LO ^ x_lo)
    shift = jnp.full_like(relation, relations % LANES)
    entries = jnp.stack([relation, column_position(source, x, z, k), target, shift, apart, near])
    rows_named = jnp.concatenate([relation, relation + relations])[None]

    own, copies = pack(features, cotangent, Y * X_LO)
    ring = [from_row(own, dz=dz) for dz in (4, 2, 6)]
    row_blocks = lax.all_to_all(copies, "pcol", 0, 0, tiled=True)
    (even,) = join([ring[2], own, ring[1], ring[0]], (((0, 0, 1), (1, 0, 1), (2, 0, 1), (3, 0, 1)),))
    across = from_row(even, dx=1)
    even, rows_named = tie(even, rows_named)
    weights = relation_weights(rows_named, coefficients.T, basis_weights)
    row_pieces = [row_blocks]
    inverse_rows, keep, send = inverse_messages(entries, live_tiles, mask, row_pieces, weights, rows_count)
    across, inverse_rows, keep, send = tie(across, inverse_rows, keep, send)
    upward, downward = join([even, across], (((0, 1, 2), (1, 1, 2)), ((0, 0, 2), (1, 0, 2))))
    up, down = from_row(upward, dz=1), from_row(downward, dz=7)
    swapped = [from_row(even, dk=1), from_row(across, dk=1)]
    inverse_part = (keep + from_row(send, dk=1).astype(F32)).astype(BF16).reshape(X_HI * RING, block, width)
    up, down, inverse_part, *swapped = tie(up, down, inverse_part, *swapped)
    columns = [even, across, up, down, *swapped, from_row(up, dk=1), from_row(down, dk=1)]
    inverse_parts = lax.all_to_all(inverse_part, "prow", 0, 0, tiled=True, axis_index_groups=row_groups(1))
    forward_rows, mine, other = gradients(
        entries, live_tiles, k.reshape(1), mask, row_pieces, inverse_rows, basis_weights, columns
    )
    arrived, forward_rows = tie(from_row(other, dk=1), forward_rows)
    held = forward_messages(entries, live_tiles, forward_rows, weights)
    gathered, (forward_pair, *sends, inverse_parts) = gather_gradients(mine, arrived, (*held, inverse_parts), place)
    sends = [from_column(part, dy=Y - dy) for dy, part in enumerate(sends, 1)]
    base = relations // LANES * LANES
    window = -(-(2 * relations - base) // LANES) * LANES
    placed = place_rows(gathered, bases, window)
    coefficient_grads = finish(k.reshape(1), placed, from_row(placed, dk=1), base, relations).T
    _, *sends = tie(placed, *sends)
    for part in sends:
        forward_pair += part.astype(F32)
    forward_sum = forward_pair[0] + from_column(forward_pair[1].astype(BF16), dx=1).astype(F32)
    layer_sum = jnp.dot(features, self_weight, preferred_element_type=F32)
    layer_sum += jnp.sum(inverse_parts.astype(F32), axis=0) + forward_sum
    return layer_sum.astype(BF16), coefficient_grads


def solution(mesh):
    return jax.shard_map(
        on_device,
        mesh=mesh,
        in_specs=(
            P(("prow", "pcol"), None),
            P(("prow", "pcol"), None),
            P(),
            P(),
            P(),
            P("prow", "pcol", None, None),
            P("prow", "pcol", None, None, None),
            P("prow", "pcol"),
        ),
        out_specs=(P(("prow", "pcol"), None), P()),
        check_vma=False,
    )
```
